128 devices in a mesh: ctx: 16 (over y, x), head: 2 (over core), dp: 4 (over z).
Axes of the slice: x: 4, y: 4, z: 4, core: 2. Of those that a mesh axis runs over, the one named last changes fastest.
Arguments:
- x_in: bfloat16 [8192, 8192], P(('dp', 'ctx'), 'head'), parts along dimension 0, may hold values from -6 to 6
- bc_in: bfloat16 [8192, 2, 512], P(('dp', 'ctx'), None, 'head'), parts along dimension 0, may hold values from -4 to 4
- conv_x: float32 [4, 8192], P(None, 'head'), may hold values from -3 to 3
- conv_bc: float32 [4, 2, 512], P(None, None, 'head'), may hold values from -3 to 3
- dt_raw: float32 [64, 8192], P('head', ('dp', 'ctx')), parts along dimension 1, may hold values from -4 to 1
- rate: float32 [64], P('head'), may hold values from 0.0003 to 0.1
- grad_ssd: bfloat16 [8192, 8192], P(('dp', 'ctx'), 'head'), parts along dimension 0, may hold values from -6 to 6
- query: bfloat16 [8192, 4096], P(('dp', 'ctx'), 'head'), parts along dimension 0, may hold values from -6 to 6
- key: bfloat16 [8192, 512], P(('dp', 'ctx'), 'head'), parts along dimension 0, may hold values from -6 to 6
- value: bfloat16 [8192, 512], P(('dp', 'ctx'), 'head'), parts along dimension 0, may hold values from -6 to 6
- d_out: bfloat16 [8192, 4096], P(('dp', 'ctx'), 'head'), parts along dimension 0, may hold values from -6 to 6
- doc_lengths: int32 [16], P('dp'), parts along dimension 0, may hold values from 1 to 1024, 2048 in all
Outputs:
- d_x_in: bfloat16 [8192, 8192], P(('dp', 'ctx'), 'head'), parts along dimension 0
- d_bc_in: bfloat16 [8192, 2, 512], P(('dp', 'ctx'), None, 'head'), parts along dimension 0
- d_dt_raw: float32 [64, 8192], P('head', ('dp', 'ctx')), parts along dimension 1
- d_conv_x: float32 [16, 8192], P('dp', 'head'), parts along dimension 0
- d_conv_bc: float32 [16, 2, 512], P('dp', None, 'head'), parts along dimension 0
- d_query: bfloat16 [8192, 4096], P(('dp', 'ctx'), 'head'), parts along dimension 0
- d_key: bfloat16 [8192, 512], P(('dp', 'ctx'), 'head'), parts along dimension 0
- d_value: bfloat16 [8192, 512], P(('dp', 'ctx'), 'head'), parts along dimension 0
The draws below stay inside these ranges and needn't reach their ends.
There are 4 independent parts, one for each index of `dp`. The reference program is written for one: setup_inputs(seed, part) draws one part's arguments, and reference() takes and returns one part's arrays. A program takes and returns all parts, laid end to end along the dimension named above; an argument that names none is the same for every part. Nothing has to cross between parts.
Inputs may be any that keep to these rules, and one draw needn't show every extreme that they name: `doc_lengths`: document lengths that fill the 2048 positions in order; the longest is exactly 1024.
All inputs are finite; a program needn't handle non-finite values.
Results may differ from the reference program's by a relative error of at most 0.018.
Values may be sent and summed in bfloat16 or wider, within the bound.
No kernel may reach another device: no remote copies, remote signals or barrier semaphores. Data moves between devices by JAX's collectives and lax.ppermute only.
A program may use at most 192 MiB of HBM per device.

```python
import math
import jax
import jax.numpy as jnp
import numpy as np
from jax import lax

P_SIZE = 128
N = 128
HD = 128
CONV = 4
HEADS = 64
GROUPS = 4
QHEADS = 32
KVHEADS = 4
STRETCH = 128
DOCS = 4
TOKENS = 2048
Q_PER_KV = 8


def aligned_plan(key):
    region_count = 8
    region_span = TOKENS // region_count
    sign_key, place_key = jax.random.split(key)
    sign_grid = jnp.where(jax.random.bernoulli(sign_key, 0.5, (KVHEADS, HD)), 1.0, -1.0).astype(jnp.float32)
    region_first = jnp.arange(region_count, dtype=jnp.int32) * region_span + jax.random.randint(place_key, (region_count,), 0, region_span - 3)
    strengths = 3.5 + (jnp.arange(region_count, dtype=jnp.int32) % 3).astype(jnp.float32)
    positions = jnp.arange(TOKENS, dtype=jnp.int32)
    relative = positions[:, None] - region_first[None, :]
    inside = (relative >= 0) & (relative < 4)
    offsets = jnp.sum(jnp.where(inside, relative + 1, 0), axis=1) - 1
    strength = jnp.sum(jnp.where(inside, strengths[None, :], 0.0), axis=1)
    return (sign_grid, offsets, strength)


def draw_query(key, part):
    sign_grid, offsets, strength = aligned_plan(key)
    key = jax.random.fold_in(key, 21)
    base = jax.random.truncated_normal(key, -6.0, 6.0, (TOKENS, QHEADS * HD), jnp.float32)
    aligned = strength[:, None, None] * jnp.repeat(sign_grid, Q_PER_KV, axis=0)[None]
    chosen = jnp.where((offsets >= 1)[:, None], aligned.reshape(TOKENS, QHEADS * HD), base)
    return chosen.astype(jnp.bfloat16)


def draw_key(key, part):
    sign_grid, offsets, strength = aligned_plan(key)
    key = jax.random.fold_in(key, 37)
    base = jax.random.truncated_normal(key, -6.0, 6.0, (TOKENS, KVHEADS * HD), jnp.float32)
    entry_ids = jnp.arange(HD, dtype=jnp.int32)
    kept = (entry_ids[None, :] >= offsets[:, None]).astype(jnp.float32)
    aligned = strength[:, None, None] * sign_grid[None] * kept[:, None, :]
    chosen = jnp.where((offsets >= 0)[:, None], aligned.reshape(TOKENS, KVHEADS * HD), base)
    return chosen.astype(jnp.bfloat16)


def block_scale(own_key, dims, cuts, low, top_value):
    level, own = 1.0, jax.random.fold_in(own_key, 6)
    for axis_at, shards_of in cuts:
        draws = jnp.exp(jax.random.uniform(jax.random.fold_in(own, axis_at), (shards_of,), jnp.float32, low / len(cuts), top_value / len(cuts)))
        level = level * jnp.repeat(draws, dims[axis_at] // shards_of).reshape([-1 if axis == axis_at else 1 for axis in range(len(dims))])
    return level


def length_profile(number_of, total, reach, skew):
    portions = [(1 << 20) // math.isqrt(grade ** skew) + 1 for grade in range(2, number_of + 1)]
    spare, given = total - reach - (number_of - 1), [1] * (number_of - 1)
    while spare > 0:
        free = [i for i in range(number_of - 1) if given[i] < reach]
        whole, left = sum([portions[i] for i in free]), spare
        for i in free:
            extra = min(reach - given[i], max(1, left * portions[i] // whole), spare)
            given[i] = given[i] + extra
            spare = spare - extra
    return np.array([reach] + given)


def uneven(rng, count, total, most, lean):
    if count == 2:
        one = jax.random.randint(rng, (), max(1, total - most), min(most, total - 1) + 1)
        return jnp.stack([one, total - one])
    tallies = jnp.asarray(length_profile(count, total, most, lean), jnp.int32)
    twos = (count - 1) // 2
    donor, taker = tallies[1:1 + 2 * twos:2], tallies[2:2 + 2 * twos:2]
    margin = jnp.minimum(donor - 1, most - taker)
    shifted = jax.random.randint(jax.random.fold_in(rng, 1), (twos,), 0, 1 << 20) % (margin + 1)
    tallies = tallies.at[1:1 + 2 * twos:2].set(donor - shifted).at[2:2 + 2 * twos:2].set(taker + shifted)
    return tallies[jax.random.permutation(jax.random.fold_in(rng, 2), count)]


def centred(stream_key, shape, spread, limit, cuts=(), kind=jnp.bfloat16):
    array = spread * jax.random.normal(stream_key, shape, jnp.float32)
    if cuts:
        array = array * block_scale(stream_key, shape, cuts, -0.22, 0.18)
    return jnp.clip(array, -limit, limit).astype(kind)


def setup_inputs(seed: int = 0, part: int = 0) -> dict:
    arg_keys = jax.random.split(jax.random.key(seed), 13)
    part_keys = jax.random.split(jax.random.fold_in(arg_keys[12], part), 13)
    return {
        "x_in": centred(part_keys[0], (TOKENS, HEADS * P_SIZE), 1.0, 6.0, ((0, 16), (1, 2))),
        "bc_in": centred(part_keys[1], (TOKENS, 2, GROUPS * N), 0.5, 4.0, ((0, 16), (2, 2))),
        "conv_x": centred(arg_keys[2], (CONV, HEADS * P_SIZE), CONV ** -0.5, 3.0, ((1, 2),), jnp.float32),
        "conv_bc": centred(arg_keys[3], (CONV, 2, GROUPS * N), CONV ** -0.5, 3.0, ((2, 2),), jnp.float32),
        "dt_raw": jnp.clip(-4.0 + 5.0 * jax.random.uniform(part_keys[4], (HEADS, TOKENS), jnp.float32) ** block_scale(part_keys[4], (HEADS, TOKENS), ((0, 2), (1, 16)), -0.2, 0.2), -4.0, 1.0),
        "rate": jnp.clip(jnp.exp(math.log(0.1) - 5.809143 * jax.random.uniform(arg_keys[5], (HEADS,), jnp.float32) ** block_scale(arg_keys[5], (HEADS,), ((0, 2),), -0.2, 0.2)), 0.0003, 0.1),
        "grad_ssd": centred(part_keys[6], (TOKENS, HEADS * P_SIZE), 1.0, 6.0, ((0, 16), (1, 2))),
        "query": draw_query(jax.random.fold_in(jax.random.fold_in(arg_keys[12], part), 71), part),
        "key": draw_key(jax.random.fold_in(jax.random.fold_in(arg_keys[12], part), 71), part),
        "value": centred(part_keys[9], (TOKENS, KVHEADS * HD), 1.0, 6.0, ((0, 16), (1, 2))),
        "d_out": centred(part_keys[10], (TOKENS, QHEADS * HD), 1.0, 6.0, ((0, 16), (1, 2))),
        "doc_lengths": uneven(part_keys[11], DOCS, TOKENS, TOKENS // 2, 2).astype(jnp.int32),
    }


HIGH = lax.Precision.HIGHEST
NEG_BIG = -1e+30

def doc_starts(doc_lengths):
    doc_ends = jnp.cumsum(doc_lengths)
    return (doc_ends - doc_lengths).astype(jnp.int32)

def segment_of(positions, starts):
    hits = (positions[:, None] >= starts[None, :]).astype(jnp.int32)
    return (lax.optimization_barrier(jnp.sum(hits, axis=1)) - 1).astype(jnp.int32)

def start_flags(positions, starts):
    return jnp.any(positions[:, None] == starts[None, :], axis=1).astype(jnp.float32)

def conv_silu(extended, weight, seg_ext):
    tap_count = weight.shape[0]
    row_count = extended.shape[0] - tap_count + 1
    last_seg = seg_ext[tap_count - 1:]
    shape_tail = (1,) * (extended.ndim - 1)
    running = jnp.zeros((row_count,) + extended.shape[1:], jnp.float32)
    for tap_index in range(tap_count):
        keep_mask = (seg_ext[tap_index:tap_index + row_count] == last_seg).astype(jnp.float32)
        running = running + extended[tap_index:tap_index + row_count] * weight[tap_index] * keep_mask.reshape((row_count,) + shape_tail)
    return jax.nn.silu(running)

def block_terms(x_conv, b_matrix, c_matrix, step_size, flags, rate_grid):
    log_decay = -step_size * rate_grid
    cum_log = jnp.cumsum(log_decay, axis=1)
    count_ids = jnp.cumsum(flags, axis=1)
    span = x_conv.shape[1]
    order_ids = jnp.arange(span, dtype=jnp.int32)
    causal = order_ids[:, None] >= order_ids[None, :]
    same_doc = (count_ids[:, :, None] == count_ids[:, None, :]) & causal[None]
    log_gap = cum_log[:, :, None] - cum_log[:, None, :]
    decay_grid = jnp.exp(jnp.where(same_doc[:, :, :, None, None], log_gap, NEG_BIG))
    inner_cb = jnp.einsum('ktgn,ksgn->ktsg', c_matrix, b_matrix, precision=HIGH)
    scores = decay_grid * inner_cb[..., None] * step_size[:, None]
    y_intra = jnp.einsum('ktsge,ksgep->ktgep', scores, x_conv, precision=HIGH)
    keep_mask = (count_ids == 0).astype(jnp.float32)
    lead_decay = jnp.exp(cum_log) * keep_mask[:, :, None, None]
    tail_same = count_ids == count_ids[:, -1:]
    tail_decay = jnp.exp(jnp.where(tail_same[:, :, None, None], cum_log[:, -1:] - cum_log, NEG_BIG)) * step_size
    s_local = jnp.einsum('ksge,ksgep,ksgn->kgepn', tail_decay, x_conv, b_matrix, precision=HIGH)
    block_decay = jnp.exp(cum_log[:, -1]) * keep_mask[:, -1][:, None, None]
    return (y_intra, lead_decay, s_local, block_decay)

def chain_output(y_intra, lead_decay, c_matrix, s_local, block_decay, start_state):

    def advance(state_now, block_item):
        s_add, factor = block_item
        return (factor[:, :, None, None] * state_now + s_add, state_now)
    final_state, inits = lax.scan(advance, start_state, (s_local, block_decay))
    carried = jnp.einsum('ktgn,kgepn->ktgep', c_matrix, inits, precision=HIGH)
    return (y_intra + lead_decay[..., None] * carried, final_state)

def mamba_part(x_in, bc_in, conv_x, conv_bc, dt_raw, rate, grad_ssd, positions, starts):
    segment = segment_of(positions, starts)
    seg_ext = jnp.concatenate([jnp.full((CONV - 1,), -1, jnp.int32), segment])
    block_count = TOKENS // STRETCH
    flags = start_flags(positions, starts).reshape(block_count, STRETCH)
    per_group = HEADS // GROUPS
    rate_grid = rate.astype(jnp.float32).reshape(GROUPS, per_group)

    def forward(x_values, bc_values, weight_x, weight_bc, dt_values):
        ext_x = jnp.concatenate([jnp.zeros((CONV - 1, x_values.shape[1]), jnp.float32), x_values])
        ext_bc = jnp.concatenate([jnp.zeros((CONV - 1,) + bc_values.shape[1:], jnp.float32), bc_values])
        x_conv = conv_silu(ext_x, weight_x, seg_ext).reshape(block_count, STRETCH, GROUPS, per_group, P_SIZE)
        bc_conv = conv_silu(ext_bc, weight_bc, seg_ext)
        b_matrix = bc_conv[:, 0].reshape(block_count, STRETCH, GROUPS, N)
        c_matrix = bc_conv[:, 1].reshape(block_count, STRETCH, GROUPS, N)
        step_size = jax.nn.softplus(dt_values).T.reshape(block_count, STRETCH, GROUPS, per_group)
        y_intra, lead_decay, s_local, block_decay = block_terms(x_conv, b_matrix, c_matrix, step_size, flags, rate_grid)
        start_state = jnp.zeros((GROUPS, per_group, P_SIZE, N), jnp.float32)
        y_out, final_state = chain_output(y_intra, lead_decay, c_matrix, s_local, block_decay, start_state)
        return y_out.reshape(TOKENS, HEADS * P_SIZE)
    _, pull_back = jax.vjp(forward, x_in.astype(jnp.float32), bc_in.astype(jnp.float32), conv_x.astype(jnp.float32), conv_bc.astype(jnp.float32), dt_raw.astype(jnp.float32))
    grad_x, grad_bc, grad_wx, grad_wbc, grad_dt = pull_back(grad_ssd.astype(jnp.float32))
    return (grad_x.astype(jnp.bfloat16), grad_bc.astype(jnp.bfloat16), grad_dt, grad_wx, grad_wbc)

def attention_part(query, key, value, d_out, segment):
    score_scale = HD ** (-0.5)
    order_ids = jnp.arange(TOKENS, dtype=jnp.int32)
    allowed = (order_ids[:, None] >= order_ids[None, :]) & (segment[:, None] == segment[None, :])
    q_heads = query.reshape(TOKENS, QHEADS, HD).transpose(1, 0, 2)
    o_heads = d_out.reshape(TOKENS, QHEADS, HD).transpose(1, 0, 2)
    k_heads = jnp.repeat(key.reshape(TOKENS, KVHEADS, HD).transpose(1, 0, 2), Q_PER_KV, axis=0)
    v_heads = jnp.repeat(value.reshape(TOKENS, KVHEADS, HD).transpose(1, 0, 2), Q_PER_KV, axis=0)

    def head_grads(head_items):
        q_float, k_float, v_float, o_float = [member.astype(jnp.float32) for member in head_items]
        scores = jnp.einsum('id,jd->ij', q_float, k_float, precision=HIGH) * score_scale
        scores = jnp.where(allowed, scores, NEG_BIG)
        row_top = lax.optimization_barrier(jnp.max(scores, axis=-1, keepdims=True))
        exp_weights = jnp.where(allowed, jnp.exp(scores - row_top), 0.0)
        log_total = row_top + jnp.log(lax.optimization_barrier(jnp.sum(exp_weights, axis=-1, keepdims=True)))
        prob_f = jnp.where(allowed, jnp.exp(scores - log_total), 0.0)
        d_prob = jnp.einsum('id,jd->ij', o_float, v_float, precision=HIGH)
        weighted = lax.optimization_barrier(jnp.sum(prob_f * d_prob, axis=-1, keepdims=True))
        d_score = prob_f * (d_prob - weighted)
        prob_b = lax.optimization_barrier(prob_f.astype(jnp.bfloat16)).astype(jnp.float32)
        score_b = lax.optimization_barrier(d_score.astype(jnp.bfloat16)).astype(jnp.float32)
        grad_v = jnp.einsum('ij,id->jd', prob_b, o_float, precision=HIGH)
        grad_k = jnp.einsum('ij,id->jd', score_b, q_float, precision=HIGH) * score_scale
        grad_q = jnp.einsum('ij,jd->id', score_b, k_float, precision=HIGH) * score_scale
        return (grad_q.astype(jnp.bfloat16), grad_k, grad_v)
    grad_q, grad_k, grad_v = lax.map(head_grads, (q_heads, k_heads, v_heads, o_heads))
    grad_q = grad_q.transpose(1, 0, 2).reshape(TOKENS, QHEADS * HD)
    grad_k = lax.optimization_barrier(jnp.sum(grad_k.reshape(KVHEADS, Q_PER_KV, TOKENS, HD), axis=1)).transpose(1, 0, 2).reshape(TOKENS, KVHEADS * HD)
    grad_v = lax.optimization_barrier(jnp.sum(grad_v.reshape(KVHEADS, Q_PER_KV, TOKENS, HD), axis=1)).transpose(1, 0, 2).reshape(TOKENS, KVHEADS * HD)
    return (grad_q, grad_k.astype(jnp.bfloat16), grad_v.astype(jnp.bfloat16))

def reference(x_in, bc_in, conv_x, conv_bc, dt_raw, rate, grad_ssd, query, key, value, d_out, doc_lengths):
    starts = doc_starts(doc_lengths)
    positions = jnp.arange(TOKENS, dtype=jnp.int32)
    grad_x, grad_bc, grad_dt, grad_wx, grad_wbc = mamba_part(x_in, bc_in, conv_x, conv_bc, dt_raw, rate, grad_ssd, positions, starts)
    segment = segment_of(positions, starts)
    grad_q, grad_k, grad_v = attention_part(query, key, value, d_out, segment)
    return (grad_x, grad_bc, grad_dt, grad_wx, grad_wbc, grad_q, grad_k, grad_v)
```

```python
import jax
import jax.numpy as jnp
from jax import lax
from jax.experimental import pallas as pl
from jax.experimental.pallas import tpu as pltpu
from jax.sharding import PartitionSpec as P

F32 = jnp.float32
BF16 = jnp.bfloat16
HD = 128
BLK = 128
TAPS = 4
BACK = 8
LOG2E = 1.4426950408889634
NEG_BIG = -1e30
HIGHEST = lax.Precision.HIGHEST


def dot_nn(a, b, precision=None):
    return lax.dot_general(
        a, b, (((1,), (0,)), ((), ())), precision=precision, preferred_element_type=F32
    )


def dot_nt(a, b):
    return lax.dot_general(a, b, (((1,), (1,)), ((), ())), preferred_element_type=F32)


def dot_tn(a, b):
    return lax.dot_general(a, b, (((0,), (0,)), ((), ())), preferred_element_type=F32)


def doc_bounds(doc_ref):
    s1 = doc_ref[0]
    s2 = s1 + doc_ref[1]
    s3 = s2 + doc_ref[2]
    return s1, s2, s3


def start_at(pos, bounds):
    s1, s2, s3 = bounds
    return jnp.where(pos >= s3, s3, jnp.where(pos >= s2, s2, jnp.where(pos >= s1, s1, 0)))


def next_start(pos, bounds, total):
    s1, s2, s3 = bounds
    return jnp.where(pos < s1, s1, jnp.where(pos < s2, s2, jnp.where(pos < s3, s3, total)))


def twice(a):
    return jnp.concatenate([a, a], axis=1)


def fold_rows(a):
    return jnp.sum(a.reshape(a.shape[0] // 8, 8, a.shape[1]), axis=0)


def ssm_kernel(
    doc_ref, idx_ref, rate_ref, r_ref, wx_ref, wbc_ref, out_ref,
    xs_s, xp_s, b_s, c_s, dsx_s, dsbc_s, st_s, ds_s,
    cols_s, elt_s, rx_s, ry_s, es_s, tapx_s, tapbc_s,
):
    blocks = r_ref.shape[0]
    total = blocks * BLK
    place = idx_ref[0]
    bounds = doc_bounds(doc_ref)
    rate0 = rate_ref[2 * place]
    rate1 = rate_ref[2 * place + 1]
    group = place // (blocks // 2)
    wx = wx_ref[:, pl.ds(pl.multiple_of(place * 256, 256), 256)]
    wbc = jnp.concatenate(
        [
            wbc_ref[:, pl.ds(pl.multiple_of(group * 128, 128), 128)],
            wbc_ref[:, pl.ds(pl.multiple_of(256 + group * 128, 128), 128)],
        ],
        axis=1,
    )

    raw = jnp.concatenate(
        [
            jnp.sum(r_ref[c, 3 * BLK : 3 * BLK + 16, :].astype(F32), axis=0, keepdims=True)
            for c in range(blocks)
        ],
        axis=0,
    )
    raw = jnp.concatenate([raw[:, :128], raw[:, 128:]], axis=0)
    step = jnp.log(1.0 + jnp.exp(raw))
    sig = 1.0 / (1.0 + jnp.exp(-raw))
    row_ids = lax.broadcasted_iota(jnp.int32, (2 * blocks, 128), 0)
    rate = jnp.where(row_ids < blocks, rate0, rate1)
    ii = lax.broadcasted_iota(jnp.int32, (128, 128), 0)
    jj = lax.broadcasted_iota(jnp.int32, (128, 128), 1)
    cum = dot_nn(-step * rate, (ii <= jj).astype(F32), HIGHEST)
    u_rows = step * jnp.exp(-cum)
    v_rows = jnp.exp(cum)
    last = jnp.broadcast_to(v_rows[:, 127:128], (2 * blocks, 128))
    for c in range(blocks):
        cols_s[c] = jnp.concatenate(
            [
                u_rows[c : c + 1], u_rows[blocks + c : blocks + c + 1],
                v_rows[c : c + 1], v_rows[blocks + c : blocks + c + 1],
                jnp.zeros((4, 128), F32),
            ],
            axis=0,
        )
        elt_s[c] = jnp.broadcast_to(
            jnp.concatenate([last[c : c + 1], last[blocks + c : blocks + c + 1]], axis=1), (8, 256)
        )

    edge = jnp.zeros((8, 256), F32)
    st_s[0] = jnp.zeros((128, 256), F32)

    def columns(c, first):
        cols = cols_s[c].T
        return jnp.concatenate(
            [jnp.broadcast_to(cols[:, first + h : first + h + 1], (128, 128)) for h in (0, 1)],
            axis=1,
        )

    def conv(edge, value, weight, keeps):
        win = jnp.concatenate([edge, value], axis=0)
        pre = value * weight[TAPS - 1 : TAPS]
        for d in range(1, TAPS):
            pre = pre + jnp.where(keeps[d - 1], win[8 - d : 8 - d + BLK], 0.0) * weight[TAPS - 1 - d : TAPS - d]
        sg = 1.0 / (1.0 + jnp.exp(-pre))
        val = pre * sg
        return val, sg + val * (1.0 - sg)

    def forward(c, carry):
        base = pl.multiple_of(c * BLK, BLK)
        edge_x, edge_bc = carry
        x = r_ref[c, 0:BLK].astype(F32)
        bc_raw = r_ref[c, 2 * BLK : 3 * BLK].astype(F32)
        pos = base + ii
        dist = twice(pos - start_at(pos, bounds))
        keeps = [dist >= d for d in range(1, TAPS)]
        xs, dsx = conv(edge_x, x, wx, keeps)
        bc, dsbc = conv(edge_bc, bc_raw, wbc, keeps)
        xs_s[c] = xs
        dsx_s[c] = dsx
        dsbc_s[c] = dsbc
        b = bc[:, :128].astype(BF16)
        b_s[c] = b
        c_s[c] = bc[:, 128:].astype(BF16)
        xp = xs * columns(c, 0)
        xp_s[c] = xp.astype(BF16)
        last_start = start_at(base + BLK - 1, bounds)
        xpm = jnp.where(twice(pos) >= last_start, xp, 0.0).astype(BF16)
        elt = elt_s[c][0:1]
        keep = jnp.where(last_start < base, elt, 0.0)
        st_s[c + 1] = keep * st_s[c] + elt * dot_tn(b, xpm)
        return x[BLK - 8 :], bc_raw[BLK - 8 :]

    lax.fori_loop(0, blocks, forward, (edge, edge))

    ds_s[...] = jnp.zeros((128, 256), F32)
    tapx_s[...] = jnp.zeros((TAPS, 8, 256), F32)
    tapbc_s[...] = jnp.zeros((TAPS, 8, 256), F32)
    lane2 = lax.broadcasted_iota(jnp.int32, (16, 256), 1)
    row2 = lax.broadcasted_iota(jnp.int32, (16, 256), 0)
    pick = (lane2 // 128 == row2).astype(BF16)

    def head_sums(a):
        hi = a.astype(BF16)
        lo = (a - hi.astype(F32)).astype(BF16)
        return (dot_nt(pick, hi) + dot_nt(pick, lo))[0:8]

    def conv_back(grad, edge, raw_in, weight, ends, taps):
        win = jnp.concatenate([grad, edge], axis=0)
        total_grad = grad * weight[TAPS - 1 : TAPS]
        taps[TAPS - 1] += fold_rows(grad * raw_in)
        for d in range(1, TAPS):
            moved = jnp.where(ends[d - 1], win[d : d + BLK], 0.0)
            total_grad = total_grad + moved * weight[TAPS - 1 - d : TAPS - d]
            taps[TAPS - 1 - d] += fold_rows(moved * raw_in)
        return total_grad

    def backward(lap, carry):
        c = blocks - 1 - lap
        base = pl.multiple_of(c * BLK, BLK)
        pos = base + ii
        start = start_at(pos, bounds)
        last_start = start_at(base + BLK - 1, bounds)
        causal = (jj <= ii) & (base + jj >= start)
        leads = start < base
        tails = pos >= last_start
        b = b_s[c]
        cc = c_s[c]
        xp = xp_s[c]
        xs = xs_s[c]
        g = r_ref[c, BLK : 2 * BLK].astype(F32)
        u = columns(c, 0)
        v = columns(c, 2)
        gv = g * v
        gp = gv.astype(BF16)
        elt = elt_s[c][0:1]
        ds = ds_s[...]
        es_s[c] = fold_rows(ds * st_s[c + 1])
        sb = st_s[c].astype(BF16)
        ds_e = elt * ds
        dsb = ds_e.astype(BF16)
        w = jnp.where(causal, dot_nt(cc, b), 0.0).astype(BF16)
        cm = jnp.where(leads, cc.astype(F32), 0.0).astype(BF16)
        bm = jnp.where(tails, b.astype(F32), 0.0).astype(BF16)
        yv = dot_nn(w, xp) + dot_nn(cm, sb)
        dxp = dot_tn(w, gp) + dot_nn(bm, dsb)
        z = jnp.where(causal, dot_nt(gp, xp), 0.0).astype(BF16)
        dc = dot_nn(z, b) + jnp.where(leads, dot_nt(gp, sb), 0.0)
        db = dot_tn(z, cc) + jnp.where(tails, dot_nt(xp, dsb), 0.0)
        ds_s[...] = jnp.where(last_start < base, ds_e, 0.0) + dot_tn(cm, gp)
        dx = u * dxp
        rx_s[c] = head_sums(xs * dx)
        ry_s[c] = head_sums(gv * yv)
        left = twice(next_start(pos, bounds, total) - pos)
        ends = [left > d for d in range(1, TAPS)]
        edge_x, edge_bc = carry
        pre_x = dx * dsx_s[c]
        pre_bc = jnp.concatenate([db, dc], axis=1) * dsbc_s[c]
        x = r_ref[c, 0:BLK].astype(F32)
        bc_raw = r_ref[c, 2 * BLK : 3 * BLK].astype(F32)
        out_ref[c, 0:BLK] = conv_back(pre_x, edge_x, x, wx, ends, tapx_s).astype(BF16)
        out_ref[c, BLK : 2 * BLK] = conv_back(
            pre_bc, edge_bc, bc_raw, wbc, ends, tapbc_s
        ).astype(BF16)
        return pre_x[0:8], pre_bc[0:8]

    lax.fori_loop(0, blocks, backward, (edge, edge))

    xdx = jnp.concatenate([rx_s[c][h : h + 1] for h in (0, 1) for c in range(blocks)], axis=0)
    gyy = jnp.concatenate([ry_s[c][h : h + 1] for h in (0, 1) for c in range(blocks)], axis=0)
    ends = jnp.concatenate(
        [
            jnp.sum(es_s[c][:, 128 * h : 128 * h + 128], axis=0, keepdims=True)
            for h in (0, 1)
            for c in range(blocks)
        ],
        axis=0,
    )
    d_log = dot_nn(gyy - xdx, (ii >= jj).astype(F32), HIGHEST) + jnp.sum(ends, axis=1, keepdims=True)
    d_raw = (xdx / step - rate * d_log) * sig
    d_raw = jnp.concatenate([d_raw[:blocks], d_raw[blocks:]], axis=1)
    raw_hi = d_raw.astype(BF16).astype(F32)
    raw_lo = d_raw - raw_hi
    tapx = jnp.concatenate([jnp.sum(tapx_s[k], axis=0, keepdims=True) for k in range(TAPS)], axis=0)
    tapbc = jnp.concatenate([jnp.sum(tapbc_s[k], axis=0, keepdims=True) for k in range(TAPS)], axis=0)
    tapx_hi = tapx.astype(BF16).astype(F32)
    rest = jnp.concatenate([tapx_hi, tapx - tapx_hi, tapbc, jnp.zeros((2, 256), F32)], axis=0)
    for c in range(blocks):
        out_ref[c, 2 * BLK : 2 * BLK + 16] = jnp.concatenate(
            [raw_hi[c : c + 1], raw_lo[c : c + 1], rest], axis=0
        ).astype(BF16)


def ssm_core(doc_lengths, place, rate, received, weight_x, weight_bc):
    blocks = received.shape[0]
    smem = pl.BlockSpec(memory_space=pltpu.SMEM)
    vmem = pl.BlockSpec(memory_space=pltpu.VMEM)

    def scratch(*shape, dtype=F32):
        return pltpu.VMEM(shape, dtype)

    return pl.pallas_call(
        ssm_kernel,
        out_shape=jax.ShapeDtypeStruct((blocks, 2 * BLK + 16, 256), BF16),
        in_specs=[smem, smem, smem, vmem, vmem, vmem],
        out_specs=vmem,
        scratch_shapes=[
            scratch(blocks, BLK, 256),
            scratch(blocks, BLK, 256, dtype=BF16),
            scratch(blocks, BLK, 128, dtype=BF16),
            scratch(blocks, BLK, 128, dtype=BF16),
            scratch(blocks, BLK, 256),
            scratch(blocks, BLK, 256),
            scratch(blocks + 1, 128, 256),
            scratch(128, 256),
            scratch(blocks, 8, 128),
            scratch(blocks, 8, 256),
            scratch(blocks, 8, 128),
            scratch(blocks, 8, 128),
            scratch(blocks, 8, 256),
            scratch(TAPS, 8, 256),
            scratch(TAPS, 8, 256),
        ],
        compiler_params=pltpu.CompilerParams(vmem_limit_bytes=56 * 2**20),
        cost_estimate=pl.CostEstimate(flops=3 * 10**9, bytes_accessed=6 * 2**20, transcendentals=4 * 10**6),
        name="mixer",
    )(doc_lengths, place, rate, received, weight_x, weight_bc)


def attention_kernel(doc_ref, r_ref, out_ref, kpad, vpad, ktpad, dk_s, dv_s, s_s, p_s):
    blocks = r_ref.shape[0]
    bounds = doc_bounds(doc_ref)
    scale = HD ** (-0.5)
    reach = BACK + 2
    kpad[0:BACK] = jnp.zeros((BACK, BLK, HD), BF16)
    vpad[0:BACK] = jnp.zeros((BACK, BLK, HD), BF16)
    ktpad[0:BACK] = jnp.zeros((BACK, HD, BLK), BF16)
    dk_s[...] = jnp.zeros(dk_s.shape, F32)
    dv_s[...] = jnp.zeros(dv_s.shape, F32)

    def fill(c, carry):
        k = r_ref[c, 2 * BLK : 3 * BLK]
        kpad[BACK + c] = k
        vpad[BACK + c] = r_ref[c, 3 * BLK : 4 * BLK]
        ktpad[BACK + c] = k.T
        return carry

    lax.fori_loop(0, blocks, fill, 0)
    jrow = lax.broadcasted_iota(jnp.int32, (BLK, 2 * BLK), 0)
    icol = lax.broadcasted_iota(jnp.int32, (BLK, 2 * BLK), 1)

    def rows8(a):
        return a.reshape(BLK // 8, 8, 2 * BLK)

    def turn(i, carry):
        q = jnp.concatenate([r_ref[2 * i, 0:BLK], r_ref[2 * i + 1, 0:BLK]], axis=0)
        do = jnp.concatenate([r_ref[2 * i, BLK : 2 * BLK], r_ref[2 * i + 1, BLK : 2 * BLK]], axis=0)
        first = (2 * i - BACK) * BLK
        ipos = 2 * i * BLK + icol
        start = start_at(ipos, bounds)
        top = jnp.full((8, 2 * BLK), NEG_BIG, F32)
        for b in range(reach):
            jpos = first + b * BLK + jrow
            allowed = jpos >= start
            if b >= BACK:
                allowed = allowed & (jpos <= ipos)
            s = jnp.where(allowed, dot_nt(kpad[2 * i + b], q), NEG_BIG)
            s_s[b] = s
            top = jnp.maximum(top, jnp.max(rows8(s), axis=0))
            p_s[b] = dot_nt(vpad[2 * i + b], do)
        top = jnp.max(top, axis=0, keepdims=True) * (scale * LOG2E)
        norm = jnp.zeros((8, 2 * BLK), F32)
        mean = jnp.zeros((8, 2 * BLK), F32)
        for b in range(reach):
            e = jnp.exp2(s_s[b] * (scale * LOG2E) - top)
            s_s[b] = e
            norm = norm + jnp.sum(rows8(e), axis=0)
            mean = mean + jnp.sum(rows8(e * p_s[b]), axis=0)
        inverse = 1.0 / jnp.sum(norm, axis=0, keepdims=True)
        mean = jnp.sum(mean, axis=0, keepdims=True) * inverse
        dqt = jnp.zeros((HD, 2 * BLK), F32)
        for b in range(reach):
            prob = s_s[b] * inverse
            grad = (prob * (p_s[b] - mean)).astype(BF16)
            dv_s[2 * i + b] += dot_nn(prob.astype(BF16), do)
            dk_s[2 * i + b] += dot_nn(grad, q)
            dqt = dqt + dot_nn(ktpad[2 * i + b], grad)
        dqt = dqt * scale
        out_ref[2 * i, 0:BLK] = dqt[:, :BLK].T.astype(BF16)
        out_ref[2 * i + 1, 0:BLK] = dqt[:, BLK:].T.astype(BF16)
        return carry

    lax.fori_loop(0, blocks // 2, turn, 0)

    def drain(c, carry):
        out_ref[c, BLK : 2 * BLK] = (dk_s[BACK + c] * scale).astype(BF16)
        out_ref[c, 2 * BLK : 3 * BLK] = dv_s[BACK + c].astype(BF16)
        return carry

    lax.fori_loop(0, blocks, drain, 0)


def attention_core(doc_lengths, received):
    blocks = received.shape[0]
    smem = pl.BlockSpec(memory_space=pltpu.SMEM)
    vmem = pl.BlockSpec(memory_space=pltpu.VMEM)
    padded = blocks + BACK
    return pl.pallas_call(
        attention_kernel,
        out_shape=jax.ShapeDtypeStruct((blocks, 3 * BLK, HD), BF16),
        in_specs=[smem, vmem],
        out_specs=vmem,
        scratch_shapes=[
            pltpu.VMEM((padded, BLK, HD), BF16),
            pltpu.VMEM((padded, BLK, HD), BF16),
            pltpu.VMEM((padded, HD, BLK), BF16),
            pltpu.VMEM((padded, BLK, HD), F32),
            pltpu.VMEM((padded, BLK, HD), F32),
            pltpu.VMEM((BACK + 2, BLK, 2 * BLK), F32),
            pltpu.VMEM((BACK + 2, BLK, 2 * BLK), F32),
        ],
        compiler_params=pltpu.CompilerParams(vmem_limit_bytes=40 * 2**20),
        cost_estimate=pl.CostEstimate(flops=4 * 10**9, bytes_accessed=4 * 2**20, transcendentals=3 * 10**6),
        name="attention",
    )(doc_lengths, received)


def swap(a):
    return lax.all_to_all(a, "ctx", 0, 0, tiled=True)


def split3(a):
    hi = lax.reduce_precision(a, 8, 7)
    mid = lax.reduce_precision(a - hi, 8, 7)
    return hi.astype(BF16), mid.astype(BF16), (a - hi - mid).astype(BF16)


def shards(
    x_in, bc_in, conv_x, conv_bc, dt_raw, rate, grad_ssd, query, key, value, d_out, doc_lengths
):
    ctx = lax.axis_size("ctx")
    rows = x_in.shape[0]
    place = lax.axis_index("ctx").astype(jnp.int32).reshape(1)

    def by_head(a, width):
        return a.reshape(rows, ctx, width).transpose(1, 0, 2)

    def by_group(a):
        two = a.reshape(rows, 2, HD).transpose(1, 0, 2)
        return jnp.repeat(two, ctx // 2, axis=0)

    bc_sent = bc_in.reshape(rows, 2, 2, HD).transpose(2, 0, 1, 3).reshape(2, rows, 2 * HD)
    dt_sent = jnp.stack(split3(dt_raw), axis=0).reshape(3, ctx, 2 * rows).transpose(1, 0, 2)
    sent = jnp.concatenate(
        [
            by_head(x_in, 2 * HD),
            by_head(grad_ssd, 2 * HD),
            jnp.repeat(bc_sent, ctx // 2, axis=0),
            jnp.pad(dt_sent, ((0, 0), (0, 13), (0, 0))),
        ],
        axis=1,
    )
    sent_attention = jnp.concatenate(
        [by_head(query, HD), by_head(d_out, HD), by_group(key), by_group(value)], axis=1
    )
    got = swap(sent)
    got_attention = swap(sent_attention)
    back = swap(
        ssm_core(doc_lengths, place, rate, got, conv_x, conv_bc.reshape(TAPS, 4 * HD))
    )
    back_attention = swap(attention_core(doc_lengths, got_attention))

    d_x = back[:, :rows].transpose(1, 0, 2).reshape(rows, ctx * 2 * HD)
    d_bc = jnp.sum(back[:, rows : 2 * rows].astype(F32).reshape(2, ctx // 2, rows, 2, HD), axis=1)
    d_bc = d_bc.transpose(1, 2, 0, 3).reshape(rows, 2, 2 * HD).astype(BF16)
    small = back[:, 2 * rows :].astype(F32)
    d_dt = (small[:, 0] + small[:, 1]).reshape(2 * ctx, rows)
    d_wx = (small[:, 2:6] + small[:, 6:10]).transpose(1, 0, 2).reshape(TAPS, ctx * 2 * HD)
    d_wbc = jnp.sum(small[:, 10:14].reshape(2, ctx // 2, TAPS, 2, HD), axis=1)
    d_wbc = d_wbc.transpose(1, 2, 0, 3).reshape(TAPS, 2, 2 * HD)
    d_query = back_attention[:, :rows].transpose(1, 0, 2).reshape(rows, ctx * HD)

    def group_sum(a):
        summed = jnp.sum(a.astype(F32).reshape(2, ctx // 2, rows, HD), axis=1)
        return summed.transpose(1, 0, 2).reshape(rows, 2 * HD).astype(BF16)

    d_key = group_sum(back_attention[:, rows : 2 * rows])
    d_value = group_sum(back_attention[:, 2 * rows :])
    return (d_x, d_bc, d_dt, d_wx, d_wbc, d_query, d_key, d_value)


def solution(mesh):
    tokens = P(("dp", "ctx"), "head")
    in_specs = (
        tokens,
        P(("dp", "ctx"), None, "head"),
        P(None, "head"),
        P(None, None, "head"),
        P("head", ("dp", "ctx")),
        P("head"),
        tokens,
        tokens,
        tokens,
        tokens,
        tokens,
        P("dp"),
    )
    out_specs = (
        tokens,
        P(("dp", "ctx"), None, "head"),
        P("head", ("dp", "ctx")),
        P("dp", "head"),
        P("dp", None, "head"),
        tokens,
        tokens,
        tokens,
    )
    return jax.shard_map(shards, mesh=mesh, in_specs=in_specs, out_specs=out_specs, check_vma=False)
```

```python
import jax
import jax.numpy as jnp
from jax import lax
from jax.experimental import pallas as pl
from jax.experimental.pallas import tpu as pltpu
from jax.sharding import PartitionSpec as P

F32 = jnp.float32
BF16 = jnp.bfloat16
HD = 128
BLK = 128
TAPS = 4
BACK = 8
LOG2E = 1.4426950408889634
NEG_BIG = -1e30
UNROLL = 4


def dot_nn(a, b):
    return lax.dot_general(a, b, (((1,), (0,)), ((), ())), preferred_element_type=F32)


def dot_nt(a, b):
    return lax.dot_general(a, b, (((1,), (1,)), ((), ())), preferred_element_type=F32)


def dot_tn(a, b):
    return lax.dot_general(a, b, (((0,), (0,)), ((), ())), preferred_element_type=F32)


def doc_bounds(doc_ref):
    s1 = doc_ref[0]
    s2 = s1 + doc_ref[1]
    s3 = s2 + doc_ref[2]
    return s1, s2, s3


def start_at(pos, bounds):
    s1, s2, s3 = bounds
    return jnp.where(pos >= s3, s3, jnp.where(pos >= s2, s2, jnp.where(pos >= s1, s1, 0)))


def next_start(pos, bounds, total):
    s1, s2, s3 = bounds
    return jnp.where(pos < s1, s1, jnp.where(pos < s2, s2, jnp.where(pos < s3, s3, total)))


def twice(a):
    return jnp.concatenate([a, a], axis=1)


def fold_rows(a):
    return jnp.sum(a.reshape(a.shape[0] // 8, 8, a.shape[1]), axis=0)


def split3(a):
    hi = a.astype(BF16)
    rest = a - hi.astype(F32)
    mid = rest.astype(BF16)
    return hi, mid, (rest - mid.astype(F32)).astype(BF16)


def dot_exact(a, ones):
    rows = a.shape[0]
    out = dot_nn(jnp.concatenate(split3(a), axis=0), ones.astype(BF16))
    return out[:rows] + out[rows : 2 * rows] + out[2 * rows :]


def ssm_kernel(
    doc_ref, idx_ref, rate_ref, r_ref, wx_ref, wbc_ref, out_ref,
    xs_s, xp_s, u_s, b_s, c_s, bm_s, cm_s, dsx_s, dsbc_s, st_s, ds_s,
    cols_s, elt_s, x2_s, y2_s, es_s, tapx_s, tapbc_s,
):
    blocks = r_ref.shape[0]
    total = blocks * BLK
    place = idx_ref[0]
    bounds = doc_bounds(doc_ref)
    rate0 = rate_ref[2 * place]
    rate1 = rate_ref[2 * place + 1]
    group = place // (blocks // 2)
    wx = wx_ref[:, pl.ds(pl.multiple_of(place * 256, 256), 256)]
    wbc = jnp.concatenate(
        [
            wbc_ref[:, pl.ds(pl.multiple_of(group * 128, 128), 128)],
            wbc_ref[:, pl.ds(pl.multiple_of(256 + group * 128, 128), 128)],
        ],
        axis=1,
    )

    for c in range(blocks):
        row = jnp.sum(r_ref[c, 3 * BLK : 3 * BLK + 16, :].astype(F32), axis=0, keepdims=True)
        x2_s[c : c + 1] = row[:, :128]
        x2_s[blocks + c : blocks + c + 1] = row[:, 128:]
    raw = x2_s[...]
    step = jnp.log(1.0 + jnp.exp(raw))
    sig = 1.0 / (1.0 + jnp.exp(-raw))
    row_ids = lax.broadcasted_iota(jnp.int32, (2 * blocks, 128), 0)
    rate = jnp.where(row_ids < blocks, rate0, rate1)
    ii = lax.broadcasted_iota(jnp.int32, (128, 128), 0)
    jj = lax.broadcasted_iota(jnp.int32, (128, 128), 1)
    cum = dot_exact(-step * rate, (ii <= jj).astype(F32))
    v_rows = jnp.exp(cum)
    u_hi, u_lo, _ = split3(step * jnp.exp(-cum))
    v_hi, v_lo, _ = split3(v_rows)
    last = jnp.broadcast_to(v_rows[:, 127:128], (2 * blocks, 128))
    pieces = [a.astype(F32) for a in (u_hi, u_lo, v_hi, v_lo)]
    for c in range(blocks):
        rows = [a[at : at + 1] for a in pieces for at in (c, blocks + c)]
        cols_s[c] = jnp.concatenate(rows, axis=0)
        elt_s[c] = jnp.broadcast_to(
            jnp.concatenate([last[c : c + 1], last[blocks + c : blocks + c + 1]], axis=1), (8, 256)
        )
    row8 = lax.broadcasted_iota(jnp.int32, (8, 512), 0)
    lane8 = lax.broadcasted_iota(jnp.int32, (8, 512), 1) // 128
    spread = ((lane8 // 2 == row8 // 4) & (lane8 % 2 == row8 % 2)).astype(BF16)

    edge = jnp.zeros((8, 256), F32)
    st_s[0] = jnp.zeros((128, 256), F32)

    def conv(edge, value, weight, keeps):
        win = jnp.concatenate([edge, value], axis=0)
        pre = value * weight[TAPS - 1 : TAPS]
        for d in range(1, TAPS):
            pre = pre + jnp.where(keeps[d - 1], win[8 - d : 8 - d + BLK], 0.0) * weight[TAPS - 1 - d : TAPS - d]
        sg = 0.5 * jnp.tanh(0.5 * pre) + 0.5
        val = pre * sg
        return val, sg + val * (1.0 - sg)

    def forward(c, carry):
        base = pl.multiple_of(c * BLK, BLK)
        edge_x, edge_bc = carry
        x = r_ref[c, 0:BLK].astype(F32)
        bc_raw = r_ref[c, 2 * BLK : 3 * BLK].astype(F32)
        pos = base + ii
        start = start_at(pos, bounds)
        last_start = start_at(base + BLK - 1, bounds)
        tails = pos >= last_start
        dist = pos - start
        keeps = [twice(dist >= d) for d in range(1, TAPS)]
        xs, dsx = conv(edge_x, x, wx, keeps)
        bc, dsbc = conv(edge_bc, bc_raw, wbc, keeps)
        xs_s[c] = xs
        dsx_s[c] = dsx
        dsbc_s[c] = dsbc
        b = bc[:, :128]
        cc = bc[:, 128:]
        b_s[c] = b.astype(BF16)
        c_s[c] = cc.astype(BF16)
        bm = jnp.where(tails, b, 0.0).astype(BF16)
        bm_s[c] = bm
        cm_s[c] = jnp.where(start < base, cc, 0.0).astype(BF16)
        u = dot_tn(cols_s[c].astype(BF16), spread[:, :256])
        u_s[c] = u
        xp = (xs * u).astype(BF16)
        xp_s[c] = xp
        elt = elt_s[c][0:1]
        keep = jnp.where(last_start < base, elt, 0.0)
        st_s[c + 1] = keep * st_s[c] + elt * dot_tn(bm, xp)
        return x[BLK - 8 :], bc_raw[BLK - 8 :]

    lax.fori_loop(0, blocks, forward, (edge, edge), unroll=UNROLL)

    ds_s[...] = jnp.zeros((128, 256), F32)
    tapx_s[...] = jnp.zeros((TAPS, 8, 256), F32)
    tapbc_s[...] = jnp.zeros((TAPS, 8, 256), F32)
    lane2 = lax.broadcasted_iota(jnp.int32, (16, 256), 1)
    row2 = lax.broadcasted_iota(jnp.int32, (16, 256), 0)
    pick = (lane2 // 128 == row2).astype(BF16)

    def head_sums(out, c, a):
        sums = dot_nt(pick, a.astype(BF16))
        out[pl.ds(c, 1)] = sums[0:1]
        out[pl.ds(blocks + c, 1)] = sums[1:2]

    def conv_back(grad, edge, raw_in, weight, ends, taps):
        win = jnp.concatenate([grad, edge], axis=0)
        total_grad = grad * weight[TAPS - 1 : TAPS]
        taps[TAPS - 1] += fold_rows(grad * raw_in)
        for d in range(1, TAPS):
            moved = jnp.where(ends[d - 1], win[d : d + BLK], 0.0)
            total_grad = total_grad + moved * weight[TAPS - 1 - d : TAPS - d]
            taps[TAPS - 1 - d] += fold_rows(moved * raw_in)
        return total_grad

    def backward(lap, carry):
        c = blocks - 1 - lap
        base = pl.multiple_of(c * BLK, BLK)
        pos = base + ii
        start = start_at(pos, bounds)
        last_start = start_at(base + BLK - 1, bounds)
        causal = (jj <= ii) & (base + jj >= start)
        leads = start < base
        tails = pos >= last_start
        b = b_s[c]
        cc = c_s[c]
        xp = xp_s[c]
        cm = cm_s[c]
        gv = r_ref[c, BLK : 2 * BLK].astype(F32) * dot_tn(cols_s[c].astype(BF16), spread[:, 256:])
        gp = gv.astype(BF16)
        elt = elt_s[c][0:1]
        ds = ds_s[...]
        es_s[pl.ds(pl.multiple_of(c * 8, 8), 8)] = fold_rows(ds * st_s[c + 1])
        sb = st_s[c].astype(BF16)
        ds_e = elt * ds
        dsb = ds_e.astype(BF16)
        ds_s[...] = jnp.where(last_start < base, ds_e, 0.0) + dot_tn(cm, gp)
        w = jnp.where(causal, dot_nt(cc, b), 0.0).astype(BF16)
        yv = dot_nn(w, xp) + dot_nn(cm, sb)
        dxp = dot_tn(w, gp) + dot_nn(bm_s[c], dsb)
        z = jnp.where(causal, dot_nt(gp, xp), 0.0).astype(BF16)
        dc = dot_nn(z, b) + jnp.where(leads, dot_nt(gp, sb), 0.0)
        db = dot_tn(z, cc) + jnp.where(tails, dot_nt(xp, dsb), 0.0)
        dx = u_s[c] * dxp
        head_sums(x2_s, c, xs_s[c] * dx)
        head_sums(y2_s, c, gv * yv)
        left = next_start(pos, bounds, total) - pos
        ends = [twice(left > d) for d in range(1, TAPS)]
        edge_x, edge_bc = carry
        pre_x = dx * dsx_s[c]
        pre_bc = jnp.concatenate([db, dc], axis=1) * dsbc_s[c]
        x = r_ref[c, 0:BLK].astype(F32)
        bc_raw = r_ref[c, 2 * BLK : 3 * BLK].astype(F32)
        out_ref[c, 0:BLK] = conv_back(pre_x, edge_x, x, wx, ends, tapx_s).astype(BF16)
        out_ref[c, BLK : 2 * BLK] = conv_back(
            pre_bc, edge_bc, bc_raw, wbc, ends, tapbc_s
        ).astype(BF16)
        return pre_x[0:8], pre_bc[0:8]

    lax.fori_loop(0, blocks, backward, (edge, edge), unroll=UNROLL)

    xdx = x2_s[...]
    carry_sum = jnp.sum(es_s[...].reshape(blocks, 8, 256), axis=1)
    carry_sum = jnp.concatenate([carry_sum[:, :128], carry_sum[:, 128:]], axis=0)
    d_log = dot_exact(y2_s[...] - xdx, (ii >= jj).astype(F32))
    d_log = d_log + jnp.sum(carry_sum, axis=1, keepdims=True)
    d_raw = (xdx / step - rate * d_log) * sig
    d_raw = jnp.concatenate([d_raw[:blocks], d_raw[blocks:]], axis=1)
    raw_hi = d_raw.astype(BF16).astype(F32)
    raw_lo = d_raw - raw_hi
    tapx = jnp.concatenate([jnp.sum(tapx_s[k], axis=0, keepdims=True) for k in range(TAPS)], axis=0)
    tapbc = jnp.concatenate([jnp.sum(tapbc_s[k], axis=0, keepdims=True) for k in range(TAPS)], axis=0)
    tapx_hi = tapx.astype(BF16).astype(F32)
    rest = jnp.concatenate([tapx_hi, tapx - tapx_hi, tapbc, jnp.zeros((2, 256), F32)], axis=0)
    for c in range(blocks):
        out_ref[c, 2 * BLK : 2 * BLK + 16] = jnp.concatenate(
            [raw_hi[c : c + 1], raw_lo[c : c + 1], rest], axis=0
        ).astype(BF16)


def ssm_core(doc_lengths, place, rate, received, weight_x, weight_bc):
    blocks = received.shape[0]
    smem = pl.BlockSpec(memory_space=pltpu.SMEM)
    vmem = pl.BlockSpec(memory_space=pltpu.VMEM)

    def scratch(*shape, dtype=F32):
        return pltpu.VMEM(shape, dtype)

    return pl.pallas_call(
        ssm_kernel,
        out_shape=jax.ShapeDtypeStruct((blocks, 2 * BLK + 16, 256), BF16),
        in_specs=[smem, smem, smem, vmem, vmem, vmem],
        out_specs=vmem,
        scratch_shapes=[
            scratch(blocks, BLK, 256),
            scratch(blocks, BLK, 256, dtype=BF16),
            scratch(blocks, BLK, 256),
            scratch(blocks, BLK, 128, dtype=BF16),
            scratch(blocks, BLK, 128, dtype=BF16),
            scratch(blocks, BLK, 128, dtype=BF16),
            scratch(blocks, BLK, 128, dtype=BF16),
            scratch(blocks, BLK, 256),
            scratch(blocks, BLK, 256),
            scratch(blocks + 1, 128, 256),
            scratch(128, 256),
            scratch(blocks, 8, 128),
            scratch(blocks, 8, 256),
            scratch(2 * blocks, 128),
            scratch(2 * blocks, 128),
            scratch(8 * blocks, 256),
            scratch(TAPS, 8, 256),
            scratch(TAPS, 8, 256),
        ],
        compiler_params=pltpu.CompilerParams(vmem_limit_bytes=24 * 2**20),
        cost_estimate=pl.CostEstimate(flops=3 * 10**9, bytes_accessed=6 * 2**20, transcendentals=4 * 10**6),
        name="mixer",
    )(doc_lengths, place, rate, received, weight_x, weight_bc)


def attention_kernel(
    doc_ref, idx_ref, q_ref, do_ref, got_ref, kv0, kv1, kv2, kv3, kv4,
    dq_own, dq_sent, d0, d1, d2, d3, d4, kt_s, dk_s, dv_s, s_s, p_s,
):
    kv_refs = (kv4, kv3, kv2, kv1, kv0)
    d_refs = (d4, d3, d2, d1, d0)
    count = 2 * len(kv_refs)
    bounds = doc_bounds(doc_ref)
    scale = HD ** (-0.5)
    place = idx_ref[0]
    odd = lax.rem(place, 2)
    base = (place - odd) * BLK
    jrow = lax.broadcasted_iota(jnp.int32, (BLK, 2 * BLK), 0)
    icol = lax.broadcasted_iota(jnp.int32, (BLK, 2 * BLK), 1)
    start = start_at(base + icol[0:1], bounds) - base
    heads = got_ref.shape[1] // (2 * HD)

    def rows8(a):
        return a.reshape(BLK // 8, 8, 2 * BLK)

    def half(b):
        return slice((b % 2) * BLK, (b % 2 + 1) * BLK)

    def key_rows(b):
        return kv_refs[b // 2][half(b), 0:HD]

    def value_rows(b):
        return kv_refs[b // 2][half(b), HD : 2 * HD]

    def in_order(own, other):
        first = jnp.where(odd == 0, own, other)
        second = jnp.where(odd == 0, other, own)
        return jnp.concatenate([first, second], axis=0)

    for b in range(count):
        kt_s[b] = key_rows(b).T
    dk_s[...] = jnp.zeros(dk_s.shape, F32)
    dv_s[...] = jnp.zeros(dv_s.shape, F32)

    def turn(head, carry):
        at = pl.multiple_of(head * HD, HD)
        own_at = pl.multiple_of((odd * heads + head) * HD, HD)
        q = in_order(q_ref[:, pl.ds(own_at, HD)], got_ref[:, pl.ds(at, HD)])
        do = in_order(
            do_ref[:, pl.ds(own_at, HD)], got_ref[:, pl.ds(pl.multiple_of(heads * HD + at, HD), HD)]
        )
        top = jnp.full((8, 2 * BLK), NEG_BIG, F32)
        for b in range(count):
            allowed = jrow >= start + (BACK - b) * BLK
            if b >= BACK:
                allowed = allowed & (jrow + (b - BACK) * BLK <= icol)
            s = jnp.where(allowed, dot_nt(key_rows(b), q), NEG_BIG)
            s_s[b] = s
            top = jnp.maximum(top, jnp.max(rows8(s), axis=0))
            p_s[b] = dot_nt(value_rows(b), do)
        top = jnp.max(top, axis=0, keepdims=True) * (scale * LOG2E)
        norm = jnp.zeros((8, 2 * BLK), F32)
        mean = jnp.zeros((8, 2 * BLK), F32)
        for b in range(count):
            e = jnp.exp2(s_s[b] * (scale * LOG2E) - top)
            s_s[b] = e
            norm = norm + jnp.sum(rows8(e), axis=0)
            mean = mean + jnp.sum(rows8(e * p_s[b]), axis=0)
        inverse = 1.0 / jnp.sum(norm, axis=0, keepdims=True)
        mean = jnp.sum(mean, axis=0, keepdims=True) * inverse
        dqt = jnp.zeros((HD, 2 * BLK), F32)
        for b in range(count):
            prob = s_s[b] * inverse
            grad = (prob * (p_s[b] - mean)).astype(BF16)
            dv_s[b] += dot_nn(prob.astype(BF16), do)
            dk_s[b] += dot_nn(grad, q)
            dqt = dqt + dot_nn(kt_s[b], grad)
        dqt = dqt * scale
        first = dqt[:, :BLK].T
        second = dqt[:, BLK:].T
        dq_own[:, pl.ds(at, HD)] = jnp.where(odd == 0, first, second).astype(BF16)
        dq_sent[:, pl.ds(at, HD)] = jnp.where(odd == 0, second, first).astype(BF16)
        return carry

    lax.fori_loop(0, heads, turn, 0)
    for b in range(count):
        out = d_refs[b // 2]
        out[half(b), 0:HD] = (dk_s[b] * scale).astype(out.dtype)
        out[half(b), HD : 2 * HD] = dv_s[b].astype(out.dtype)


def attention_core(doc_lengths, place, query, d_out, got, kv_pairs):
    smem = pl.BlockSpec(memory_space=pltpu.SMEM)
    vmem = pl.BlockSpec(memory_space=pltpu.VMEM)
    pairs = len(kv_pairs)
    count = 2 * pairs
    rows, width = query.shape
    part = jax.ShapeDtypeStruct((rows, width // 2), BF16)
    kv_shape = kv_pairs[0].shape
    outs = [part, part, jax.ShapeDtypeStruct(kv_shape, F32)]
    outs += [jax.ShapeDtypeStruct(kv_shape, BF16)] * (pairs - 1)
    return pl.pallas_call(
        attention_kernel,
        out_shape=outs,
        in_specs=[smem, smem] + [vmem] * (3 + pairs),
        out_specs=[vmem] * (2 + pairs),
        scratch_shapes=[
            pltpu.VMEM((count, HD, BLK), BF16),
            pltpu.VMEM((count, BLK, HD), F32),
            pltpu.VMEM((count, BLK, HD), F32),
            pltpu.VMEM((count, BLK, 2 * BLK), F32),
            pltpu.VMEM((count, BLK, 2 * BLK), F32),
        ],
        compiler_params=pltpu.CompilerParams(vmem_limit_bytes=16 * 2**20),
        cost_estimate=pl.CostEstimate(flops=4 * 10**9, bytes_accessed=4 * 2**20, transcendentals=3 * 10**6),
        name="attention",
    )(doc_lengths, place, query, d_out, got, *kv_pairs)


def shift(a, by):
    devices = lax.axis_size("ctx")
    return lax.ppermute(
        a, "ctx", [(i, i + by) for i in range(devices) if 0 <= i + by < devices]
    )


def partner(a):
    return lax.ppermute(a, "ctx", [(i, i ^ 1) for i in range(lax.axis_size("ctx"))])


def pack_kernel(x_ref, g_ref, bc_ref, dt_ref, out_ref, buf, in_sems, out_sems):
    blocks = out_ref.shape[0]
    loads = []
    for d in range(blocks):
        lanes = pl.ds(d * 2 * HD, 2 * HD)
        pair = [
            pltpu.make_async_copy(src, buf.at[d, pl.ds(at * BLK, BLK)], in_sems.at[2 * d + at])
            for at, src in enumerate((x_ref.at[:, lanes], g_ref.at[:, lanes]))
        ]
        for one in pair:
            one.start()
        loads.append(pair)
    for d in range(blocks):
        buf[d, 2 * BLK : 3 * BLK] = bc_ref[d // (blocks // 2)]
        raw = jnp.concatenate([dt_ref[2 * d : 2 * d + 1], dt_ref[2 * d + 1 : 2 * d + 2]], axis=1)
        hi = raw.astype(BF16).astype(F32)
        mid = (raw - hi).astype(BF16).astype(F32)
        parts = [hi, mid, raw - hi - mid, jnp.zeros((13, 2 * BLK), F32)]
        buf[d, 3 * BLK : 3 * BLK + 16] = jnp.concatenate(parts, axis=0).astype(BF16)
    stores = []
    for d in range(blocks):
        for one in loads[d]:
            one.wait()
        stores.append(pltpu.make_async_copy(buf.at[d], out_ref.at[d], out_sems.at[d]))
        stores[-1].start()
    for one in stores:
        one.wait()


def pack(x_in, grad, bc_sent, dt_raw, blocks):
    hbm = pl.BlockSpec(memory_space=pltpu.HBM)
    vmem = pl.BlockSpec(memory_space=pltpu.VMEM)
    return pl.pallas_call(
        pack_kernel,
        out_shape=jax.ShapeDtypeStruct((blocks, 3 * BLK + 16, 2 * HD), BF16),
        in_specs=[hbm, hbm, vmem, vmem],
        out_specs=hbm,
        scratch_shapes=[
            pltpu.VMEM((blocks, 3 * BLK + 16, 2 * HD), BF16),
            pltpu.SemaphoreType.DMA((2 * blocks,)),
            pltpu.SemaphoreType.DMA((blocks,)),
        ],
        cost_estimate=pl.CostEstimate(flops=0, bytes_accessed=7 * 2**20, transcendentals=0),
        name="pack",
    )(x_in, grad, bc_sent, dt_raw)


def unpack_kernel(part, dx_ref, dbc_ref, dt_ref, wx_ref, wbc_ref, sems):
    blocks = part.shape[0]
    half = blocks // 2
    copies = []
    for d in range(blocks):
        lanes = pl.ds(d * 2 * HD, 2 * HD)
        copies.append(pltpu.make_async_copy(part.at[d, pl.ds(0, BLK)], dx_ref.at[:, lanes], sems.at[d]))
        copies[-1].start()
    for group in range(2):
        at = [group * half + d for d in range(half)]
        total = part[at[0], BLK : 2 * BLK].astype(F32)
        taps = part[at[0], 2 * BLK : 2 * BLK + 16].astype(F32)
        for d in at[1:]:
            total = total + part[d, BLK : 2 * BLK].astype(F32)
            taps = taps + part[d, 2 * BLK : 2 * BLK + 16].astype(F32)
        for which in range(2):
            lanes = slice(which * HD, (which + 1) * HD)
            out = slice((2 * which + group) * HD, (2 * which + group + 1) * HD)
            dbc_ref[:, out] = total[:, lanes].astype(BF16)
            wbc_ref[:, which, group * HD : (group + 1) * HD] = taps[10:14, lanes]
    for d in range(blocks):
        small = part[d, 2 * BLK : 2 * BLK + 16].astype(F32)
        raw = small[0:1] + small[1:2]
        dt_ref[2 * d : 2 * d + 1] = raw[:, :BLK]
        dt_ref[2 * d + 1 : 2 * d + 2] = raw[:, BLK:]
        wx_ref[:, d * 2 * HD : (d + 1) * 2 * HD] = small[2:6] + small[6:10]
    for done in copies:
        done.wait()


def unpack(received):
    blocks = received.shape[0]
    hbm = pl.BlockSpec(memory_space=pltpu.HBM)
    vmem = pl.BlockSpec(memory_space=pltpu.VMEM)
    return pl.pallas_call(
        unpack_kernel,
        out_shape=[
            jax.ShapeDtypeStruct((BLK, blocks * 2 * HD), BF16),
            jax.ShapeDtypeStruct((BLK, 4 * HD), BF16),
            jax.ShapeDtypeStruct((2 * blocks, BLK), F32),
            jax.ShapeDtypeStruct((TAPS, blocks * 2 * HD), F32),
            jax.ShapeDtypeStruct((TAPS, 2, 2 * HD), F32),
        ],
        in_specs=[vmem],
        out_specs=[hbm, vmem, vmem, vmem, vmem],
        scratch_shapes=[pltpu.SemaphoreType.DMA((blocks,))],
        compiler_params=pltpu.CompilerParams(vmem_limit_bytes=8 * 2**20),
        cost_estimate=pl.CostEstimate(flops=10**6, bytes_accessed=4 * 2**20, transcendentals=0),
        name="unpack",
    )(received)


def gate_kernel(*refs):
    pass


def gate(value, *others):
    hbm = pl.BlockSpec(memory_space=pltpu.HBM)
    anywhere = pl.BlockSpec(memory_space=pl.ANY)
    return pl.pallas_call(
        gate_kernel,
        out_shape=jax.ShapeDtypeStruct(value.shape, value.dtype),
        in_specs=[hbm] + [anywhere] * len(others),
        out_specs=hbm,
        input_output_aliases={0: 0},
        name="gate",
    )(value, *others)


def kv_sum_kernel(idx_ref, own, r1, r2, r3, r4, after, mine, sent):
    total = own[...]
    for got in (r1, r2, r3, r4):
        total = total + got[...].astype(F32)
    rows = mine.shape[0]
    first = total[:rows].astype(BF16)
    second = total[rows:].astype(BF16)
    odd = lax.rem(idx_ref[0], 2)
    mine[...] = jnp.where(odd == 0, first, second)
    sent[...] = jnp.where(odd == 0, second, first)


def kv_total(place, own, received, after):
    vmem = pl.BlockSpec(memory_space=pltpu.VMEM)
    half = jax.ShapeDtypeStruct((own.shape[0] // 2, own.shape[1]), BF16)
    return pl.pallas_call(
        kv_sum_kernel,
        out_shape=[half, half],
        in_specs=[pl.BlockSpec(memory_space=pltpu.SMEM)]
        + [vmem] * (1 + len(received))
        + [pl.BlockSpec(memory_space=pl.ANY)],
        out_specs=[vmem, vmem],
        name="kv_total",
    )(place, own, *received, after)


def kv_place_kernel(idx_ref, mine, other, dk_ref, dv_ref):
    odd = lax.rem(idx_ref[0], 2)
    a = mine[...]
    b = other[...]
    first = jnp.where(odd == 0, a, b)
    second = jnp.where(odd == 0, b, a)
    dk_ref[...] = jnp.concatenate([first[:, :HD], second[:, :HD]], axis=1)
    dv_ref[...] = jnp.concatenate([first[:, HD:], second[:, HD:]], axis=1)


def kv_place(place, mine, other):
    vmem = pl.BlockSpec(memory_space=pltpu.VMEM)
    return pl.pallas_call(
        kv_place_kernel,
        out_shape=[jax.ShapeDtypeStruct(mine.shape, BF16)] * 2,
        in_specs=[pl.BlockSpec(memory_space=pltpu.SMEM), vmem, vmem],
        out_specs=[vmem, vmem],
        name="kv_place",
    )(place, mine, other)


def swap(a):
    return lax.all_to_all(a, "ctx", 0, 0, tiled=True)


def shards(
    x_in, bc_in, conv_x, conv_bc, dt_raw, rate, grad_ssd, query, key, value, d_out, doc_lengths
):
    ctx = lax.axis_size("ctx")
    rows = x_in.shape[0]
    place = lax.axis_index("ctx").astype(jnp.int32).reshape(1)

    odd = place[0] % 2

    def half(a, which):
        return lax.dynamic_slice_in_dim(a, which * (a.shape[1] // 2), a.shape[1] // 2, 1)

    def pick(own, other):
        return jnp.where(odd == 0, own, other), jnp.where(odd == 0, other, own)

    bc_sent = bc_in.reshape(rows, 2, 2, HD).transpose(2, 0, 1, 3).reshape(2, rows, 2 * HD)
    packed = pack(x_in, grad_ssd, bc_sent, dt_raw, ctx)
    kv_own = jnp.concatenate([half(key, odd), half(value, odd)], axis=1)
    kv_got = partner(jnp.concatenate([half(key, 1 - odd), half(value, 1 - odd)], axis=1))
    kv_pair = gate(jnp.concatenate(pick(kv_own, kv_got), axis=0), packed)
    got_qo = partner(jnp.concatenate([half(query, 1 - odd), half(d_out, 1 - odd)], axis=1))
    kv_pairs = [kv_pair] + [shift(kv_pair, 2 * by) for by in range(1, BACK // 2 + 1)]
    got = swap(gate(packed, got_qo, *kv_pairs[1:]))
    dq_own, dq_sent, *d_kv = attention_core(doc_lengths, place, query, d_out, got_qo, kv_pairs)
    place_after, *d_kv = lax.optimization_barrier((place, *d_kv))
    mixed = ssm_core(
        doc_lengths, place_after, rate, got, conv_x, conv_bc.reshape(TAPS, 4 * HD)
    )
    dq_got = partner(dq_sent)
    received = [shift(d_kv[by], -2 * by) for by in range(1, BACK // 2 + 1)]
    back = swap(gate(mixed, dq_got, *received))
    mine, sent = kv_total(place, d_kv[0], received, mixed)
    d_key, d_value = kv_place(place, mine, partner(sent))
    d_query = jnp.concatenate(pick(dq_own, dq_got), axis=1)
    d_x, d_bc, d_dt, d_wx, d_wbc = unpack(back)
    return (
        d_x,
        d_bc.reshape(rows, 2, 2 * HD),
        d_dt,
        d_wx,
        d_wbc,
        d_query,
        d_key,
        d_value,
    )


def solution(mesh):
    tokens = P(("dp", "ctx"), "head")
    in_specs = (
        tokens,
        P(("dp", "ctx"), None, "head"),
        P(None, "head"),
        P(None, None, "head"),
        P("head", ("dp", "ctx")),
        P("head"),
        tokens,
        tokens,
        tokens,
        tokens,
        tokens,
        P("dp"),
    )
    out_specs = (
        tokens,
        P(("dp", "ctx"), None, "head"),
        P("head", ("dp", "ctx")),
        P("dp", "head"),
        P("dp", None, "head"),
        tokens,
        tokens,
        tokens,
    )
    return jax.shard_map(shards, mesh=mesh, in_specs=in_specs, out_specs=out_specs, check_vma=False)
```

```python
import jax
import jax.numpy as jnp
from jax import lax
from jax.experimental import pallas as pl
from jax.experimental.pallas import tpu as pltpu
from jax.sharding import PartitionSpec as P

F32 = jnp.float32
BF16 = jnp.bfloat16
HD = 128
BLK = 128
TAPS = 4
BACK = 8
LOG2E = 1.4426950408889634
NEG_BIG = -1e30
UNROLL = 4


def dot_nn(a, b):
    return lax.dot_general(a, b, (((1,), (0,)), ((), ())), preferred_element_type=F32)


def dot_nt(a, b):
    return lax.dot_general(a, b, (((1,), (1,)), ((), ())), preferred_element_type=F32)


def dot_tn(a, b):
    return lax.dot_general(a, b, (((0,), (0,)), ((), ())), preferred_element_type=F32)


def doc_bounds(doc_ref):
    s1 = doc_ref[0]
    s2 = s1 + doc_ref[1]
    s3 = s2 + doc_ref[2]
    return s1, s2, s3


def start_at(pos, bounds):
    s1, s2, s3 = bounds
    return jnp.where(pos >= s3, s3, jnp.where(pos >= s2, s2, jnp.where(pos >= s1, s1, 0)))


def next_start(pos, bounds, total):
    s1, s2, s3 = bounds
    return jnp.where(pos < s1, s1, jnp.where(pos < s2, s2, jnp.where(pos < s3, s3, total)))


def twice(a):
    return jnp.concatenate([a, a], axis=1)


def fold_rows(a):
    return jnp.sum(a.reshape(a.shape[0] // 8, 8, a.shape[1]), axis=0)


def split3(a):
    hi = a.astype(BF16)
    rest = a - hi.astype(F32)
    mid = rest.astype(BF16)
    return hi, mid, (rest - mid.astype(F32)).astype(BF16)


def dot_exact(a, ones):
    rows = a.shape[0]
    out = dot_nn(jnp.concatenate(split3(a), axis=0), ones.astype(BF16))
    return out[:rows] + out[rows : 2 * rows] + out[2 * rows :]


def ssm_kernel(
    doc_ref, idx_ref, rate_ref, r_ref, wx_ref, wbc_ref, out_ref,
    xs_s, xp_s, u_s, b_s, c_s, bm_s, cm_s, dsx_s, dsbc_s, st_s, ds_s,
    cols_s, elt_s, x2_s, y2_s, es_s, tapx_s, tapbc_s,
):
    blocks = r_ref.shape[0]
    total = blocks * BLK
    place = idx_ref[0]
    bounds = doc_bounds(doc_ref)
    rate0 = rate_ref[2 * place]
    rate1 = rate_ref[2 * place + 1]
    group = place // (blocks // 2)
    wx = wx_ref[:, pl.ds(pl.multiple_of(place * 256, 256), 256)]
    wbc = jnp.concatenate(
        [
            wbc_ref[:, pl.ds(pl.multiple_of(group * 128, 128), 128)],
            wbc_ref[:, pl.ds(pl.multiple_of(256 + group * 128, 128), 128)],
        ],
        axis=1,
    )

    for c in range(blocks):
        row = jnp.sum(r_ref[c, 3 * BLK : 3 * BLK + 16, :].astype(F32), axis=0, keepdims=True)
        x2_s[c : c + 1] = row[:, :128]
        x2_s[blocks + c : blocks + c + 1] = row[:, 128:]
    raw = x2_s[...]
    step = jnp.log(1.0 + jnp.exp(raw))
    sig = 1.0 / (1.0 + jnp.exp(-raw))
    row_ids = lax.broadcasted_iota(jnp.int32, (2 * blocks, 128), 0)
    rate = jnp.where(row_ids < blocks, rate0, rate1)
    ii = lax.broadcasted_iota(jnp.int32, (128, 128), 0)
    jj = lax.broadcasted_iota(jnp.int32, (128, 128), 1)
    cum = dot_exact(-step * rate, (ii <= jj).astype(F32))
    v_rows = jnp.exp(cum)
    u_hi, u_lo, _ = split3(step * jnp.exp(-cum))
    v_hi, v_lo, _ = split3(v_rows)
    last = jnp.broadcast_to(v_rows[:, 127:128], (2 * blocks, 128))
    pieces = [a.astype(F32) for a in (u_hi, u_lo, v_hi, v_lo)]
    for c in range(blocks):
        rows = [a[at : at + 1] for a in pieces for at in (c, blocks + c)]
        cols_s[c] = jnp.concatenate(rows, axis=0)
        elt_s[c] = jnp.broadcast_to(
            jnp.concatenate([last[c : c + 1], last[blocks + c : blocks + c + 1]], axis=1), (8, 256)
        )
    row8 = lax.broadcasted_iota(jnp.int32, (8, 512), 0)
    lane8 = lax.broadcasted_iota(jnp.int32, (8, 512), 1) // 128
    spread = ((lane8 // 2 == row8 // 4) & (lane8 % 2 == row8 % 2)).astype(BF16)

    edge = jnp.zeros((8, 256), F32)
    st_s[0] = jnp.zeros((128, 256), F32)

    def conv(edge, value, weight, keeps):
        win = jnp.concatenate([edge, value], axis=0)
        pre = value * weight[TAPS - 1 : TAPS]
        for d in range(1, TAPS):
            pre = pre + jnp.where(keeps[d - 1], win[8 - d : 8 - d + BLK], 0.0) * weight[TAPS - 1 - d : TAPS - d]
        sg = 0.5 * jnp.tanh(0.5 * pre) + 0.5
        val = pre * sg
        return val, sg + val * (1.0 - sg)

    def forward(c, carry):
        base = pl.multiple_of(c * BLK, BLK)
        edge_x, edge_bc = carry
        x = r_ref[c, 0:BLK].astype(F32)
        bc_raw = r_ref[c, 2 * BLK : 3 * BLK].astype(F32)
        pos = base + ii
        start = start_at(pos, bounds)
        last_start = start_at(base + BLK - 1, bounds)
        tails = pos >= last_start
        dist = pos - start
        keeps = [twice(dist >= d) for d in range(1, TAPS)]
        xs, dsx = conv(edge_x, x, wx, keeps)
        bc, dsbc = conv(edge_bc, bc_raw, wbc, keeps)
        xs_s[c] = xs
        dsx_s[c] = dsx
        dsbc_s[c] = dsbc
        b = bc[:, :128]
        cc = bc[:, 128:]
        b_s[c] = b.astype(BF16)
        c_s[c] = cc.astype(BF16)
        bm = jnp.where(tails, b, 0.0).astype(BF16)
        bm_s[c] = bm
        cm_s[c] = jnp.where(start < base, cc, 0.0).astype(BF16)
        u = dot_tn(cols_s[c].astype(BF16), spread[:, :256])
        u_s[c] = u
        xp = (xs * u).astype(BF16)
        xp_s[c] = xp
        elt = elt_s[c][0:1]
        keep = jnp.where(last_start < base, elt, 0.0)
        st_s[c + 1] = keep * st_s[c] + elt * dot_tn(bm, xp)
        return x[BLK - 8 :], bc_raw[BLK - 8 :]

    lax.fori_loop(0, blocks, forward, (edge, edge), unroll=UNROLL)

    ds_s[...] = jnp.zeros((128, 256), F32)
    tapx_s[...] = jnp.zeros((TAPS, 8, 256), F32)
    tapbc_s[...] = jnp.zeros((TAPS, 8, 256), F32)
    lane2 = lax.broadcasted_iota(jnp.int32, (16, 256), 1)
    row2 = lax.broadcasted_iota(jnp.int32, (16, 256), 0)
    pick = (lane2 // 128 == row2).astype(BF16)

    def head_sums(out, c, a):
        sums = dot_nt(pick, a.astype(BF16))
        out[pl.ds(c, 1)] = sums[0:1]
        out[pl.ds(blocks + c, 1)] = sums[1:2]

    def conv_back(grad, edge, raw_in, weight, ends, taps):
        win = jnp.concatenate([grad, edge], axis=0)
        total_grad = grad * weight[TAPS - 1 : TAPS]
        taps[TAPS - 1] += fold_rows(grad * raw_in)
        for d in range(1, TAPS):
            moved = jnp.where(ends[d - 1], win[d : d + BLK], 0.0)
            total_grad = total_grad + moved * weight[TAPS - 1 - d : TAPS - d]
            taps[TAPS - 1 - d] += fold_rows(moved * raw_in)
        return total_grad

    def backward(lap, carry):
        c = blocks - 1 - lap
        base = pl.multiple_of(c * BLK, BLK)
        pos = base + ii
        start = start_at(pos, bounds)
        last_start = start_at(base + BLK - 1, bounds)
        causal = (jj <= ii) & (base + jj >= start)
        leads = start < base
        tails = pos >= last_start
        b = b_s[c]
        cc = c_s[c]
        xp = xp_s[c]
        cm = cm_s[c]
        gv = r_ref[c, BLK : 2 * BLK].astype(F32) * dot_tn(cols_s[c].astype(BF16), spread[:, 256:])
        gp = gv.astype(BF16)
        elt = elt_s[c][0:1]
        ds = ds_s[...]
        es_s[pl.ds(pl.multiple_of(c * 8, 8), 8)] = fold_rows(ds * st_s[c + 1])
        sb = st_s[c].astype(BF16)
        ds_e = elt * ds
        dsb = ds_e.astype(BF16)
        ds_s[...] = jnp.where(last_start < base, ds_e, 0.0) + dot_tn(cm, gp)
        w = jnp.where(causal, dot_nt(cc, b), 0.0).astype(BF16)
        yv = dot_nn(w, xp) + dot_nn(cm, sb)
        dxp = dot_tn(w, gp) + dot_nn(bm_s[c], dsb)
        z = jnp.where(causal, dot_nt(gp, xp), 0.0).astype(BF16)
        dc = dot_nn(z, b) + jnp.where(leads, dot_nt(gp, sb), 0.0)
        db = dot_tn(z, cc) + jnp.where(tails, dot_nt(xp, dsb), 0.0)
        dx = u_s[c] * dxp
        head_sums(x2_s, c, xs_s[c] * dx)
        head_sums(y2_s, c, gv * yv)
        left = next_start(pos, bounds, total) - pos
        ends = [twice(left > d) for d in range(1, TAPS)]
        edge_x, edge_bc = carry
        pre_x = dx * dsx_s[c]
        pre_bc = jnp.concatenate([db, dc], axis=1) * dsbc_s[c]
        x = r_ref[c, 0:BLK].astype(F32)
        bc_raw = r_ref[c, 2 * BLK : 3 * BLK].astype(F32)
        out_ref[c, 0:BLK] = conv_back(pre_x, edge_x, x, wx, ends, tapx_s).astype(BF16)
        out_ref[c, BLK : 2 * BLK] = conv_back(
            pre_bc, edge_bc, bc_raw, wbc, ends, tapbc_s
        ).astype(BF16)
        return pre_x[0:8], pre_bc[0:8]

    lax.fori_loop(0, blocks, backward, (edge, edge), unroll=UNROLL)

    xdx = x2_s[...]
    carry_sum = jnp.sum(es_s[...].reshape(blocks, 8, 256), axis=1)
    carry_sum = jnp.concatenate([carry_sum[:, :128], carry_sum[:, 128:]], axis=0)
    d_log = dot_exact(y2_s[...] - xdx, (ii >= jj).astype(F32))
    d_log = d_log + jnp.sum(carry_sum, axis=1, keepdims=True)
    d_raw = (xdx / step - rate * d_log) * sig
    d_raw = jnp.concatenate([d_raw[:blocks], d_raw[blocks:]], axis=1)
    raw_hi = d_raw.astype(BF16).astype(F32)
    raw_lo = d_raw - raw_hi
    tapx = jnp.concatenate([jnp.sum(tapx_s[k], axis=0, keepdims=True) for k in range(TAPS)], axis=0)
    tapbc = jnp.concatenate([jnp.sum(tapbc_s[k], axis=0, keepdims=True) for k in range(TAPS)], axis=0)
    tapx_hi = tapx.astype(BF16).astype(F32)
    rest = jnp.concatenate([tapx_hi, tapx - tapx_hi, tapbc, jnp.zeros((2, 256), F32)], axis=0)
    for c in range(blocks):
        out_ref[c, 2 * BLK : 2 * BLK + 16] = jnp.concatenate(
            [raw_hi[c : c + 1], raw_lo[c : c + 1], rest], axis=0
        ).astype(BF16)


def ssm_core(doc_lengths, place, rate, received, weight_x, weight_bc):
    blocks = received.shape[0]
    smem = pl.BlockSpec(memory_space=pltpu.SMEM)
    vmem = pl.BlockSpec(memory_space=pltpu.VMEM)

    def scratch(*shape, dtype=F32):
        return pltpu.VMEM(shape, dtype)

    return pl.pallas_call(
        ssm_kernel,
        out_shape=jax.ShapeDtypeStruct((blocks, 2 * BLK + 16, 256), BF16),
        in_specs=[smem, smem, smem, vmem, vmem, vmem],
        out_specs=vmem,
        scratch_shapes=[
            scratch(blocks, BLK, 256),
            scratch(blocks, BLK, 256, dtype=BF16),
            scratch(blocks, BLK, 256),
            scratch(blocks, BLK, 128, dtype=BF16),
            scratch(blocks, BLK, 128, dtype=BF16),
            scratch(blocks, BLK, 128, dtype=BF16),
            scratch(blocks, BLK, 128, dtype=BF16),
            scratch(blocks, BLK, 256),
            scratch(blocks, BLK, 256),
            scratch(blocks + 1, 128, 256),
            scratch(128, 256),
            scratch(blocks, 8, 128),
            scratch(blocks, 8, 256),
            scratch(2 * blocks, 128),
            scratch(2 * blocks, 128),
            scratch(8 * blocks, 256),
            scratch(TAPS, 8, 256),
            scratch(TAPS, 8, 256),
        ],
        compiler_params=pltpu.CompilerParams(vmem_limit_bytes=24 * 2**20),
        cost_estimate=pl.CostEstimate(flops=3 * 10**9, bytes_accessed=6 * 2**20, transcendentals=4 * 10**6),
        name="mixer",
    )(doc_lengths, place, rate, received, weight_x, weight_bc)


def attention_kernel(
    doc_ref, idx_ref, q_ref, do_ref, got_ref, kv_ref,
    dq_own, dq_sent, d0, d1, d2, d3, d4, kt_s, dk_s, dv_s, s_s, p_s,
):
    d_refs = (d4, d3, d2, d1, d0)
    count = 2 * len(d_refs)
    bounds = doc_bounds(doc_ref)
    scale = HD ** (-0.5)
    place = idx_ref[0]
    odd = lax.rem(place, 2)
    base = (place - odd) * BLK
    jrow = lax.broadcasted_iota(jnp.int32, (BLK, 2 * BLK), 0)
    icol = lax.broadcasted_iota(jnp.int32, (BLK, 2 * BLK), 1)
    start = start_at(base + icol[0:1], bounds) - base
    heads = got_ref.shape[1] // (2 * HD)

    def rows8(a):
        return a.reshape(BLK // 8, 8, 2 * BLK)

    def half(b):
        return slice((b % 2) * BLK, (b % 2 + 1) * BLK)

    def key_rows(b):
        return kv_ref[jnp.maximum(place - odd - BACK + b, 0), :, 0:HD]

    def value_rows(b):
        return kv_ref[jnp.maximum(place - odd - BACK + b, 0), :, HD : 2 * HD]

    def in_order(own, other):
        first = jnp.where(odd == 0, own, other)
        second = jnp.where(odd == 0, other, own)
        return jnp.concatenate([first, second], axis=0)

    for b in range(count):
        kt_s[b] = key_rows(b).T
    dk_s[...] = jnp.zeros(dk_s.shape, F32)
    dv_s[...] = jnp.zeros(dv_s.shape, F32)

    def turn(head, carry):
        at = pl.multiple_of(head * HD, HD)
        own_at = pl.multiple_of((odd * heads + head) * HD, HD)
        q = in_order(q_ref[:, pl.ds(own_at, HD)], got_ref[:, pl.ds(at, HD)])
        do = in_order(
            do_ref[:, pl.ds(own_at, HD)], got_ref[:, pl.ds(pl.multiple_of(heads * HD + at, HD), HD)]
        )
        top = jnp.full((8, 2 * BLK), NEG_BIG, F32)
        for b in range(count):
            allowed = jrow >= start + (BACK - b) * BLK
            if b >= BACK:
                allowed = allowed & (jrow + (b - BACK) * BLK <= icol)
            s = jnp.where(allowed, dot_nt(key_rows(b), q), NEG_BIG)
            s_s[b] = s
            top = jnp.maximum(top, jnp.max(rows8(s), axis=0))
            p_s[b] = dot_nt(value_rows(b), do)
        top = jnp.max(top, axis=0, keepdims=True) * (scale * LOG2E)
        norm = jnp.zeros((8, 2 * BLK), F32)
        mean = jnp.zeros((8, 2 * BLK), F32)
        for b in range(count):
            e = jnp.exp2(s_s[b] * (scale * LOG2E) - top)
            s_s[b] = e
            norm = norm + jnp.sum(rows8(e), axis=0)
            mean = mean + jnp.sum(rows8(e * p_s[b]), axis=0)
        inverse = 1.0 / jnp.sum(norm, axis=0, keepdims=True)
        mean = jnp.sum(mean, axis=0, keepdims=True) * inverse
        dqt = jnp.zeros((HD, 2 * BLK), F32)
        for b in range(count):
            prob = s_s[b] * inverse
            grad = (prob * (p_s[b] - mean)).astype(BF16)
            dv_s[b] += dot_nn(prob.astype(BF16), do)
            dk_s[b] += dot_nn(grad, q)
            dqt = dqt + dot_nn(kt_s[b], grad)
        dqt = dqt * scale
        first = dqt[:, :BLK].T
        second = dqt[:, BLK:].T
        dq_own[:, pl.ds(at, HD)] = jnp.where(odd == 0, first, second).astype(BF16)
        dq_sent[:, pl.ds(at, HD)] = jnp.where(odd == 0, second, first).astype(BF16)
        return carry

    lax.fori_loop(0, heads, turn, 0)
    for b in range(count):
        out = d_refs[b // 2]
        out[half(b), 0:HD] = (dk_s[b] * scale).astype(out.dtype)
        out[half(b), HD : 2 * HD] = dv_s[b].astype(out.dtype)


def attention_core(doc_lengths, place, query, d_out, got, kv):
    smem = pl.BlockSpec(memory_space=pltpu.SMEM)
    vmem = pl.BlockSpec(memory_space=pltpu.VMEM)
    pairs = BACK // 2 + 1
    count = 2 * pairs
    rows, width = query.shape
    part = jax.ShapeDtypeStruct((rows, width // 2), BF16)
    kv_shape = (2 * rows, 2 * HD)
    outs = [part, part, jax.ShapeDtypeStruct(kv_shape, F32)]
    outs += [jax.ShapeDtypeStruct(kv_shape, BF16)] * (pairs - 1)
    return pl.pallas_call(
        attention_kernel,
        out_shape=outs,
        in_specs=[smem, smem] + [vmem] * 4,
        out_specs=[vmem] * (2 + pairs),
        scratch_shapes=[
            pltpu.VMEM((count, HD, BLK), BF16),
            pltpu.VMEM((count, BLK, HD), F32),
            pltpu.VMEM((count, BLK, HD), F32),
            pltpu.VMEM((count, BLK, 2 * BLK), F32),
            pltpu.VMEM((count, BLK, 2 * BLK), F32),
        ],
        compiler_params=pltpu.CompilerParams(vmem_limit_bytes=16 * 2**20),
        cost_estimate=pl.CostEstimate(flops=4 * 10**9, bytes_accessed=4 * 2**20, transcendentals=3 * 10**6),
        name="attention",
    )(doc_lengths, place, query, d_out, got, kv)


def shift(a, by):
    devices = lax.axis_size("ctx")
    return lax.ppermute(
        a, "ctx", [(i, i + by) for i in range(devices) if 0 <= i + by < devices]
    )


def partner(a):
    return lax.ppermute(a, "ctx", [(i, i ^ 1) for i in range(lax.axis_size("ctx"))])


def pack_kernel(x_ref, g_ref, bc_ref, dt_ref, out_ref, buf, in_sems, out_sems):
    blocks = out_ref.shape[0]
    loads = []
    for d in range(blocks):
        lanes = pl.ds(d * 2 * HD, 2 * HD)
        pair = [
            pltpu.make_async_copy(src, buf.at[d, pl.ds(at * BLK, BLK)], in_sems.at[2 * d + at])
            for at, src in enumerate((x_ref.at[:, lanes], g_ref.at[:, lanes]))
        ]
        for one in pair:
            one.start()
        loads.append(pair)
    for d in range(blocks):
        buf[d, 2 * BLK : 3 * BLK] = bc_ref[d // (blocks // 2)]
        raw = jnp.concatenate([dt_ref[2 * d : 2 * d + 1], dt_ref[2 * d + 1 : 2 * d + 2]], axis=1)
        hi = raw.astype(BF16).astype(F32)
        mid = (raw - hi).astype(BF16).astype(F32)
        parts = [hi, mid, raw - hi - mid, jnp.zeros((13, 2 * BLK), F32)]
        buf[d, 3 * BLK : 3 * BLK + 16] = jnp.concatenate(parts, axis=0).astype(BF16)
    stores = []
    for d in range(blocks):
        for one in loads[d]:
            one.wait()
        stores.append(pltpu.make_async_copy(buf.at[d], out_ref.at[d], out_sems.at[d]))
        stores[-1].start()
    for one in stores:
        one.wait()


def pack(x_in, grad, bc_sent, dt_raw, blocks):
    hbm = pl.BlockSpec(memory_space=pltpu.HBM)
    vmem = pl.BlockSpec(memory_space=pltpu.VMEM)
    return pl.pallas_call(
        pack_kernel,
        out_shape=jax.ShapeDtypeStruct((blocks, 3 * BLK + 16, 2 * HD), BF16),
        in_specs=[hbm, hbm, vmem, vmem],
        out_specs=hbm,
        scratch_shapes=[
            pltpu.VMEM((blocks, 3 * BLK + 16, 2 * HD), BF16),
            pltpu.SemaphoreType.DMA((2 * blocks,)),
            pltpu.SemaphoreType.DMA((blocks,)),
        ],
        cost_estimate=pl.CostEstimate(flops=0, bytes_accessed=7 * 2**20, transcendentals=0),
        name="pack",
    )(x_in, grad, bc_sent, dt_raw)


def unpack_kernel(
    idx_ref, part, dq_own, dq_got, own, dx_ref, dbc_ref, dt_ref, wx_ref, wbc_ref, dq_ref, passed, sems
):
    blocks = part.shape[0]
    half = blocks // 2
    copies = []
    for d in range(blocks):
        lanes = pl.ds(d * 2 * HD, 2 * HD)
        copies.append(pltpu.make_async_copy(part.at[d, pl.ds(0, BLK)], dx_ref.at[:, lanes], sems.at[d]))
        copies[-1].start()
    for group in range(2):
        at = [group * half + d for d in range(half)]
        total = part[at[0], BLK : 2 * BLK].astype(F32)
        taps = part[at[0], 2 * BLK : 2 * BLK + 16].astype(F32)
        for d in at[1:]:
            total = total + part[d, BLK : 2 * BLK].astype(F32)
            taps = taps + part[d, 2 * BLK : 2 * BLK + 16].astype(F32)
        for which in range(2):
            lanes = slice(which * HD, (which + 1) * HD)
            out = slice((2 * which + group) * HD, (2 * which + group + 1) * HD)
            dbc_ref[:, out] = total[:, lanes].astype(BF16)
            wbc_ref[:, which, group * HD : (group + 1) * HD] = taps[10:14, lanes]
    for d in range(blocks):
        small = part[d, 2 * BLK : 2 * BLK + 16].astype(F32)
        raw = small[0:1] + small[1:2]
        dt_ref[2 * d : 2 * d + 1] = raw[:, :BLK]
        dt_ref[2 * d + 1 : 2 * d + 2] = raw[:, BLK:]
        wx_ref[:, d * 2 * HD : (d + 1) * 2 * HD] = small[2:6] + small[6:10]
    odd = lax.rem(idx_ref[0], 2)
    a = dq_own[...]
    b = dq_got[...]
    dq_ref[:, : a.shape[1]] = jnp.where(odd == 0, a, b)
    dq_ref[:, a.shape[1] :] = jnp.where(odd == 0, b, a)
    for done in copies:
        done.wait()


def unpack(place, received, dq_own, dq_got, own):
    blocks = received.shape[0]
    hbm = pl.BlockSpec(memory_space=pltpu.HBM)
    vmem = pl.BlockSpec(memory_space=pltpu.VMEM)
    return pl.pallas_call(
        unpack_kernel,
        out_shape=[
            jax.ShapeDtypeStruct((BLK, blocks * 2 * HD), BF16),
            jax.ShapeDtypeStruct((BLK, 4 * HD), BF16),
            jax.ShapeDtypeStruct((2 * blocks, BLK), F32),
            jax.ShapeDtypeStruct((TAPS, blocks * 2 * HD), F32),
            jax.ShapeDtypeStruct((TAPS, 2, 2 * HD), F32),
            jax.ShapeDtypeStruct((BLK, 2 * dq_own.shape[1]), BF16),
            jax.ShapeDtypeStruct(own.shape, own.dtype),
        ],
        in_specs=[pl.BlockSpec(memory_space=pltpu.SMEM), vmem, vmem, vmem, pl.BlockSpec(memory_space=pl.ANY)],
        out_specs=[hbm, vmem, vmem, vmem, vmem, vmem, pl.BlockSpec(memory_space=pl.ANY)],
        input_output_aliases={4: 6},
        scratch_shapes=[pltpu.SemaphoreType.DMA((blocks,))],
        compiler_params=pltpu.CompilerParams(vmem_limit_bytes=8 * 2**20),
        cost_estimate=pl.CostEstimate(flops=10**6, bytes_accessed=4 * 2**20, transcendentals=0),
        name="unpack",
    )(place, received, dq_own, dq_got, own)


def gate_kernel(*refs):
    pass


def gate(value, *others):
    hbm = pl.BlockSpec(memory_space=pltpu.HBM)
    anywhere = pl.BlockSpec(memory_space=pl.ANY)
    return pl.pallas_call(
        gate_kernel,
        out_shape=jax.ShapeDtypeStruct(value.shape, value.dtype),
        in_specs=[hbm] + [anywhere] * len(others),
        out_specs=hbm,
        input_output_aliases={0: 0},
        compiler_params=pltpu.CompilerParams(vmem_limit_bytes=2**20),
        name="gate",
    )(value, *others)


def kv_pack_kernel(k_ref, v_ref, got, kv_ref):
    for d in range(kv_ref.shape[0]):
        head = slice((d % 2) * HD, (d % 2 + 1) * HD)
        kv_ref[d] = jnp.concatenate([k_ref[:, head], v_ref[:, head]], axis=1)


def kv_pack(key, value, got):
    vmem = pl.BlockSpec(memory_space=pltpu.VMEM)
    shape = (got.shape[0],) + key.shape
    return pl.pallas_call(
        kv_pack_kernel,
        out_shape=jax.ShapeDtypeStruct(shape, BF16),
        in_specs=[vmem, vmem, pl.BlockSpec(memory_space=pl.ANY)],
        out_specs=vmem,
        compiler_params=pltpu.CompilerParams(vmem_limit_bytes=4 * 2**20),
        name="kv_pack",
    )(key, value, got)


def kv_sum_kernel(idx_ref, own, r1, r2, r3, r4, mine, sent):
    total = own[...]
    for got in (r1, r2, r3, r4):
        total = total + got[...].astype(F32)
    rows = mine.shape[0]
    first = total[:rows].astype(BF16)
    second = total[rows:].astype(BF16)
    odd = lax.rem(idx_ref[0], 2)
    mine[...] = jnp.where(odd == 0, first, second)
    sent[...] = jnp.where(odd == 0, second, first)


def kv_total(place, own, received):
    vmem = pl.BlockSpec(memory_space=pltpu.VMEM)
    half = jax.ShapeDtypeStruct((own.shape[0] // 2, own.shape[1]), BF16)
    return pl.pallas_call(
        kv_sum_kernel,
        out_shape=[half, half],
        in_specs=[pl.BlockSpec(memory_space=pltpu.SMEM)]
        + [vmem] * (1 + len(received)),
        out_specs=[vmem, vmem],
        compiler_params=pltpu.CompilerParams(vmem_limit_bytes=4 * 2**20),
        name="kv_total",
    )(place, own, *received)


def kv_place_kernel(idx_ref, mine, other, dk_ref, dv_ref):
    odd = lax.rem(idx_ref[0], 2)
    a = mine[...]
    b = other[...]
    first = jnp.where(odd == 0, a, b)
    second = jnp.where(odd == 0, b, a)
    dk_ref[...] = jnp.concatenate([first[:, :HD], second[:, :HD]], axis=1)
    dv_ref[...] = jnp.concatenate([first[:, HD:], second[:, HD:]], axis=1)


def kv_place(place, mine, other):
    vmem = pl.BlockSpec(memory_space=pltpu.VMEM)
    return pl.pallas_call(
        kv_place_kernel,
        out_shape=[jax.ShapeDtypeStruct(mine.shape, BF16)] * 2,
        in_specs=[pl.BlockSpec(memory_space=pltpu.SMEM), vmem, vmem],
        out_specs=[vmem, vmem],
        compiler_params=pltpu.CompilerParams(vmem_limit_bytes=4 * 2**20),
        name="kv_place",
    )(place, mine, other)


def swap(a):
    return lax.all_to_all(a, "ctx", 0, 0, tiled=True)


def shards(
    x_in, bc_in, conv_x, conv_bc, dt_raw, rate, grad_ssd, query, key, value, d_out, doc_lengths
):
    ctx = lax.axis_size("ctx")
    rows = x_in.shape[0]
    place = lax.axis_index("ctx").astype(jnp.int32).reshape(1)

    odd = place[0] % 2

    def half(a, which):
        return lax.dynamic_slice_in_dim(a, which * (a.shape[1] // 2), a.shape[1] // 2, 1)

    def pick(own, other):
        return jnp.where(odd == 0, own, other), jnp.where(odd == 0, other, own)

    bc_sent = bc_in.reshape(rows, 2, 2, HD).transpose(2, 0, 1, 3).reshape(2, rows, 2 * HD)
    packed = pack(x_in, grad_ssd, bc_sent, dt_raw, ctx)
    qo = jnp.concatenate([half(query, 1 - odd), half(d_out, 1 - odd)], axis=1)
    got = swap(packed)
    kv = swap(kv_pack(key, value, got))
    got_qo = partner(qo)
    mixed = ssm_core(doc_lengths, place, rate, got, conv_x, conv_bc.reshape(TAPS, 4 * HD))
    mixed, kv, got_qo = lax.optimization_barrier((mixed, kv, got_qo))
    back = swap(mixed)
    dq_own, dq_sent, *d_kv = attention_core(doc_lengths, place, query, d_out, got_qo, kv)
    received = [shift(d_kv[by], -2 * by) for by in range(1, BACK // 2 + 1)]
    d_x, d_bc, d_dt, d_wx, d_wbc, d_query, own = unpack(
        place, back, dq_own, partner(dq_sent), d_kv[0]
    )
    mine, sent = kv_total(place, own, received)
    d_key, d_value = kv_place(place, mine, partner(sent))
    return (
        d_x,
        d_bc.reshape(rows, 2, 2 * HD),
        d_dt,
        d_wx,
        d_wbc,
        d_query,
        d_key,
        d_value,
    )


def solution(mesh):
    tokens = P(("dp", "ctx"), "head")
    in_specs = (
        tokens,
        P(("dp", "ctx"), None, "head"),
        P(None, "head"),
        P(None, None, "head"),
        P("head", ("dp", "ctx")),
        P("head"),
        tokens,
        tokens,
        tokens,
        tokens,
        tokens,
        P("dp"),
    )
    out_specs = (
        tokens,
        P(("dp", "ctx"), None, "head"),
        P("head", ("dp", "ctx")),
        P("dp", "head"),
        P("dp", None, "head"),
        tokens,
        tokens,
        tokens,
    )
    return jax.shard_map(shards, mesh=mesh, in_specs=in_specs, out_specs=out_specs, check_vma=False)
```

```python
import jax
import jax.numpy as jnp
from jax import lax
from jax.experimental import pallas as pl
from jax.experimental.pallas import tpu as pltpu
from jax.sharding import PartitionSpec as P

F32 = jnp.float32
BF16 = jnp.bfloat16
HD = 128
BLK = 128
TAPS = 4
BACK = 8
LOG2E = 1.4426950408889634
NEG_BIG = -1e30
UNROLL = 4


def dot_nn(a, b):
    return lax.dot_general(a, b, (((1,), (0,)), ((), ())), preferred_element_type=F32)


def dot_nt(a, b):
    return lax.dot_general(a, b, (((1,), (1,)), ((), ())), preferred_element_type=F32)


def dot_tn(a, b):
    return lax.dot_general(a, b, (((0,), (0,)), ((), ())), preferred_element_type=F32)


def doc_bounds(doc_ref):
    s1 = doc_ref[0]
    s2 = s1 + doc_ref[1]
    s3 = s2 + doc_ref[2]
    return s1, s2, s3


def start_at(pos, bounds):
    s1, s2, s3 = bounds
    return jnp.where(pos >= s3, s3, jnp.where(pos >= s2, s2, jnp.where(pos >= s1, s1, 0)))


def next_start(pos, bounds, total):
    s1, s2, s3 = bounds
    return jnp.where(pos < s1, s1, jnp.where(pos < s2, s2, jnp.where(pos < s3, s3, total)))


def twice(a):
    return jnp.concatenate([a, a], axis=1)


def fold_rows(a):
    return jnp.sum(a.reshape(a.shape[0] // 8, 8, a.shape[1]), axis=0)


def split3(a):
    hi = a.astype(BF16)
    rest = a - hi.astype(F32)
    mid = rest.astype(BF16)
    return hi, mid, (rest - mid.astype(F32)).astype(BF16)


def dot_exact(a, ones):
    rows = a.shape[0]
    out = dot_nn(jnp.concatenate(split3(a), axis=0), ones.astype(BF16))
    return out[:rows] + out[rows : 2 * rows] + out[2 * rows :]


def ssm_kernel(
    doc_ref, idx_ref, rate_ref, r_ref, wx_ref, wbc_ref, out_ref,
    xs_s, xp_s, u_s, b_s, c_s, bm_s, cm_s, dsx_s, dsbc_s, st_s, ds_s,
    cols_s, elt_s, x2_s, y2_s, es_s, tapx_s, tapbc_s,
):
    blocks = r_ref.shape[0]
    total = blocks * BLK
    place = idx_ref[0]
    bounds = doc_bounds(doc_ref)
    rate0 = rate_ref[2 * place]
    rate1 = rate_ref[2 * place + 1]
    group = place // (blocks // 2)
    wx = wx_ref[:, pl.ds(pl.multiple_of(place * 256, 256), 256)]
    wbc = jnp.concatenate(
        [
            wbc_ref[:, 0, pl.ds(pl.multiple_of(group * 128, 128), 128)],
            wbc_ref[:, 1, pl.ds(pl.multiple_of(group * 128, 128), 128)],
        ],
        axis=1,
    )

    for c in range(blocks):
        row = jnp.sum(r_ref[c, 3 * BLK : 3 * BLK + 16, :].astype(F32), axis=0, keepdims=True)
        x2_s[c : c + 1] = row[:, :128]
        x2_s[blocks + c : blocks + c + 1] = row[:, 128:]
    raw = x2_s[...]
    step = jnp.log(1.0 + jnp.exp(raw))
    sig = 1.0 / (1.0 + jnp.exp(-raw))
    row_ids = lax.broadcasted_iota(jnp.int32, (2 * blocks, 128), 0)
    rate = jnp.where(row_ids < blocks, rate0, rate1)
    ii = lax.broadcasted_iota(jnp.int32, (128, 128), 0)
    jj = lax.broadcasted_iota(jnp.int32, (128, 128), 1)
    cum = dot_exact(-step * rate, (ii <= jj).astype(F32))
    v_rows = jnp.exp(cum)
    u_hi, u_lo, _ = split3(step * jnp.exp(-cum))
    v_hi, v_lo, _ = split3(v_rows)
    last = jnp.broadcast_to(v_rows[:, 127:128], (2 * blocks, 128))
    pieces = [a.astype(F32) for a in (u_hi, u_lo, v_hi, v_lo)]
    for c in range(blocks):
        rows = [a[at : at + 1] for a in pieces for at in (c, blocks + c)]
        cols_s[c] = jnp.concatenate(rows, axis=0)
        elt_s[c] = jnp.broadcast_to(
            jnp.concatenate([last[c : c + 1], last[blocks + c : blocks + c + 1]], axis=1), (8, 256)
        )
    row8 = lax.broadcasted_iota(jnp.int32, (8, 512), 0)
    lane8 = lax.broadcasted_iota(jnp.int32, (8, 512), 1) // 128
    spread = ((lane8 // 2 == row8 // 4) & (lane8 % 2 == row8 % 2)).astype(BF16)

    edge = jnp.zeros((8, 256), F32)
    st_s[0] = jnp.zeros((128, 256), F32)

    def conv(edge, value, weight, keeps):
        win = jnp.concatenate([edge, value], axis=0)
        pre = value * weight[TAPS - 1 : TAPS]
        for d in range(1, TAPS):
            pre = pre + jnp.where(keeps[d - 1], win[8 - d : 8 - d + BLK], 0.0) * weight[TAPS - 1 - d : TAPS - d]
        sg = 0.5 * jnp.tanh(0.5 * pre) + 0.5
        val = pre * sg
        return val, sg + val * (1.0 - sg)

    def forward(c, carry):
        base = pl.multiple_of(c * BLK, BLK)
        edge_x, edge_bc = carry
        x = r_ref[c, 0:BLK].astype(F32)
        bc_raw = r_ref[c, 2 * BLK : 3 * BLK].astype(F32)
        pos = base + ii
        start = start_at(pos, bounds)
        last_start = start_at(base + BLK - 1, bounds)
        tails = pos >= last_start
        dist = pos - start
        keeps = [twice(dist >= d) for d in range(1, TAPS)]
        xs, dsx = conv(edge_x, x, wx, keeps)
        bc, dsbc = conv(edge_bc, bc_raw, wbc, keeps)
        xs_s[c] = xs
        dsx_s[c] = dsx
        dsbc_s[c] = dsbc
        b = bc[:, :128]
        cc = bc[:, 128:]
        b_s[c] = b.astype(BF16)
        c_s[c] = cc.astype(BF16)
        bm = jnp.where(tails, b, 0.0).astype(BF16)
        bm_s[c] = bm
        cm_s[c] = jnp.where(start < base, cc, 0.0).astype(BF16)
        u = dot_tn(cols_s[c].astype(BF16), spread[:, :256])
        u_s[c] = u
        xp = (xs * u).astype(BF16)
        xp_s[c] = xp
        elt = elt_s[c][0:1]
        keep = jnp.where(last_start < base, elt, 0.0)
        st_s[c + 1] = keep * st_s[c] + elt * dot_tn(bm, xp)
        return x[BLK - 8 :], bc_raw[BLK - 8 :]

    lax.fori_loop(0, blocks, forward, (edge, edge), unroll=UNROLL)

    ds_s[...] = jnp.zeros((128, 256), F32)
    tapx_s[...] = jnp.zeros((TAPS, 8, 256), F32)
    tapbc_s[...] = jnp.zeros((TAPS, 8, 256), F32)
    lane2 = lax.broadcasted_iota(jnp.int32, (16, 256), 1)
    row2 = lax.broadcasted_iota(jnp.int32, (16, 256), 0)
    pick = (lane2 // 128 == row2).astype(BF16)

    def head_sums(out, c, a):
        sums = dot_nt(pick, a.astype(BF16))
        out[pl.ds(c, 1)] = sums[0:1]
        out[pl.ds(blocks + c, 1)] = sums[1:2]

    def conv_back(grad, edge, raw_in, weight, ends, taps):
        win = jnp.concatenate([grad, edge], axis=0)
        total_grad = grad * weight[TAPS - 1 : TAPS]
        taps[TAPS - 1] += fold_rows(grad * raw_in)
        for d in range(1, TAPS):
            moved = jnp.where(ends[d - 1], win[d : d + BLK], 0.0)
            total_grad = total_grad + moved * weight[TAPS - 1 - d : TAPS - d]
            taps[TAPS - 1 - d] += fold_rows(moved * raw_in)
        return total_grad

    def backward(lap, carry):
        c = blocks - 1 - lap
        base = pl.multiple_of(c * BLK, BLK)
        pos = base + ii
        start = start_at(pos, bounds)
        last_start = start_at(base + BLK - 1, bounds)
        causal = (jj <= ii) & (base + jj >= start)
        leads = start < base
        tails = pos >= last_start
        b = b_s[c]
        cc = c_s[c]
        xp = xp_s[c]
        cm = cm_s[c]
        gv = r_ref[c, BLK : 2 * BLK].astype(F32) * dot_tn(cols_s[c].astype(BF16), spread[:, 256:])
        gp = gv.astype(BF16)
        elt = elt_s[c][0:1]
        ds = ds_s[...]
        es_s[pl.ds(pl.multiple_of(c * 8, 8), 8)] = fold_rows(ds * st_s[c + 1])
        sb = st_s[c].astype(BF16)
        ds_e = elt * ds
        dsb = ds_e.astype(BF16)
        ds_s[...] = jnp.where(last_start < base, ds_e, 0.0) + dot_tn(cm, gp)
        w = jnp.where(causal, dot_nt(cc, b), 0.0).astype(BF16)
        yv = dot_nn(w, xp) + dot_nn(cm, sb)
        dxp = dot_tn(w, gp) + dot_nn(bm_s[c], dsb)
        z = jnp.where(causal, dot_nt(gp, xp), 0.0).astype(BF16)
        dc = dot_nn(z, b) + jnp.where(leads, dot_nt(gp, sb), 0.0)
        db = dot_tn(z, cc) + jnp.where(tails, dot_nt(xp, dsb), 0.0)
        dx = u_s[c] * dxp
        head_sums(x2_s, c, xs_s[c] * dx)
        head_sums(y2_s, c, gv * yv)
        left = next_start(pos, bounds, total) - pos
        ends = [twice(left > d) for d in range(1, TAPS)]
        edge_x, edge_bc = carry
        pre_x = dx * dsx_s[c]
        pre_bc = jnp.concatenate([db, dc], axis=1) * dsbc_s[c]
        x = r_ref[c, 0:BLK].astype(F32)
        bc_raw = r_ref[c, 2 * BLK : 3 * BLK].astype(F32)
        out_ref[c, 0:BLK] = conv_back(pre_x, edge_x, x, wx, ends, tapx_s).astype(BF16)
        out_ref[c, BLK : 2 * BLK] = conv_back(
            pre_bc, edge_bc, bc_raw, wbc, ends, tapbc_s
        ).astype(BF16)
        return pre_x[0:8], pre_bc[0:8]

    lax.fori_loop(0, blocks, backward, (edge, edge), unroll=UNROLL)

    xdx = x2_s[...]
    carry_sum = jnp.sum(es_s[...].reshape(blocks, 8, 256), axis=1)
    carry_sum = jnp.concatenate([carry_sum[:, :128], carry_sum[:, 128:]], axis=0)
    d_log = dot_exact(y2_s[...] - xdx, (ii >= jj).astype(F32))
    d_log = d_log + jnp.sum(carry_sum, axis=1, keepdims=True)
    d_raw = (xdx / step - rate * d_log) * sig
    d_raw = jnp.concatenate([d_raw[:blocks], d_raw[blocks:]], axis=1)
    raw_hi = d_raw.astype(BF16).astype(F32)
    raw_lo = d_raw - raw_hi
    tapx = jnp.concatenate([jnp.sum(tapx_s[k], axis=0, keepdims=True) for k in range(TAPS)], axis=0)
    tapbc = jnp.concatenate([jnp.sum(tapbc_s[k], axis=0, keepdims=True) for k in range(TAPS)], axis=0)
    tapx_hi = tapx.astype(BF16).astype(F32)
    rest = jnp.concatenate([tapx_hi, tapx - tapx_hi, tapbc, jnp.zeros((2, 256), F32)], axis=0)
    for c in range(blocks):
        out_ref[c, 2 * BLK : 2 * BLK + 16] = jnp.concatenate(
            [raw_hi[c : c + 1], raw_lo[c : c + 1], rest], axis=0
        ).astype(BF16)


def ssm_core(doc_lengths, place, rate, received, weight_x, weight_bc):
    blocks = received.shape[0]
    smem = pl.BlockSpec(memory_space=pltpu.SMEM)
    vmem = pl.BlockSpec(memory_space=pltpu.VMEM)

    def scratch(*shape, dtype=F32):
        return pltpu.VMEM(shape, dtype)

    return pl.pallas_call(
        ssm_kernel,
        out_shape=jax.ShapeDtypeStruct((blocks, 2 * BLK + 16, 256), BF16),
        in_specs=[smem, smem, smem, vmem, vmem, vmem],
        out_specs=vmem,
        scratch_shapes=[
            scratch(blocks, BLK, 256),
            scratch(blocks, BLK, 256, dtype=BF16),
            scratch(blocks, BLK, 256),
            scratch(blocks, BLK, 128, dtype=BF16),
            scratch(blocks, BLK, 128, dtype=BF16),
            scratch(blocks, BLK, 128, dtype=BF16),
            scratch(blocks, BLK, 128, dtype=BF16),
            scratch(blocks, BLK, 256),
            scratch(blocks, BLK, 256),
            scratch(blocks + 1, 128, 256),
            scratch(128, 256),
            scratch(blocks, 8, 128),
            scratch(blocks, 8, 256),
            scratch(2 * blocks, 128),
            scratch(2 * blocks, 128),
            scratch(8 * blocks, 256),
            scratch(TAPS, 8, 256),
            scratch(TAPS, 8, 256),
        ],
        compiler_params=pltpu.CompilerParams(vmem_limit_bytes=24 * 2**20),
        cost_estimate=pl.CostEstimate(flops=3 * 10**9, bytes_accessed=6 * 2**20, transcendentals=4 * 10**6),
        name="mixer",
    )(doc_lengths, place, rate, received, weight_x, weight_bc)


def attention_kernel(
    doc_ref, idx_ref, q_ref, do_ref, got_ref, kv_ref,
    dq_own, dq_sent, d0, d1, d2, d3, d4, kt_s, dk_s, dv_s, s_s, p_s,
):
    d_refs = (d4, d3, d2, d1, d0)
    count = 2 * len(d_refs)
    bounds = doc_bounds(doc_ref)
    scale = HD ** (-0.5)
    place = idx_ref[0]
    odd = lax.rem(place, 2)
    base = (place - odd) * BLK
    jrow = lax.broadcasted_iota(jnp.int32, (BLK, 2 * BLK), 0)
    icol = lax.broadcasted_iota(jnp.int32, (BLK, 2 * BLK), 1)
    start = start_at(base + icol[0:1], bounds) - base
    heads = got_ref.shape[1] // (2 * HD)

    def rows8(a):
        return a.reshape(BLK // 8, 8, 2 * BLK)

    def half(b):
        return slice((b % 2) * BLK, (b % 2 + 1) * BLK)

    def key_rows(b):
        return kv_ref[jnp.maximum(place - odd - BACK + b, 0), :, 0:HD]

    def value_rows(b):
        return kv_ref[jnp.maximum(place - odd - BACK + b, 0), :, HD : 2 * HD]

    def in_order(own, other):
        first = jnp.where(odd == 0, own, other)
        second = jnp.where(odd == 0, other, own)
        return jnp.concatenate([first, second], axis=0)

    for b in range(count):
        kt_s[b] = key_rows(b).T
    dk_s[...] = jnp.zeros(dk_s.shape, F32)
    dv_s[...] = jnp.zeros(dv_s.shape, F32)

    def turn(head, carry):
        at = pl.multiple_of(head * HD, HD)
        own_at = pl.multiple_of((odd * heads + head) * HD, HD)
        q = in_order(q_ref[:, pl.ds(own_at, HD)], got_ref[:, pl.ds(at, HD)])
        do = in_order(
            do_ref[:, pl.ds(own_at, HD)], got_ref[:, pl.ds(pl.multiple_of(heads * HD + at, HD), HD)]
        )
        top = jnp.full((8, 2 * BLK), NEG_BIG, F32)
        for b in range(count):
            allowed = jrow >= start + (BACK - b) * BLK
            if b >= BACK:
                allowed = allowed & (jrow + (b - BACK) * BLK <= icol)
            s = jnp.where(allowed, dot_nt(key_rows(b), q), NEG_BIG)
            s_s[b] = s
            top = jnp.maximum(top, jnp.max(rows8(s), axis=0))
            p_s[b] = dot_nt(value_rows(b), do)
        top = jnp.max(top, axis=0, keepdims=True) * (scale * LOG2E)
        norm = jnp.zeros((8, 2 * BLK), F32)
        mean = jnp.zeros((8, 2 * BLK), F32)
        for b in range(count):
            e = jnp.exp2(s_s[b] * (scale * LOG2E) - top)
            s_s[b] = e
            norm = norm + jnp.sum(rows8(e), axis=0)
            mean = mean + jnp.sum(rows8(e * p_s[b]), axis=0)
        inverse = 1.0 / jnp.sum(norm, axis=0, keepdims=True)
        mean = jnp.sum(mean, axis=0, keepdims=True) * inverse
        dqt = jnp.zeros((HD, 2 * BLK), F32)
        for b in range(count):
            prob = s_s[b] * inverse
            grad = (prob * (p_s[b] - mean)).astype(BF16)
            dv_s[b] += dot_nn(prob.astype(BF16), do)
            dk_s[b] += dot_nn(grad, q)
            dqt = dqt + dot_nn(kt_s[b], grad)
        dqt = dqt * scale
        first = dqt[:, :BLK].T
        second = dqt[:, BLK:].T
        dq_own[:, pl.ds(at, HD)] = jnp.where(odd == 0, first, second).astype(BF16)
        dq_sent[:, pl.ds(at, HD)] = jnp.where(odd == 0, second, first).astype(BF16)
        return carry

    lax.fori_loop(0, heads, turn, 0)
    for b in range(count):
        out = d_refs[b // 2]
        out[half(b), 0:HD] = (dk_s[b] * scale).astype(out.dtype)
        out[half(b), HD : 2 * HD] = dv_s[b].astype(out.dtype)


def attention_core(doc_lengths, place, query, d_out, got, kv):
    smem = pl.BlockSpec(memory_space=pltpu.SMEM)
    vmem = pl.BlockSpec(memory_space=pltpu.VMEM)
    pairs = BACK // 2 + 1
    count = 2 * pairs
    rows, width = query.shape
    part = jax.ShapeDtypeStruct((rows, width // 2), BF16)
    kv_shape = (2 * rows, 2 * HD)
    outs = [part, part, jax.ShapeDtypeStruct(kv_shape, F32)]
    outs += [jax.ShapeDtypeStruct(kv_shape, BF16)] * (pairs - 1)
    return pl.pallas_call(
        attention_kernel,
        out_shape=outs,
        in_specs=[smem, smem] + [vmem] * 4,
        out_specs=[vmem] * (2 + pairs),
        scratch_shapes=[
            pltpu.VMEM((count, HD, BLK), BF16),
            pltpu.VMEM((count, BLK, HD), F32),
            pltpu.VMEM((count, BLK, HD), F32),
            pltpu.VMEM((count, BLK, 2 * BLK), F32),
            pltpu.VMEM((count, BLK, 2 * BLK), F32),
        ],
        compiler_params=pltpu.CompilerParams(vmem_limit_bytes=16 * 2**20),
        cost_estimate=pl.CostEstimate(flops=4 * 10**9, bytes_accessed=4 * 2**20, transcendentals=3 * 10**6),
        name="attention",
    )(doc_lengths, place, query, d_out, got, kv)


def shift(a, by):
    devices = lax.axis_size("ctx")
    return lax.ppermute(
        a, "ctx", [(i, i + by) for i in range(devices) if 0 <= i + by < devices]
    )


def partner(a):
    return lax.ppermute(a, "ctx", [(i, i ^ 1) for i in range(lax.axis_size("ctx"))])


def pack_kernel(
    x_ref, g_ref, bc_ref, dt_ref, k_ref, v_ref, out_ref, kv_ref, buf, kv_buf, in_sems, out_sems, kv_sem
):
    blocks = out_ref.shape[0]
    loads = []
    for d in range(blocks):
        lanes = pl.ds(d * 2 * HD, 2 * HD)
        pair = [
            pltpu.make_async_copy(src, buf.at[d, pl.ds(at * BLK, BLK)], in_sems.at[2 * d + at])
            for at, src in enumerate((x_ref.at[:, lanes], g_ref.at[:, lanes]))
        ]
        for one in pair:
            one.start()
        loads.append(pair)
    b_all = bc_ref[:, 0, :]
    c_all = bc_ref[:, 1, :]
    bc = [
        jnp.concatenate([b_all[:, at : at + HD], c_all[:, at : at + HD]], axis=1) for at in (0, HD)
    ]
    for d in range(blocks):
        buf[d, 2 * BLK : 3 * BLK] = bc[d // (blocks // 2)]
        raw = jnp.concatenate([dt_ref[2 * d : 2 * d + 1], dt_ref[2 * d + 1 : 2 * d + 2]], axis=1)
        hi = raw.astype(BF16).astype(F32)
        mid = (raw - hi).astype(BF16).astype(F32)
        parts = [hi, mid, raw - hi - mid, jnp.zeros((13, 2 * BLK), F32)]
        buf[d, 3 * BLK : 3 * BLK + 16] = jnp.concatenate(parts, axis=0).astype(BF16)
        head = slice((d % 2) * HD, (d % 2 + 1) * HD)
        kv_buf[d] = jnp.concatenate([k_ref[:, head], v_ref[:, head]], axis=1)
    stores = []
    for d in range(blocks):
        for one in loads[d]:
            one.wait()
        stores.append(pltpu.make_async_copy(buf.at[d], out_ref.at[d], out_sems.at[d]))
        stores[-1].start()
    stores.append(pltpu.make_async_copy(kv_buf, kv_ref, kv_sem))
    stores[-1].start()
    for one in stores:
        one.wait()


def pack(x_in, grad, bc_sent, dt_raw, key, value, blocks):
    hbm = pl.BlockSpec(memory_space=pltpu.HBM)
    vmem = pl.BlockSpec(memory_space=pltpu.VMEM)
    return pl.pallas_call(
        pack_kernel,
        out_shape=[
            jax.ShapeDtypeStruct((blocks, 3 * BLK + 16, 2 * HD), BF16),
            jax.ShapeDtypeStruct((blocks, BLK, 2 * HD), BF16),
        ],
        in_specs=[hbm, hbm, vmem, vmem, vmem, vmem],
        out_specs=[hbm, hbm],
        scratch_shapes=[
            pltpu.VMEM((blocks, 3 * BLK + 16, 2 * HD), BF16),
            pltpu.VMEM((blocks, BLK, 2 * HD), BF16),
            pltpu.SemaphoreType.DMA((2 * blocks,)),
            pltpu.SemaphoreType.DMA((blocks,)),
            pltpu.SemaphoreType.DMA(()),
        ],
        cost_estimate=pl.CostEstimate(flops=0, bytes_accessed=7 * 2**20, transcendentals=0),
        name="pack",
    )(x_in, grad, bc_sent, dt_raw, key, value)


def unpack_kernel(
    idx_ref, part, dq_own, dq_got, own, dx_ref, dbc_ref, dt_ref, wx_ref, wbc_ref, dq_ref, passed, sems
):
    blocks = part.shape[0]
    half = blocks // 2
    copies = []
    for d in range(blocks):
        lanes = pl.ds(d * 2 * HD, 2 * HD)
        copies.append(pltpu.make_async_copy(part.at[d, pl.ds(0, BLK)], dx_ref.at[:, lanes], sems.at[d]))
        copies[-1].start()
    for group in range(2):
        at = [group * half + d for d in range(half)]
        total = part[at[0], BLK : 2 * BLK].astype(F32)
        taps = part[at[0], 2 * BLK : 2 * BLK + 16].astype(F32)
        for d in at[1:]:
            total = total + part[d, BLK : 2 * BLK].astype(F32)
            taps = taps + part[d, 2 * BLK : 2 * BLK + 16].astype(F32)
        for which in range(2):
            lanes = slice(which * HD, (which + 1) * HD)
            out = slice((2 * which + group) * HD, (2 * which + group + 1) * HD)
            dbc_ref[:, out] = total[:, lanes].astype(BF16)
            wbc_ref[:, which, group * HD : (group + 1) * HD] = taps[10:14, lanes]
    for d in range(blocks):
        small = part[d, 2 * BLK : 2 * BLK + 16].astype(F32)
        raw = small[0:1] + small[1:2]
        dt_ref[2 * d : 2 * d + 1] = raw[:, :BLK]
        dt_ref[2 * d + 1 : 2 * d + 2] = raw[:, BLK:]
        wx_ref[:, d * 2 * HD : (d + 1) * 2 * HD] = small[2:6] + small[6:10]
    odd = lax.rem(idx_ref[0], 2)
    a = dq_own[...]
    b = dq_got[...]
    dq_ref[:, : a.shape[1]] = jnp.where(odd == 0, a, b)
    dq_ref[:, a.shape[1] :] = jnp.where(odd == 0, b, a)
    for done in copies:
        done.wait()


def unpack(place, received, dq_own, dq_got, own):
    blocks = received.shape[0]
    hbm = pl.BlockSpec(memory_space=pltpu.HBM)
    vmem = pl.BlockSpec(memory_space=pltpu.VMEM)
    return pl.pallas_call(
        unpack_kernel,
        out_shape=[
            jax.ShapeDtypeStruct((BLK, blocks * 2 * HD), BF16),
            jax.ShapeDtypeStruct((BLK, 4 * HD), BF16),
            jax.ShapeDtypeStruct((2 * blocks, BLK), F32),
            jax.ShapeDtypeStruct((TAPS, blocks * 2 * HD), F32),
            jax.ShapeDtypeStruct((TAPS, 2, 2 * HD), F32),
            jax.ShapeDtypeStruct((BLK, 2 * dq_own.shape[1]), BF16),
            jax.ShapeDtypeStruct(own.shape, own.dtype),
        ],
        in_specs=[pl.BlockSpec(memory_space=pltpu.SMEM), vmem, vmem, vmem, pl.BlockSpec(memory_space=pl.ANY)],
        out_specs=[hbm, vmem, vmem, vmem, vmem, vmem, pl.BlockSpec(memory_space=pl.ANY)],
        input_output_aliases={4: 6},
        scratch_shapes=[pltpu.SemaphoreType.DMA((blocks,))],
        compiler_params=pltpu.CompilerParams(vmem_limit_bytes=8 * 2**20),
        cost_estimate=pl.CostEstimate(flops=10**6, bytes_accessed=4 * 2**20, transcendentals=0),
        name="unpack",
    )(place, received, dq_own, dq_got, own)


def gate_kernel(*refs):
    pass


def gate(value, *others):
    hbm = pl.BlockSpec(memory_space=pltpu.HBM)
    anywhere = pl.BlockSpec(memory_space=pl.ANY)
    return pl.pallas_call(
        gate_kernel,
        out_shape=jax.ShapeDtypeStruct(value.shape, value.dtype),
        in_specs=[hbm] + [anywhere] * len(others),
        out_specs=hbm,
        input_output_aliases={0: 0},
        compiler_params=pltpu.CompilerParams(vmem_limit_bytes=2**20),
        name="gate",
    )(value, *others)


def kv_pack_kernel(k_ref, v_ref, got, kv_ref):
    for d in range(kv_ref.shape[0]):
        head = slice((d % 2) * HD, (d % 2 + 1) * HD)
        kv_ref[d] = jnp.concatenate([k_ref[:, head], v_ref[:, head]], axis=1)


def kv_pack(key, value, got):
    vmem = pl.BlockSpec(memory_space=pltpu.VMEM)
    shape = (got.shape[0],) + key.shape
    return pl.pallas_call(
        kv_pack_kernel,
        out_shape=jax.ShapeDtypeStruct(shape, BF16),
        in_specs=[vmem, vmem, pl.BlockSpec(memory_space=pl.ANY)],
        out_specs=vmem,
        compiler_params=pltpu.CompilerParams(vmem_limit_bytes=4 * 2**20),
        name="kv_pack",
    )(key, value, got)


def kv_sum_kernel(idx_ref, own, r1, r2, r3, r4, mine, sent):
    total = own[...]
    for got in (r1, r2, r3, r4):
        total = total + got[...].astype(F32)
    rows = mine.shape[0]
    first = total[:rows].astype(BF16)
    second = total[rows:].astype(BF16)
    odd = lax.rem(idx_ref[0], 2)
    mine[...] = jnp.where(odd == 0, first, second)
    sent[...] = jnp.where(odd == 0, second, first)


def kv_total(place, own, received):
    vmem = pl.BlockSpec(memory_space=pltpu.VMEM)
    half = jax.ShapeDtypeStruct((own.shape[0] // 2, own.shape[1]), BF16)
    return pl.pallas_call(
        kv_sum_kernel,
        out_shape=[half, half],
        in_specs=[pl.BlockSpec(memory_space=pltpu.SMEM)]
        + [vmem] * (1 + len(received)),
        out_specs=[vmem, vmem],
        compiler_params=pltpu.CompilerParams(vmem_limit_bytes=4 * 2**20),
        name="kv_total",
    )(place, own, *received)


def kv_place_kernel(idx_ref, mine, other, dk_ref, dv_ref):
    odd = lax.rem(idx_ref[0], 2)
    a = mine[...]
    b = other[...]
    first = jnp.where(odd == 0, a, b)
    second = jnp.where(odd == 0, b, a)
    dk_ref[...] = jnp.concatenate([first[:, :HD], second[:, :HD]], axis=1)
    dv_ref[...] = jnp.concatenate([first[:, HD:], second[:, HD:]], axis=1)


def kv_place(place, mine, other):
    vmem = pl.BlockSpec(memory_space=pltpu.VMEM)
    return pl.pallas_call(
        kv_place_kernel,
        out_shape=[jax.ShapeDtypeStruct(mine.shape, BF16)] * 2,
        in_specs=[pl.BlockSpec(memory_space=pltpu.SMEM), vmem, vmem],
        out_specs=[vmem, vmem],
        compiler_params=pltpu.CompilerParams(vmem_limit_bytes=4 * 2**20),
        name="kv_place",
    )(place, mine, other)


def swap(a):
    return lax.all_to_all(a, "ctx", 0, 0, tiled=True)


def shards(
    x_in, bc_in, conv_x, conv_bc, dt_raw, rate, grad_ssd, query, key, value, d_out, doc_lengths
):
    ctx = lax.axis_size("ctx")
    rows = x_in.shape[0]
    place = lax.axis_index("ctx").astype(jnp.int32).reshape(1)

    odd = place[0] % 2

    def half(a, which):
        return lax.dynamic_slice_in_dim(a, which * (a.shape[1] // 2), a.shape[1] // 2, 1)

    def pick(own, other):
        return jnp.where(odd == 0, own, other), jnp.where(odd == 0, other, own)

    packed, kv_sent = pack(x_in, grad_ssd, bc_in, dt_raw, key, value, ctx)
    qo = jnp.concatenate([half(query, 1 - odd), half(d_out, 1 - odd)], axis=1)
    got = swap(packed)
    got, kv_sent = lax.optimization_barrier((got, kv_sent))
    kv = swap(kv_sent)
    got_qo = partner(qo)
    mixed = ssm_core(doc_lengths, place, rate, got, conv_x, conv_bc)
    mixed, kv, got_qo = lax.optimization_barrier((mixed, kv, got_qo))
    back = swap(mixed)
    dq_own, dq_sent, *d_kv = attention_core(doc_lengths, place, query, d_out, got_qo, kv)
    received = [shift(d_kv[by], -2 * by) for by in range(1, BACK // 2 + 1)]
    d_x, d_bc, d_dt, d_wx, d_wbc, d_query, own = unpack(
        place, back, dq_own, partner(dq_sent), d_kv[0]
    )
    mine, sent = kv_total(place, own, received)
    d_key, d_value = kv_place(place, mine, partner(sent))
    return (
        d_x,
        d_bc.reshape(rows, 2, 2 * HD),
        d_dt,
        d_wx,
        d_wbc,
        d_query,
        d_key,
        d_value,
    )


def solution(mesh):
    tokens = P(("dp", "ctx"), "head")
    in_specs = (
        tokens,
        P(("dp", "ctx"), None, "head"),
        P(None, "head"),
        P(None, None, "head"),
        P("head", ("dp", "ctx")),
        P("head"),
        tokens,
        tokens,
        tokens,
        tokens,
        tokens,
        P("dp"),
    )
    out_specs = (
        tokens,
        P(("dp", "ctx"), None, "head"),
        P("head", ("dp", "ctx")),
        P("dp", "head"),
        P("dp", None, "head"),
        tokens,
        tokens,
        tokens,
    )
    return jax.shard_map(shards, mesh=mesh, in_specs=in_specs, out_specs=out_specs, check_vma=False)
```

```python
import jax
import jax.numpy as jnp
from jax import lax
from jax.experimental import pallas as pl
from jax.experimental.pallas import tpu as pltpu
from jax.sharding import PartitionSpec as P

F32 = jnp.float32
BF16 = jnp.bfloat16
HD = 128
BLK = 128
TAPS = 4
BACK = 8
LOG2E = 1.4426950408889634
NEG_BIG = -1e30
UNROLL = 8


def dot_nn(a, b):
    return lax.dot_general(a, b, (((1,), (0,)), ((), ())), preferred_element_type=F32)


def dot_nt(a, b):
    return lax.dot_general(a, b, (((1,), (1,)), ((), ())), preferred_element_type=F32)


def dot_tn(a, b):
    return lax.dot_general(a, b, (((0,), (0,)), ((), ())), preferred_element_type=F32)


def doc_bounds(doc_ref):
    s1 = doc_ref[0]
    s2 = s1 + doc_ref[1]
    s3 = s2 + doc_ref[2]
    return s1, s2, s3


def start_at(pos, bounds):
    s1, s2, s3 = bounds
    return jnp.where(pos >= s3, s3, jnp.where(pos >= s2, s2, jnp.where(pos >= s1, s1, 0)))


def next_start(pos, bounds, total):
    s1, s2, s3 = bounds
    return jnp.where(pos < s1, s1, jnp.where(pos < s2, s2, jnp.where(pos < s3, s3, total)))


def twice(a):
    return jnp.concatenate([a, a], axis=1)


def fold_rows(a):
    return jnp.sum(a.reshape(a.shape[0] // 8, 8, a.shape[1]), axis=0)


def split3(a):
    hi = a.astype(BF16)
    rest = a - hi.astype(F32)
    mid = rest.astype(BF16)
    return hi, mid, (rest - mid.astype(F32)).astype(BF16)


def dot_exact(a, ones):
    rows = a.shape[0]
    out = dot_nn(jnp.concatenate(split3(a), axis=0), ones.astype(BF16))
    return out[:rows] + out[rows : 2 * rows] + out[2 * rows :]


def ssm_kernel(
    doc_ref, idx_ref, rate_ref, r_ref, wx_ref, wbc_ref, out_ref,
    xs_s, xp_s, u_s, b_s, c_s, bm_s, cm_s, dsx_s, dsbc_s, st_s, ds_s,
    cols_s, elt_s, x2_s, y2_s, es_s, tapx_s, tapbc_s,
):
    blocks = r_ref.shape[0]
    total = blocks * BLK
    place = idx_ref[0]
    bounds = doc_bounds(doc_ref)
    rate0 = rate_ref[2 * place]
    rate1 = rate_ref[2 * place + 1]
    group = place // (blocks // 2)
    wx = wx_ref[:, pl.ds(pl.multiple_of(place * 256, 256), 256)]
    wbc = jnp.concatenate(
        [
            wbc_ref[:, 0, pl.ds(pl.multiple_of(group * 128, 128), 128)],
            wbc_ref[:, 1, pl.ds(pl.multiple_of(group * 128, 128), 128)],
        ],
        axis=1,
    )

    for c in range(blocks):
        row = jnp.sum(r_ref[c, 3 * BLK : 3 * BLK + 16, :].astype(F32), axis=0, keepdims=True)
        x2_s[c : c + 1] = row[:, :128]
        x2_s[blocks + c : blocks + c + 1] = row[:, 128:]
    raw = x2_s[...]
    step = jnp.log(1.0 + jnp.exp(raw))
    sig = 1.0 / (1.0 + jnp.exp(-raw))
    row_ids = lax.broadcasted_iota(jnp.int32, (2 * blocks, 128), 0)
    rate = jnp.where(row_ids < blocks, rate0, rate1)
    ii = lax.broadcasted_iota(jnp.int32, (128, 128), 0)
    jj = lax.broadcasted_iota(jnp.int32, (128, 128), 1)
    cum = dot_exact(-step * rate, (ii <= jj).astype(F32))
    v_rows = jnp.exp(cum)
    u_hi, u_lo, _ = split3(step * jnp.exp(-cum))
    v_hi, v_lo, _ = split3(v_rows)
    last = jnp.broadcast_to(v_rows[:, 127:128], (2 * blocks, 128))
    pieces = [a.astype(F32) for a in (u_hi, u_lo, v_hi, v_lo)]
    for c in range(blocks):
        rows = [a[at : at + 1] for a in pieces for at in (c, blocks + c)]
        cols_s[c] = jnp.concatenate(rows, axis=0)
        elt_s[c] = jnp.broadcast_to(
            jnp.concatenate([last[c : c + 1], last[blocks + c : blocks + c + 1]], axis=1), (8, 256)
        )
    row8 = lax.broadcasted_iota(jnp.int32, (8, 512), 0)
    lane8 = lax.broadcasted_iota(jnp.int32, (8, 512), 1) // 128
    spread = ((lane8 // 2 == row8 // 4) & (lane8 % 2 == row8 % 2)).astype(BF16)

    edge = jnp.zeros((8, 256), F32)
    st_s[0] = jnp.zeros((128, 256), F32)

    def conv(edge, value, weight, keeps):
        win = jnp.concatenate([edge, value], axis=0)
        pre = value * weight[TAPS - 1 : TAPS]
        for d in range(1, TAPS):
            pre = pre + jnp.where(keeps[d - 1], win[8 - d : 8 - d + BLK], 0.0) * weight[TAPS - 1 - d : TAPS - d]
        sg = 0.5 * jnp.tanh(0.5 * pre) + 0.5
        val = pre * sg
        return val, sg + val * (1.0 - sg)

    def forward(c, carry):
        base = pl.multiple_of(c * BLK, BLK)
        edge_x, edge_bc = carry
        x = r_ref[c, 0:BLK].astype(F32)
        bc_raw = r_ref[c, 2 * BLK : 3 * BLK].astype(F32)
        pos = base + ii
        start = start_at(pos, bounds)
        last_start = start_at(base + BLK - 1, bounds)
        tails = pos >= last_start
        dist = pos - start
        keeps = [twice(dist >= d) for d in range(1, TAPS)]
        xs, dsx = conv(edge_x, x, wx, keeps)
        bc, dsbc = conv(edge_bc, bc_raw, wbc, keeps)
        xs_s[c] = xs
        dsx_s[c] = dsx
        dsbc_s[c] = dsbc
        b = bc[:, :128]
        cc = bc[:, 128:]
        b_s[c] = b.astype(BF16)
        c_s[c] = cc.astype(BF16)
        bm = jnp.where(tails, b, 0.0).astype(BF16)
        bm_s[c] = bm
        cm_s[c] = jnp.where(start < base, cc, 0.0).astype(BF16)
        u = dot_tn(cols_s[c].astype(BF16), spread[:, :256])
        u_s[c] = u
        xp = (xs * u).astype(BF16)
        xp_s[c] = xp
        elt = elt_s[c][0:1]
        keep = jnp.where(last_start < base, elt, 0.0)
        st_s[c + 1] = keep * st_s[c] + elt * dot_tn(bm, xp)
        return x[BLK - 8 :], bc_raw[BLK - 8 :]

    lax.fori_loop(0, blocks, forward, (edge, edge), unroll=UNROLL)

    ds_s[...] = jnp.zeros((128, 256), F32)
    tapx_s[...] = jnp.zeros((TAPS, 8, 256), F32)
    tapbc_s[...] = jnp.zeros((TAPS, 8, 256), F32)
    lane2 = lax.broadcasted_iota(jnp.int32, (16, 256), 1)
    row2 = lax.broadcasted_iota(jnp.int32, (16, 256), 0)
    pick = (lane2 // 128 == row2).astype(BF16)

    def head_sums(out, c, a):
        sums = dot_nt(pick, a.astype(BF16))
        out[pl.ds(c, 1)] = sums[0:1]
        out[pl.ds(blocks + c, 1)] = sums[1:2]

    def conv_back(grad, edge, raw_in, weight, ends, taps):
        win = jnp.concatenate([grad, edge], axis=0)
        total_grad = grad * weight[TAPS - 1 : TAPS]
        taps[TAPS - 1] += fold_rows(grad * raw_in)
        for d in range(1, TAPS):
            moved = jnp.where(ends[d - 1], win[d : d + BLK], 0.0)
            total_grad = total_grad + moved * weight[TAPS - 1 - d : TAPS - d]
            taps[TAPS - 1 - d] += fold_rows(moved * raw_in)
        return total_grad

    def backward(lap, carry):
        c = blocks - 1 - lap
        base = pl.multiple_of(c * BLK, BLK)
        pos = base + ii
        start = start_at(pos, bounds)
        last_start = start_at(base + BLK - 1, bounds)
        causal = (jj <= ii) & (base + jj >= start)
        leads = start < base
        tails = pos >= last_start
        b = b_s[c]
        cc = c_s[c]
        xp = xp_s[c]
        cm = cm_s[c]
        gv = r_ref[c, BLK : 2 * BLK].astype(F32) * dot_tn(cols_s[c].astype(BF16), spread[:, 256:])
        gp = gv.astype(BF16)
        elt = elt_s[c][0:1]
        ds = ds_s[...]
        es_s[pl.ds(pl.multiple_of(c * 8, 8), 8)] = fold_rows(ds * st_s[c + 1])
        sb = st_s[c].astype(BF16)
        ds_e = elt * ds
        dsb = ds_e.astype(BF16)
        ds_s[...] = jnp.where(last_start < base, ds_e, 0.0) + dot_tn(cm, gp)
        w = jnp.where(causal, dot_nt(cc, b), 0.0).astype(BF16)
        yv = dot_nn(w, xp) + dot_nn(cm, sb)
        dxp = dot_tn(w, gp) + dot_nn(bm_s[c], dsb)
        z = jnp.where(causal, dot_nt(gp, xp), 0.0).astype(BF16)
        dc = dot_nn(z, b) + jnp.where(leads, dot_nt(gp, sb), 0.0)
        db = dot_tn(z, cc) + jnp.where(tails, dot_nt(xp, dsb), 0.0)
        dx = u_s[c] * dxp
        head_sums(x2_s, c, xs_s[c] * dx)
        head_sums(y2_s, c, gv * yv)
        left = next_start(pos, bounds, total) - pos
        ends = [twice(left > d) for d in range(1, TAPS)]
        edge_x, edge_bc = carry
        pre_x = dx * dsx_s[c]
        pre_bc = jnp.concatenate([db, dc], axis=1) * dsbc_s[c]
        x = r_ref[c, 0:BLK].astype(F32)
        bc_raw = r_ref[c, 2 * BLK : 3 * BLK].astype(F32)
        out_ref[c, 0:BLK] = conv_back(pre_x, edge_x, x, wx, ends, tapx_s).astype(BF16)
        out_ref[c, BLK : 2 * BLK] = conv_back(
            pre_bc, edge_bc, bc_raw, wbc, ends, tapbc_s
        ).astype(BF16)
        return pre_x[0:8], pre_bc[0:8]

    lax.fori_loop(0, blocks, backward, (edge, edge), unroll=UNROLL)

    xdx = x2_s[...]
    carry_sum = jnp.sum(es_s[...].reshape(blocks, 8, 256), axis=1)
    carry_sum = jnp.concatenate([carry_sum[:, :128], carry_sum[:, 128:]], axis=0)
    d_log = dot_exact(y2_s[...] - xdx, (ii >= jj).astype(F32))
    d_log = d_log + jnp.sum(carry_sum, axis=1, keepdims=True)
    d_raw = (xdx / step - rate * d_log) * sig
    d_raw = jnp.concatenate([d_raw[:blocks], d_raw[blocks:]], axis=1)
    raw_hi = d_raw.astype(BF16).astype(F32)
    raw_lo = d_raw - raw_hi
    tapx = jnp.concatenate([jnp.sum(tapx_s[k], axis=0, keepdims=True) for k in range(TAPS)], axis=0)
    tapbc = jnp.concatenate([jnp.sum(tapbc_s[k], axis=0, keepdims=True) for k in range(TAPS)], axis=0)
    tapx_hi = tapx.astype(BF16).astype(F32)
    rest = jnp.concatenate([tapx_hi, tapx - tapx_hi, tapbc, jnp.zeros((2, 256), F32)], axis=0)
    for c in range(blocks):
        out_ref[c, 2 * BLK : 2 * BLK + 16] = jnp.concatenate(
            [raw_hi[c : c + 1], raw_lo[c : c + 1], rest], axis=0
        ).astype(BF16)


def ssm_core(doc_lengths, place, rate, received, weight_x, weight_bc):
    blocks = received.shape[0]
    smem = pl.BlockSpec(memory_space=pltpu.SMEM)
    vmem = pl.BlockSpec(memory_space=pltpu.VMEM)

    def scratch(*shape, dtype=F32):
        return pltpu.VMEM(shape, dtype)

    return pl.pallas_call(
        ssm_kernel,
        out_shape=jax.ShapeDtypeStruct((blocks, 2 * BLK + 16, 256), BF16),
        in_specs=[smem, smem, smem, vmem, vmem, vmem],
        out_specs=vmem,
        scratch_shapes=[
            scratch(blocks, BLK, 256),
            scratch(blocks, BLK, 256, dtype=BF16),
            scratch(blocks, BLK, 256),
            scratch(blocks, BLK, 128, dtype=BF16),
            scratch(blocks, BLK, 128, dtype=BF16),
            scratch(blocks, BLK, 128, dtype=BF16),
            scratch(blocks, BLK, 128, dtype=BF16),
            scratch(blocks, BLK, 256),
            scratch(blocks, BLK, 256),
            scratch(blocks + 1, 128, 256),
            scratch(128, 256),
            scratch(blocks, 8, 128),
            scratch(blocks, 8, 256),
            scratch(2 * blocks, 128),
            scratch(2 * blocks, 128),
            scratch(8 * blocks, 256),
            scratch(TAPS, 8, 256),
            scratch(TAPS, 8, 256),
        ],
        compiler_params=pltpu.CompilerParams(vmem_limit_bytes=24 * 2**20),
        cost_estimate=pl.CostEstimate(flops=3 * 10**9, bytes_accessed=6 * 2**20, transcendentals=4 * 10**6),
        name="mixer",
    )(doc_lengths, place, rate, received, weight_x, weight_bc)


def attention_kernel(
    doc_ref, idx_ref, q_ref, do_ref, got_q_ref, got_do_ref, kv_ref,
    dq_own, dq_sent, d0, d1, d2, d3, d4, kt_s, dk_s, dv_s, s_s, p_s,
):
    d_refs = (d4, d3, d2, d1, d0)
    count = 2 * len(d_refs)
    bounds = doc_bounds(doc_ref)
    scale = HD ** (-0.5)
    place = idx_ref[0]
    odd = lax.rem(place, 2)
    base = (place - odd) * BLK
    jrow = lax.broadcasted_iota(jnp.int32, (BLK, 2 * BLK), 0)
    icol = lax.broadcasted_iota(jnp.int32, (BLK, 2 * BLK), 1)
    start = start_at(base + icol[0:1], bounds) - base
    heads = got_q_ref.shape[1] // HD

    def rows8(a):
        return a.reshape(BLK // 8, 8, 2 * BLK)

    def half(b):
        return slice((b % 2) * BLK, (b % 2 + 1) * BLK)

    def key_rows(b):
        return kv_ref[jnp.maximum(place - odd - BACK + b, 0), :, 0:HD]

    def value_rows(b):
        return kv_ref[jnp.maximum(place - odd - BACK + b, 0), :, HD : 2 * HD]

    def in_order(own, other):
        first = jnp.where(odd == 0, own, other)
        second = jnp.where(odd == 0, other, own)
        return jnp.concatenate([first, second], axis=0)

    for b in range(count):
        kt_s[b] = key_rows(b).T
    dk_s[...] = jnp.zeros(dk_s.shape, F32)
    dv_s[...] = jnp.zeros(dv_s.shape, F32)

    def turn(head, carry):
        at = pl.multiple_of(head * HD, HD)
        own_at = pl.multiple_of((odd * heads + head) * HD, HD)
        q = in_order(q_ref[:, pl.ds(own_at, HD)], got_q_ref[:, pl.ds(at, HD)])
        do = in_order(
            do_ref[:, pl.ds(own_at, HD)], got_do_ref[:, pl.ds(at, HD)]
        )
        top = jnp.full((8, 2 * BLK), NEG_BIG, F32)
        for b in range(count):
            allowed = jrow >= start + (BACK - b) * BLK
            if b >= BACK:
                allowed = allowed & (jrow + (b - BACK) * BLK <= icol)
            s = jnp.where(allowed, dot_nt(key_rows(b), q), NEG_BIG)
            s_s[b] = s
            top = jnp.maximum(top, jnp.max(rows8(s), axis=0))
            p_s[b] = dot_nt(value_rows(b), do)
        top = jnp.max(top, axis=0, keepdims=True) * (scale * LOG2E)
        norm = jnp.zeros((8, 2 * BLK), F32)
        mean = jnp.zeros((8, 2 * BLK), F32)
        for b in range(count):
            e = jnp.exp2(s_s[b] * (scale * LOG2E) - top)
            s_s[b] = e
            norm = norm + jnp.sum(rows8(e), axis=0)
            mean = mean + jnp.sum(rows8(e * p_s[b]), axis=0)
        inverse = 1.0 / jnp.sum(norm, axis=0, keepdims=True)
        mean = jnp.sum(mean, axis=0, keepdims=True) * inverse
        dqt = jnp.zeros((HD, 2 * BLK), F32)
        for b in range(count):
            prob = s_s[b] * inverse
            grad = (prob * (p_s[b] - mean)).astype(BF16)
            dv_s[b] += dot_nn(prob.astype(BF16), do)
            dk_s[b] += dot_nn(grad, q)
            dqt = dqt + dot_nn(kt_s[b], grad)
        dqt = dqt * scale
        first = dqt[:, :BLK].T
        second = dqt[:, BLK:].T
        dq_own[:, pl.ds(at, HD)] = jnp.where(odd == 0, first, second).astype(BF16)
        dq_sent[:, pl.ds(at, HD)] = jnp.where(odd == 0, second, first).astype(BF16)
        return carry

    lax.fori_loop(0, heads, turn, 0)
    for b in range(count):
        out = d_refs[b // 2]
        out[half(b), 0:HD] = (dk_s[b] * scale).astype(out.dtype)
        out[half(b), HD : 2 * HD] = dv_s[b].astype(out.dtype)


def attention_core(doc_lengths, place, query, d_out, got_q, got_do, kv):
    smem = pl.BlockSpec(memory_space=pltpu.SMEM)
    vmem = pl.BlockSpec(memory_space=pltpu.VMEM)
    pairs = BACK // 2 + 1
    count = 2 * pairs
    rows, width = query.shape
    part = jax.ShapeDtypeStruct((rows, width // 2), BF16)
    kv_shape = (2 * rows, 2 * HD)
    outs = [part, part, jax.ShapeDtypeStruct(kv_shape, F32)]
    outs += [jax.ShapeDtypeStruct(kv_shape, BF16)] * (pairs - 1)
    return pl.pallas_call(
        attention_kernel,
        out_shape=outs,
        in_specs=[smem, smem] + [vmem] * 5,
        out_specs=[vmem] * (2 + pairs),
        scratch_shapes=[
            pltpu.VMEM((count, HD, BLK), BF16),
            pltpu.VMEM((count, BLK, HD), F32),
            pltpu.VMEM((count, BLK, HD), F32),
            pltpu.VMEM((count, BLK, 2 * BLK), F32),
            pltpu.VMEM((count, BLK, 2 * BLK), F32),
        ],
        compiler_params=pltpu.CompilerParams(vmem_limit_bytes=16 * 2**20),
        cost_estimate=pl.CostEstimate(flops=4 * 10**9, bytes_accessed=4 * 2**20, transcendentals=3 * 10**6),
        name="attention",
    )(doc_lengths, place, query, d_out, got_q, got_do, kv)


def shift(a, by):
    devices = lax.axis_size("ctx")
    return lax.ppermute(
        a, "ctx", [(i, i + by) for i in range(devices) if 0 <= i + by < devices]
    )


def partner(a):
    return lax.ppermute(a, "ctx", [(i, i ^ 1) for i in range(lax.axis_size("ctx"))])


def pack_kernel(
    x_ref, g_ref, bc_ref, dt_ref, k_ref, v_ref, out_ref, kv_ref, buf, kv_buf, in_sems, out_sems, kv_sem
):
    blocks = out_ref.shape[0]
    loads = []
    for d in range(blocks):
        lanes = pl.ds(d * 2 * HD, 2 * HD)
        pair = [
            pltpu.make_async_copy(src, buf.at[d, pl.ds(at * BLK, BLK)], in_sems.at[2 * d + at])
            for at, src in enumerate((x_ref.at[:, lanes], g_ref.at[:, lanes]))
        ]
        for one in pair:
            one.start()
        loads.append(pair)
    b_all = bc_ref[:, 0, :]
    c_all = bc_ref[:, 1, :]
    bc = [
        jnp.concatenate([b_all[:, at : at + HD], c_all[:, at : at + HD]], axis=1) for at in (0, HD)
    ]
    for d in range(blocks):
        buf[d, 2 * BLK : 3 * BLK] = bc[d // (blocks // 2)]
        raw = jnp.concatenate([dt_ref[2 * d : 2 * d + 1], dt_ref[2 * d + 1 : 2 * d + 2]], axis=1)
        hi = raw.astype(BF16).astype(F32)
        mid = (raw - hi).astype(BF16).astype(F32)
        parts = [hi, mid, raw - hi - mid, jnp.zeros((13, 2 * BLK), F32)]
        buf[d, 3 * BLK : 3 * BLK + 16] = jnp.concatenate(parts, axis=0).astype(BF16)
        head = slice((d % 2) * HD, (d % 2 + 1) * HD)
        kv_buf[d] = jnp.concatenate([k_ref[:, head], v_ref[:, head]], axis=1)
    stores = []
    for d in range(blocks):
        for one in loads[d]:
            one.wait()
        stores.append(pltpu.make_async_copy(buf.at[d], out_ref.at[d], out_sems.at[d]))
        stores[-1].start()
    stores.append(pltpu.make_async_copy(kv_buf, kv_ref, kv_sem))
    stores[-1].start()
    for one in stores:
        one.wait()


def pack(x_in, grad, bc_sent, dt_raw, key, value, blocks):
    hbm = pl.BlockSpec(memory_space=pltpu.HBM)
    vmem = pl.BlockSpec(memory_space=pltpu.VMEM)
    return pl.pallas_call(
        pack_kernel,
        out_shape=[
            jax.ShapeDtypeStruct((blocks, 3 * BLK + 16, 2 * HD), BF16),
            jax.ShapeDtypeStruct((blocks, BLK, 2 * HD), BF16),
        ],
        in_specs=[hbm, hbm, vmem, vmem, vmem, vmem],
        out_specs=[hbm, hbm],
        scratch_shapes=[
            pltpu.VMEM((blocks, 3 * BLK + 16, 2 * HD), BF16),
            pltpu.VMEM((blocks, BLK, 2 * HD), BF16),
            pltpu.SemaphoreType.DMA((2 * blocks,)),
            pltpu.SemaphoreType.DMA((blocks,)),
            pltpu.SemaphoreType.DMA(()),
        ],
        cost_estimate=pl.CostEstimate(flops=0, bytes_accessed=7 * 2**20, transcendentals=0),
        name="pack",
    )(x_in, grad, bc_sent, dt_raw, key, value)


def unpack_kernel(
    idx_ref, part, dq_own, dq_got, own, dx_ref, dbc_ref, dt_ref, wx_ref, wbc_ref, dq_ref, passed, sems
):
    blocks = part.shape[0]
    half = blocks // 2
    copies = []
    for d in range(blocks):
        lanes = pl.ds(d * 2 * HD, 2 * HD)
        copies.append(pltpu.make_async_copy(part.at[d, pl.ds(0, BLK)], dx_ref.at[:, lanes], sems.at[d]))
        copies[-1].start()
    for group in range(2):
        at = [group * half + d for d in range(half)]
        total = part[at[0], BLK : 2 * BLK].astype(F32)
        taps = part[at[0], 2 * BLK : 2 * BLK + 16].astype(F32)
        for d in at[1:]:
            total = total + part[d, BLK : 2 * BLK].astype(F32)
            taps = taps + part[d, 2 * BLK : 2 * BLK + 16].astype(F32)
        for which in range(2):
            lanes = slice(which * HD, (which + 1) * HD)
            out = slice((2 * which + group) * HD, (2 * which + group + 1) * HD)
            dbc_ref[:, out] = total[:, lanes].astype(BF16)
            wbc_ref[:, which, group * HD : (group + 1) * HD] = taps[10:14, lanes]
    for d in range(blocks):
        small = part[d, 2 * BLK : 2 * BLK + 16].astype(F32)
        raw = small[0:1] + small[1:2]
        dt_ref[2 * d : 2 * d + 1] = raw[:, :BLK]
        dt_ref[2 * d + 1 : 2 * d + 2] = raw[:, BLK:]
        wx_ref[:, d * 2 * HD : (d + 1) * 2 * HD] = small[2:6] + small[6:10]
    odd = lax.rem(idx_ref[0], 2)
    a = dq_own[...]
    b = dq_got[...]
    dq_ref[:, : a.shape[1]] = jnp.where(odd == 0, a, b)
    dq_ref[:, a.shape[1] :] = jnp.where(odd == 0, b, a)
    for done in copies:
        done.wait()


def unpack(place, received, dq_own, dq_got, own):
    blocks = received.shape[0]
    hbm = pl.BlockSpec(memory_space=pltpu.HBM)
    vmem = pl.BlockSpec(memory_space=pltpu.VMEM)
    return pl.pallas_call(
        unpack_kernel,
        out_shape=[
            jax.ShapeDtypeStruct((BLK, blocks * 2 * HD), BF16),
            jax.ShapeDtypeStruct((BLK, 4 * HD), BF16),
            jax.ShapeDtypeStruct((2 * blocks, BLK), F32),
            jax.ShapeDtypeStruct((TAPS, blocks * 2 * HD), F32),
            jax.ShapeDtypeStruct((TAPS, 2, 2 * HD), F32),
            jax.ShapeDtypeStruct((BLK, 2 * dq_own.shape[1]), BF16),
            jax.ShapeDtypeStruct(own.shape, own.dtype),
        ],
        in_specs=[pl.BlockSpec(memory_space=pltpu.SMEM), vmem, vmem, vmem, pl.BlockSpec(memory_space=pl.ANY)],
        out_specs=[hbm, vmem, vmem, vmem, vmem, vmem, pl.BlockSpec(memory_space=pl.ANY)],
        input_output_aliases={4: 6},
        scratch_shapes=[pltpu.SemaphoreType.DMA((blocks,))],
        compiler_params=pltpu.CompilerParams(vmem_limit_bytes=8 * 2**20),
        cost_estimate=pl.CostEstimate(flops=10**6, bytes_accessed=4 * 2**20, transcendentals=0),
        name="unpack",
    )(place, received, dq_own, dq_got, own)


def kv_sum_kernel(idx_ref, own, r1, r2, r3, r4, mine, sent):
    total = own[...]
    for got in (r1, r2, r3, r4):
        total = total + got[...].astype(F32)
    rows = mine.shape[0]
    first = total[:rows].astype(BF16)
    second = total[rows:].astype(BF16)
    odd = lax.rem(idx_ref[0], 2)
    mine[...] = jnp.where(odd == 0, first, second)
    sent[...] = jnp.where(odd == 0, second, first)


def kv_total(place, own, received):
    vmem = pl.BlockSpec(memory_space=pltpu.VMEM)
    half = jax.ShapeDtypeStruct((own.shape[0] // 2, own.shape[1]), BF16)
    return pl.pallas_call(
        kv_sum_kernel,
        out_shape=[half, half],
        in_specs=[pl.BlockSpec(memory_space=pltpu.SMEM)]
        + [vmem] * (1 + len(received)),
        out_specs=[vmem, vmem],
        compiler_params=pltpu.CompilerParams(vmem_limit_bytes=4 * 2**20),
        name="kv_total",
    )(place, own, *received)


def kv_place_kernel(idx_ref, mine, other, dk_ref, dv_ref):
    odd = lax.rem(idx_ref[0], 2)
    a = mine[...]
    b = other[...]
    first = jnp.where(odd == 0, a, b)
    second = jnp.where(odd == 0, b, a)
    dk_ref[...] = jnp.concatenate([first[:, :HD], second[:, :HD]], axis=1)
    dv_ref[...] = jnp.concatenate([first[:, HD:], second[:, HD:]], axis=1)


def kv_place(place, mine, other):
    vmem = pl.BlockSpec(memory_space=pltpu.VMEM)
    return pl.pallas_call(
        kv_place_kernel,
        out_shape=[jax.ShapeDtypeStruct(mine.shape, BF16)] * 2,
        in_specs=[pl.BlockSpec(memory_space=pltpu.SMEM), vmem, vmem],
        out_specs=[vmem, vmem],
        compiler_params=pltpu.CompilerParams(vmem_limit_bytes=4 * 2**20),
        name="kv_place",
    )(place, mine, other)


def swap(a):
    return lax.all_to_all(a, "ctx", 0, 0, tiled=True)


def shards(
    x_in, bc_in, conv_x, conv_bc, dt_raw, rate, grad_ssd, query, key, value, d_out, doc_lengths
):
    ctx = lax.axis_size("ctx")
    rows = x_in.shape[0]
    place = lax.axis_index("ctx").astype(jnp.int32).reshape(1)

    odd = place[0] % 2

    def half(a, which):
        return lax.dynamic_slice_in_dim(a, which * (a.shape[1] // 2), a.shape[1] // 2, 1)

    def pick(own, other):
        return jnp.where(odd == 0, own, other), jnp.where(odd == 0, other, own)

    packed, kv_sent = pack(x_in, grad_ssd, bc_in, dt_raw, key, value, ctx)
    got = swap(packed)
    got, kv_sent = lax.optimization_barrier((got, kv_sent))
    kv = swap(kv_sent)
    got_q = partner(half(query, 1 - odd))
    got_do = partner(half(d_out, 1 - odd))
    mixed = ssm_core(doc_lengths, place, rate, got, conv_x, conv_bc)
    mixed, kv, got_q, got_do = lax.optimization_barrier((mixed, kv, got_q, got_do))
    back = swap(mixed)
    dq_own, dq_sent, *d_kv = attention_core(doc_lengths, place, query, d_out, got_q, got_do, kv)
    received = [shift(d_kv[by], -2 * by) for by in range(1, BACK // 2 + 1)]
    d_x, d_bc, d_dt, d_wx, d_wbc, d_query, own = unpack(
        place, back, dq_own, partner(dq_sent), d_kv[0]
    )
    mine, sent = kv_total(place, own, received)
    d_key, d_value = kv_place(place, mine, partner(sent))
    return (
        d_x,
        d_bc.reshape(rows, 2, 2 * HD),
        d_dt,
        d_wx,
        d_wbc,
        d_query,
        d_key,
        d_value,
    )


def solution(mesh):
    tokens = P(("dp", "ctx"), "head")
    in_specs = (
        tokens,
        P(("dp", "ctx"), None, "head"),
        P(None, "head"),
        P(None, None, "head"),
        P("head", ("dp", "ctx")),
        P("head"),
        tokens,
        tokens,
        tokens,
        tokens,
        tokens,
        P("dp"),
    )
    out_specs = (
        tokens,
        P(("dp", "ctx"), None, "head"),
        P("head", ("dp", "ctx")),
        P("dp", "head"),
        P("dp", None, "head"),
        tokens,
        tokens,
        tokens,
    )
    return jax.shard_map(shards, mesh=mesh, in_specs=in_specs, out_specs=out_specs, check_vma=False)
```

```python
import jax
import jax.numpy as jnp
from jax import lax
from jax.experimental import pallas as pl
from jax.experimental.pallas import tpu as pltpu
from jax.sharding import PartitionSpec as P

F32 = jnp.float32
BF16 = jnp.bfloat16
HD = 128
BLK = 128
TAPS = 4
BACK = 8
LOG2E = 1.4426950408889634
NEG_BIG = -1e30
UNROLL = 8


def dot_nn(a, b):
    return lax.dot_general(a, b, (((1,), (0,)), ((), ())), preferred_element_type=F32)


def dot_nt(a, b):
    return lax.dot_general(a, b, (((1,), (1,)), ((), ())), preferred_element_type=F32)


def dot_tn(a, b):
    return lax.dot_general(a, b, (((0,), (0,)), ((), ())), preferred_element_type=F32)


def doc_bounds(doc_ref):
    s1 = doc_ref[0]
    s2 = s1 + doc_ref[1]
    s3 = s2 + doc_ref[2]
    return s1, s2, s3


def start_at(pos, bounds):
    s1, s2, s3 = bounds
    return jnp.where(pos >= s3, s3, jnp.where(pos >= s2, s2, jnp.where(pos >= s1, s1, 0)))


def next_start(pos, bounds, total):
    s1, s2, s3 = bounds
    return jnp.where(pos < s1, s1, jnp.where(pos < s2, s2, jnp.where(pos < s3, s3, total)))


def twice(a):
    return jnp.concatenate([a, a], axis=1)


def fold_rows(a):
    return jnp.sum(a.reshape(a.shape[0] // 8, 8, a.shape[1]), axis=0)


def split3(a):
    hi = a.astype(BF16)
    rest = a - hi.astype(F32)
    mid = rest.astype(BF16)
    return hi, mid, (rest - mid.astype(F32)).astype(BF16)


def dot_exact(a, ones):
    rows = a.shape[0]
    out = dot_nn(jnp.concatenate(split3(a), axis=0), ones.astype(BF16))
    return out[:rows] + out[rows : 2 * rows] + out[2 * rows :]


def ssm_kernel(
    doc_ref, idx_ref, rate_ref, r_ref, wx_ref, wbc_ref, out_ref,
    xs_s, xp_s, u_s, b_s, c_s, bm_s, cm_s, dsx_s, dsbc_s, st_s, ds_s,
    cols_s, elt_s, x2_s, y2_s, es_s, tapx_s, tapbc_s,
):
    blocks = r_ref.shape[0]
    total = blocks * BLK
    place = idx_ref[0]
    bounds = doc_bounds(doc_ref)
    rate0 = rate_ref[2 * place]
    rate1 = rate_ref[2 * place + 1]
    group = place // (blocks // 2)
    wx = wx_ref[:, pl.ds(pl.multiple_of(place * 256, 256), 256)]
    wbc = jnp.concatenate(
        [
            wbc_ref[:, 0, pl.ds(pl.multiple_of(group * 128, 128), 128)],
            wbc_ref[:, 1, pl.ds(pl.multiple_of(group * 128, 128), 128)],
        ],
        axis=1,
    )

    for c in range(blocks):
        row = jnp.sum(r_ref[c, 3 * BLK : 3 * BLK + 16, :].astype(F32), axis=0, keepdims=True)
        x2_s[c : c + 1] = row[:, :128]
        x2_s[blocks + c : blocks + c + 1] = row[:, 128:]
    raw = x2_s[...]
    step = jnp.log(1.0 + jnp.exp(raw))
    sig = 1.0 / (1.0 + jnp.exp(-raw))
    row_ids = lax.broadcasted_iota(jnp.int32, (2 * blocks, 128), 0)
    rate = jnp.where(row_ids < blocks, rate0, rate1)
    ii = lax.broadcasted_iota(jnp.int32, (128, 128), 0)
    jj = lax.broadcasted_iota(jnp.int32, (128, 128), 1)
    cum = dot_exact(-step * rate, (ii <= jj).astype(F32))
    v_rows = jnp.exp(cum)
    u_hi, u_lo, _ = split3(step * jnp.exp(-cum))
    v_hi, v_lo, _ = split3(v_rows)
    last = jnp.broadcast_to(v_rows[:, 127:128], (2 * blocks, 128))
    pieces = [a.astype(F32) for a in (u_hi, u_lo, v_hi, v_lo)]
    for c in range(blocks):
        rows = [a[at : at + 1] for a in pieces for at in (c, blocks + c)]
        cols_s[c] = jnp.concatenate(rows, axis=0)
        elt_s[c] = jnp.broadcast_to(
            jnp.concatenate([last[c : c + 1], last[blocks + c : blocks + c + 1]], axis=1), (8, 256)
        )
    row8 = lax.broadcasted_iota(jnp.int32, (8, 512), 0)
    lane8 = lax.broadcasted_iota(jnp.int32, (8, 512), 1) // 128
    spread = ((lane8 // 2 == row8 // 4) & (lane8 % 2 == row8 % 2)).astype(BF16)

    edge = jnp.zeros((8, 256), F32)
    st_s[0] = jnp.zeros((128, 256), F32)

    def conv(edge, value, weight, keeps):
        win = jnp.concatenate([edge, value], axis=0)
        pre = value * weight[TAPS - 1 : TAPS]
        for d in range(1, TAPS):
            pre = pre + jnp.where(keeps[d - 1], win[8 - d : 8 - d + BLK], 0.0) * weight[TAPS - 1 - d : TAPS - d]
        sg = 0.5 * jnp.tanh(0.5 * pre) + 0.5
        val = pre * sg
        return val, sg + val * (1.0 - sg)

    def forward(c, carry):
        base = pl.multiple_of(c * BLK, BLK)
        edge_x, edge_bc = carry
        x = r_ref[c, 0:BLK].astype(F32)
        bc_raw = r_ref[c, 2 * BLK : 3 * BLK].astype(F32)
        pos = base + ii
        start = start_at(pos, bounds)
        last_start = start_at(base + BLK - 1, bounds)
        tails = pos >= last_start
        dist = pos - start
        keeps = [twice(dist >= d) for d in range(1, TAPS)]
        xs, dsx = conv(edge_x, x, wx, keeps)
        bc, dsbc = conv(edge_bc, bc_raw, wbc, keeps)
        xs_s[c] = xs
        dsx_s[c] = dsx
        dsbc_s[c] = dsbc
        b = bc[:, :128]
        cc = bc[:, 128:]
        b_s[c] = b.astype(BF16)
        c_s[c] = cc.astype(BF16)
        bm = jnp.where(tails, b, 0.0).astype(BF16)
        bm_s[c] = bm
        cm_s[c] = jnp.where(start < base, cc, 0.0).astype(BF16)
        u = dot_tn(cols_s[c].astype(BF16), spread[:, :256])
        u_s[c] = u
        xp = (xs * u).astype(BF16)
        xp_s[c] = xp
        elt = elt_s[c][0:1]
        keep = jnp.where(last_start < base, elt, 0.0)
        st_s[c + 1] = keep * st_s[c] + elt * dot_tn(bm, xp)
        return x[BLK - 8 :], bc_raw[BLK - 8 :]

    lax.fori_loop(0, blocks, forward, (edge, edge), unroll=UNROLL)

    ds_s[...] = jnp.zeros((128, 256), F32)
    tapx_s[...] = jnp.zeros((TAPS, 8, 256), F32)
    tapbc_s[...] = jnp.zeros((TAPS, 8, 256), F32)
    lane2 = lax.broadcasted_iota(jnp.int32, (16, 256), 1)
    row2 = lax.broadcasted_iota(jnp.int32, (16, 256), 0)
    pick = (lane2 // 128 == row2).astype(BF16)

    def head_sums(out, c, a):
        sums = dot_nt(pick, a.astype(BF16))
        out[pl.ds(c, 1)] = sums[0:1]
        out[pl.ds(blocks + c, 1)] = sums[1:2]

    def conv_back(grad, edge, raw_in, weight, ends, taps):
        win = jnp.concatenate([grad, edge], axis=0)
        total_grad = grad * weight[TAPS - 1 : TAPS]
        taps[TAPS - 1] += fold_rows(grad * raw_in)
        for d in range(1, TAPS):
            moved = jnp.where(ends[d - 1], win[d : d + BLK], 0.0)
            total_grad = total_grad + moved * weight[TAPS - 1 - d : TAPS - d]
            taps[TAPS - 1 - d] += fold_rows(moved * raw_in)
        return total_grad

    def backward(lap, carry):
        c = blocks - 1 - lap
        base = pl.multiple_of(c * BLK, BLK)
        pos = base + ii
        start = start_at(pos, bounds)
        last_start = start_at(base + BLK - 1, bounds)
        causal = (jj <= ii) & (base + jj >= start)
        leads = start < base
        tails = pos >= last_start
        b = b_s[c]
        cc = c_s[c]
        xp = xp_s[c]
        cm = cm_s[c]
        gv = r_ref[c, BLK : 2 * BLK].astype(F32) * dot_tn(cols_s[c].astype(BF16), spread[:, 256:])
        gp = gv.astype(BF16)
        elt = elt_s[c][0:1]
        ds = ds_s[...]
        es_s[pl.ds(pl.multiple_of(c * 8, 8), 8)] = fold_rows(ds * st_s[c + 1])
        sb = st_s[c].astype(BF16)
        ds_e = elt * ds
        dsb = ds_e.astype(BF16)
        ds_s[...] = jnp.where(last_start < base, ds_e, 0.0) + dot_tn(cm, gp)
        w = jnp.where(causal, dot_nt(cc, b), 0.0).astype(BF16)
        yv = dot_nn(w, xp) + dot_nn(cm, sb)
        dxp = dot_tn(w, gp) + dot_nn(bm_s[c], dsb)
        z = jnp.where(causal, dot_nt(gp, xp), 0.0).astype(BF16)
        dc = dot_nn(z, b) + jnp.where(leads, dot_nt(gp, sb), 0.0)
        db = dot_tn(z, cc) + jnp.where(tails, dot_nt(xp, dsb), 0.0)
        dx = u_s[c] * dxp
        head_sums(x2_s, c, xs_s[c] * dx)
        head_sums(y2_s, c, gv * yv)
        left = next_start(pos, bounds, total) - pos
        ends = [twice(left > d) for d in range(1, TAPS)]
        edge_x, edge_bc = carry
        pre_x = dx * dsx_s[c]
        pre_bc = jnp.concatenate([db, dc], axis=1) * dsbc_s[c]
        x = r_ref[c, 0:BLK].astype(F32)
        bc_raw = r_ref[c, 2 * BLK : 3 * BLK].astype(F32)
        out_ref[c, 0:BLK] = conv_back(pre_x, edge_x, x, wx, ends, tapx_s).astype(BF16)
        out_ref[c, BLK : 2 * BLK] = conv_back(
            pre_bc, edge_bc, bc_raw, wbc, ends, tapbc_s
        ).astype(BF16)
        return pre_x[0:8], pre_bc[0:8]

    lax.fori_loop(0, blocks, backward, (edge, edge), unroll=UNROLL)

    xdx = x2_s[...]
    carry_sum = jnp.sum(es_s[...].reshape(blocks, 8, 256), axis=1)
    carry_sum = jnp.concatenate([carry_sum[:, :128], carry_sum[:, 128:]], axis=0)
    d_log = dot_exact(y2_s[...] - xdx, (ii >= jj).astype(F32))
    d_log = d_log + jnp.sum(carry_sum, axis=1, keepdims=True)
    d_raw = (xdx / step - rate * d_log) * sig
    d_raw = jnp.concatenate([d_raw[:blocks], d_raw[blocks:]], axis=1)
    raw_hi = d_raw.astype(BF16).astype(F32)
    raw_lo = d_raw - raw_hi
    tapx = jnp.concatenate([jnp.sum(tapx_s[k], axis=0, keepdims=True) for k in range(TAPS)], axis=0)
    tapbc = jnp.concatenate([jnp.sum(tapbc_s[k], axis=0, keepdims=True) for k in range(TAPS)], axis=0)
    tapx_hi = tapx.astype(BF16).astype(F32)
    rest = jnp.concatenate([tapx_hi, tapx - tapx_hi, tapbc, jnp.zeros((2, 256), F32)], axis=0)
    for c in range(blocks):
        out_ref[c, 2 * BLK : 2 * BLK + 16] = jnp.concatenate(
            [raw_hi[c : c + 1], raw_lo[c : c + 1], rest], axis=0
        ).astype(BF16)


def ssm_core(doc_lengths, place, rate, received, weight_x, weight_bc):
    blocks = received.shape[0]
    smem = pl.BlockSpec(memory_space=pltpu.SMEM)
    vmem = pl.BlockSpec(memory_space=pltpu.VMEM)

    def scratch(*shape, dtype=F32):
        return pltpu.VMEM(shape, dtype)

    return pl.pallas_call(
        ssm_kernel,
        out_shape=jax.ShapeDtypeStruct((blocks, 2 * BLK + 16, 256), BF16),
        in_specs=[smem, smem, smem, vmem, vmem, vmem],
        out_specs=vmem,
        scratch_shapes=[
            scratch(blocks, BLK, 256),
            scratch(blocks, BLK, 256, dtype=BF16),
            scratch(blocks, BLK, 256),
            scratch(blocks, BLK, 128, dtype=BF16),
            scratch(blocks, BLK, 128, dtype=BF16),
            scratch(blocks, BLK, 128, dtype=BF16),
            scratch(blocks, BLK, 128, dtype=BF16),
            scratch(blocks, BLK, 256),
            scratch(blocks, BLK, 256),
            scratch(blocks + 1, 128, 256),
            scratch(128, 256),
            scratch(blocks, 8, 128),
            scratch(blocks, 8, 256),
            scratch(2 * blocks, 128),
            scratch(2 * blocks, 128),
            scratch(8 * blocks, 256),
            scratch(TAPS, 8, 256),
            scratch(TAPS, 8, 256),
        ],
        compiler_params=pltpu.CompilerParams(vmem_limit_bytes=24 * 2**20),
        cost_estimate=pl.CostEstimate(flops=3 * 10**9, bytes_accessed=6 * 2**20, transcendentals=4 * 10**6),
        name="mixer",
    )(doc_lengths, place, rate, received, weight_x, weight_bc)


def attention_kernel(
    doc_ref, idx_ref, q_ref, do_ref, got_q_ref, got_do_ref, kv_ref,
    dq_own, dq_sent, d0, d1, d2, d3, d4, kt_s, dk_s, dv_s, s_s, p_s,
):
    d_refs = (d4, d3, d2, d1, d0)
    count = 2 * len(d_refs)
    bounds = doc_bounds(doc_ref)
    scale = HD ** (-0.5)
    place = idx_ref[0]
    odd = lax.rem(place, 2)
    base = (place - odd) * BLK
    jrow = lax.broadcasted_iota(jnp.int32, (BLK, 2 * BLK), 0)
    icol = lax.broadcasted_iota(jnp.int32, (BLK, 2 * BLK), 1)
    start = start_at(base + icol[0:1], bounds) - base
    heads = got_q_ref.shape[1] // HD

    def rows8(a):
        return a.reshape(BLK // 8, 8, 2 * BLK)

    def half(b):
        return slice((b % 2) * BLK, (b % 2 + 1) * BLK)

    def key_rows(b):
        return kv_ref[jnp.maximum(place - odd - BACK + b, 0), :, 0:HD]

    def value_rows(b):
        return kv_ref[jnp.maximum(place - odd - BACK + b, 0), :, HD : 2 * HD]

    def in_order(own, other):
        first = jnp.where(odd == 0, own, other)
        second = jnp.where(odd == 0, other, own)
        return jnp.concatenate([first, second], axis=0)

    for b in range(count):
        kt_s[b] = key_rows(b).T
    dk_s[...] = jnp.zeros(dk_s.shape, F32)
    dv_s[...] = jnp.zeros(dv_s.shape, F32)

    def turn(head, carry):
        at = pl.multiple_of(head * HD, HD)
        own_at = pl.multiple_of((odd * heads + head) * HD, HD)
        q = in_order(q_ref[:, pl.ds(own_at, HD)], got_q_ref[:, pl.ds(at, HD)])
        do = in_order(
            do_ref[:, pl.ds(own_at, HD)], got_do_ref[:, pl.ds(at, HD)]
        )
        top = jnp.full((8, 2 * BLK), NEG_BIG, F32)
        for b in range(count):
            allowed = jrow >= start + (BACK - b) * BLK
            if b >= BACK:
                allowed = allowed & (jrow + (b - BACK) * BLK <= icol)
            s = jnp.where(allowed, dot_nt(key_rows(b), q), NEG_BIG)
            s_s[b] = s
            top = jnp.maximum(top, jnp.max(rows8(s), axis=0))
            p_s[b] = dot_nt(value_rows(b), do)
        top = jnp.max(top, axis=0, keepdims=True) * (scale * LOG2E)
        norm = jnp.zeros((8, 2 * BLK), F32)
        mean = jnp.zeros((8, 2 * BLK), F32)
        for b in range(count):
            e = jnp.exp2(s_s[b] * (scale * LOG2E) - top)
            s_s[b] = e
            norm = norm + jnp.sum(rows8(e), axis=0)
            mean = mean + jnp.sum(rows8(e * p_s[b]), axis=0)
        inverse = 1.0 / jnp.sum(norm, axis=0, keepdims=True)
        mean = jnp.sum(mean, axis=0, keepdims=True) * inverse
        dqt = jnp.zeros((HD, 2 * BLK), F32)
        for b in range(count):
            prob = s_s[b] * inverse
            grad = (prob * (p_s[b] - mean)).astype(BF16)
            dv_s[b] += dot_nn(prob.astype(BF16), do)
            dk_s[b] += dot_nn(grad, q)
            dqt = dqt + dot_nn(kt_s[b], grad)
        dqt = dqt * scale
        first = dqt[:, :BLK].T
        second = dqt[:, BLK:].T
        dq_own[:, pl.ds(at, HD)] = jnp.where(odd == 0, first, second).astype(BF16)
        dq_sent[:, pl.ds(at, HD)] = jnp.where(odd == 0, second, first).astype(BF16)
        return carry

    lax.fori_loop(0, heads, turn, 0)
    for b in range(count):
        out = d_refs[b // 2]
        out[half(b), 0:HD] = (dk_s[b] * scale).astype(out.dtype)
        out[half(b), HD : 2 * HD] = dv_s[b].astype(out.dtype)


def attention_core(doc_lengths, place, query, d_out, got_q, got_do, kv):
    smem = pl.BlockSpec(memory_space=pltpu.SMEM)
    vmem = pl.BlockSpec(memory_space=pltpu.VMEM)
    pairs = BACK // 2 + 1
    count = 2 * pairs
    rows, width = query.shape
    part = jax.ShapeDtypeStruct((rows, width // 2), BF16)
    kv_shape = (2 * rows, 2 * HD)
    outs = [part, part, jax.ShapeDtypeStruct(kv_shape, F32)]
    outs += [jax.ShapeDtypeStruct(kv_shape, BF16)] * (pairs - 1)
    return pl.pallas_call(
        attention_kernel,
        out_shape=outs,
        in_specs=[smem, smem] + [vmem] * 5,
        out_specs=[vmem] * (2 + pairs),
        scratch_shapes=[
            pltpu.VMEM((count, HD, BLK), BF16),
            pltpu.VMEM((count, BLK, HD), F32),
            pltpu.VMEM((count, BLK, HD), F32),
            pltpu.VMEM((count, BLK, 2 * BLK), F32),
            pltpu.VMEM((count, BLK, 2 * BLK), F32),
        ],
        compiler_params=pltpu.CompilerParams(vmem_limit_bytes=16 * 2**20),
        cost_estimate=pl.CostEstimate(flops=4 * 10**9, bytes_accessed=4 * 2**20, transcendentals=3 * 10**6),
        name="attention",
    )(doc_lengths, place, query, d_out, got_q, got_do, kv)


def shift(a, by):
    devices = lax.axis_size("ctx")
    return lax.ppermute(
        a, "ctx", [(i, i + by) for i in range(devices) if 0 <= i + by < devices]
    )


def partner(a):
    return lax.ppermute(a, "ctx", [(i, i ^ 1) for i in range(lax.axis_size("ctx"))])


def pack_kernel(
    idx_ref, x_ref, g_ref, bc_ref, dt_ref, k_ref, v_ref, q_ref, do_ref, out_ref, kv_ref, qs_ref, dos_ref,
    buf, kv_buf, qo_buf, in_sems, out_sems, kv_sem, qo_sems,
):
    blocks = out_ref.shape[0]
    loads = []
    for d in range(blocks):
        lanes = pl.ds(d * 2 * HD, 2 * HD)
        pair = [
            pltpu.make_async_copy(src, buf.at[d, pl.ds(at * BLK, BLK)], in_sems.at[2 * d + at])
            for at, src in enumerate((x_ref.at[:, lanes], g_ref.at[:, lanes]))
        ]
        for one in pair:
            one.start()
        loads.append(pair)
    half = qs_ref.shape[1]
    at = pl.multiple_of((1 - lax.rem(idx_ref[0], 2)) * half, half)
    qo_loads = [
        pltpu.make_async_copy(src.at[:, pl.ds(at, half)], qo_buf.at[k], qo_sems.at[k])
        for k, src in enumerate((q_ref, do_ref))
    ]
    for one in qo_loads:
        one.start()
    b_all = bc_ref[:, 0, :]
    c_all = bc_ref[:, 1, :]
    bc = [
        jnp.concatenate([b_all[:, at : at + HD], c_all[:, at : at + HD]], axis=1) for at in (0, HD)
    ]
    stores = []
    for d in range(blocks):
        buf[d, 2 * BLK : 3 * BLK] = bc[d // (blocks // 2)]
        raw = jnp.concatenate([dt_ref[2 * d : 2 * d + 1], dt_ref[2 * d + 1 : 2 * d + 2]], axis=1)
        hi = raw.astype(BF16).astype(F32)
        mid = (raw - hi).astype(BF16).astype(F32)
        parts = [hi, mid, raw - hi - mid, jnp.zeros((13, 2 * BLK), F32)]
        buf[d, 3 * BLK : 3 * BLK + 16] = jnp.concatenate(parts, axis=0).astype(BF16)
        for one in loads[d]:
            one.wait()
        stores.append(pltpu.make_async_copy(buf.at[d], out_ref.at[d], out_sems.at[d]))
        stores[-1].start()
    for d in range(blocks):
        head = slice((d % 2) * HD, (d % 2 + 1) * HD)
        kv_buf[d] = jnp.concatenate([k_ref[:, head], v_ref[:, head]], axis=1)
    stores.append(pltpu.make_async_copy(kv_buf, kv_ref, kv_sem))
    stores[-1].start()
    for k, dst in enumerate((qs_ref, dos_ref)):
        qo_loads[k].wait()
        stores.append(pltpu.make_async_copy(qo_buf.at[k], dst, qo_sems.at[2 + k]))
        stores[-1].start()
    for one in stores:
        one.wait()


def pack(place, x_in, grad, bc_sent, dt_raw, key, value, query, d_out, blocks):
    hbm = pl.BlockSpec(memory_space=pltpu.HBM)
    vmem = pl.BlockSpec(memory_space=pltpu.VMEM)
    part = jax.ShapeDtypeStruct((BLK, query.shape[1] // 2), BF16)
    return pl.pallas_call(
        pack_kernel,
        out_shape=[
            jax.ShapeDtypeStruct((blocks, 3 * BLK + 16, 2 * HD), BF16),
            jax.ShapeDtypeStruct((blocks, BLK, 2 * HD), BF16),
            part,
            part,
        ],
        in_specs=[pl.BlockSpec(memory_space=pltpu.SMEM), hbm, hbm, vmem, vmem, vmem, vmem, hbm, hbm],
        out_specs=[hbm] * 4,
        scratch_shapes=[
            pltpu.VMEM((blocks, 3 * BLK + 16, 2 * HD), BF16),
            pltpu.VMEM((blocks, BLK, 2 * HD), BF16),
            pltpu.VMEM((2,) + part.shape, BF16),
            pltpu.SemaphoreType.DMA((2 * blocks,)),
            pltpu.SemaphoreType.DMA((blocks,)),
            pltpu.SemaphoreType.DMA(()),
            pltpu.SemaphoreType.DMA((4,)),
        ],
        cost_estimate=pl.CostEstimate(flops=0, bytes_accessed=7 * 2**20, transcendentals=0),
        name="pack",
    )(place, x_in, grad, bc_sent, dt_raw, key, value, query, d_out)


def unpack_kernel(
    idx_ref, part, dq_own, dq_got, own, dx_ref, dbc_ref, dt_ref, wx_ref, wbc_ref, dq_ref, passed, sems
):
    blocks = part.shape[0]
    half = blocks // 2
    copies = []
    for d in range(blocks):
        lanes = pl.ds(d * 2 * HD, 2 * HD)
        copies.append(pltpu.make_async_copy(part.at[d, pl.ds(0, BLK)], dx_ref.at[:, lanes], sems.at[d]))
        copies[-1].start()
    for group in range(2):
        at = [group * half + d for d in range(half)]
        total = part[at[0], BLK : 2 * BLK].astype(F32)
        taps = part[at[0], 2 * BLK : 2 * BLK + 16].astype(F32)
        for d in at[1:]:
            total = total + part[d, BLK : 2 * BLK].astype(F32)
            taps = taps + part[d, 2 * BLK : 2 * BLK + 16].astype(F32)
        for which in range(2):
            lanes = slice(which * HD, (which + 1) * HD)
            out = slice((2 * which + group) * HD, (2 * which + group + 1) * HD)
            dbc_ref[:, out] = total[:, lanes].astype(BF16)
            wbc_ref[:, which, group * HD : (group + 1) * HD] = taps[10:14, lanes]
    for d in range(blocks):
        small = part[d, 2 * BLK : 2 * BLK + 16].astype(F32)
        raw = small[0:1] + small[1:2]
        dt_ref[2 * d : 2 * d + 1] = raw[:, :BLK]
        dt_ref[2 * d + 1 : 2 * d + 2] = raw[:, BLK:]
        wx_ref[:, d * 2 * HD : (d + 1) * 2 * HD] = small[2:6] + small[6:10]
    odd = lax.rem(idx_ref[0], 2)
    a = dq_own[...]
    b = dq_got[...]
    dq_ref[:, : a.shape[1]] = jnp.where(odd == 0, a, b)
    dq_ref[:, a.shape[1] :] = jnp.where(odd == 0, b, a)
    for done in copies:
        done.wait()


def unpack(place, received, dq_own, dq_got, own):
    blocks = received.shape[0]
    hbm = pl.BlockSpec(memory_space=pltpu.HBM)
    vmem = pl.BlockSpec(memory_space=pltpu.VMEM)
    return pl.pallas_call(
        unpack_kernel,
        out_shape=[
            jax.ShapeDtypeStruct((BLK, blocks * 2 * HD), BF16),
            jax.ShapeDtypeStruct((BLK, 4 * HD), BF16),
            jax.ShapeDtypeStruct((2 * blocks, BLK), F32),
            jax.ShapeDtypeStruct((TAPS, blocks * 2 * HD), F32),
            jax.ShapeDtypeStruct((TAPS, 2, 2 * HD), F32),
            jax.ShapeDtypeStruct((BLK, 2 * dq_own.shape[1]), BF16),
            jax.ShapeDtypeStruct(own.shape, own.dtype),
        ],
        in_specs=[pl.BlockSpec(memory_space=pltpu.SMEM), vmem, vmem, vmem, pl.BlockSpec(memory_space=pl.ANY)],
        out_specs=[hbm, vmem, vmem, vmem, vmem, vmem, pl.BlockSpec(memory_space=pl.ANY)],
        input_output_aliases={4: 6},
        scratch_shapes=[pltpu.SemaphoreType.DMA((blocks,))],
        compiler_params=pltpu.CompilerParams(vmem_limit_bytes=8 * 2**20),
        cost_estimate=pl.CostEstimate(flops=10**6, bytes_accessed=4 * 2**20, transcendentals=0),
        name="unpack",
    )(place, received, dq_own, dq_got, own)


def kv_sum_kernel(idx_ref, own, r1, r2, r3, r4, mine, sent):
    total = own[...]
    for got in (r1, r2, r3, r4):
        total = total + got[...].astype(F32)
    rows = mine.shape[0]
    first = total[:rows].astype(BF16)
    second = total[rows:].astype(BF16)
    odd = lax.rem(idx_ref[0], 2)
    mine[...] = jnp.where(odd == 0, first, second)
    sent[...] = jnp.where(odd == 0, second, first)


def kv_total(place, own, received):
    vmem = pl.BlockSpec(memory_space=pltpu.VMEM)
    half = jax.ShapeDtypeStruct((own.shape[0] // 2, own.shape[1]), BF16)
    return pl.pallas_call(
        kv_sum_kernel,
        out_shape=[half, half],
        in_specs=[pl.BlockSpec(memory_space=pltpu.SMEM)]
        + [vmem] * (1 + len(received)),
        out_specs=[vmem, vmem],
        compiler_params=pltpu.CompilerParams(vmem_limit_bytes=4 * 2**20),
        name="kv_total",
    )(place, own, *received)


def kv_place_kernel(idx_ref, mine, other, dk_ref, dv_ref):
    odd = lax.rem(idx_ref[0], 2)
    a = mine[...]
    b = other[...]
    first = jnp.where(odd == 0, a, b)
    second = jnp.where(odd == 0, b, a)
    dk_ref[...] = jnp.concatenate([first[:, :HD], second[:, :HD]], axis=1)
    dv_ref[...] = jnp.concatenate([first[:, HD:], second[:, HD:]], axis=1)


def kv_place(place, mine, other):
    vmem = pl.BlockSpec(memory_space=pltpu.VMEM)
    return pl.pallas_call(
        kv_place_kernel,
        out_shape=[jax.ShapeDtypeStruct(mine.shape, BF16)] * 2,
        in_specs=[pl.BlockSpec(memory_space=pltpu.SMEM), vmem, vmem],
        out_specs=[vmem, vmem],
        compiler_params=pltpu.CompilerParams(vmem_limit_bytes=4 * 2**20),
        name="kv_place",
    )(place, mine, other)


def swap(a):
    return lax.all_to_all(a, "ctx", 0, 0, tiled=True)


def shards(
    x_in, bc_in, conv_x, conv_bc, dt_raw, rate, grad_ssd, query, key, value, d_out, doc_lengths
):
    ctx = lax.axis_size("ctx")
    rows = x_in.shape[0]
    place = lax.axis_index("ctx").astype(jnp.int32).reshape(1)

    odd = place[0] % 2

    def half(a, which):
        return lax.dynamic_slice_in_dim(a, which * (a.shape[1] // 2), a.shape[1] // 2, 1)

    def pick(own, other):
        return jnp.where(odd == 0, own, other), jnp.where(odd == 0, other, own)

    packed, kv_sent, q_sent, do_sent = pack(
        place, x_in, grad_ssd, bc_in, dt_raw, key, value, query, d_out, ctx
    )
    got = swap(packed)
    got, kv_sent = lax.optimization_barrier((got, kv_sent))
    kv = swap(kv_sent)
    got_q = partner(q_sent)
    got_do = partner(do_sent)
    mixed = ssm_core(doc_lengths, place, rate, got, conv_x, conv_bc)
    mixed, kv, got_q, got_do = lax.optimization_barrier((mixed, kv, got_q, got_do))
    back = swap(mixed)
    dq_own, dq_sent, *d_kv = attention_core(doc_lengths, place, query, d_out, got_q, got_do, kv)
    received = [shift(d_kv[by], -2 * by) for by in range(1, BACK // 2 + 1)]
    d_x, d_bc, d_dt, d_wx, d_wbc, d_query, own = unpack(
        place, back, dq_own, partner(dq_sent), d_kv[0]
    )
    mine, sent = kv_total(place, own, received)
    d_key, d_value = kv_place(place, mine, partner(sent))
    return (
        d_x,
        d_bc.reshape(rows, 2, 2 * HD),
        d_dt,
        d_wx,
        d_wbc,
        d_query,
        d_key,
        d_value,
    )


def solution(mesh):
    tokens = P(("dp", "ctx"), "head")
    in_specs = (
        tokens,
        P(("dp", "ctx"), None, "head"),
        P(None, "head"),
        P(None, None, "head"),
        P("head", ("dp", "ctx")),
        P("head"),
        tokens,
        tokens,
        tokens,
        tokens,
        tokens,
        P("dp"),
    )
    out_specs = (
        tokens,
        P(("dp", "ctx"), None, "head"),
        P("head", ("dp", "ctx")),
        P("dp", "head"),
        P("dp", None, "head"),
        tokens,
        tokens,
        tokens,
    )
    return jax.shard_map(shards, mesh=mesh, in_specs=in_specs, out_specs=out_specs, check_vma=False)
```

```python
import jax
import jax.numpy as jnp
from jax import lax
from jax.experimental import pallas as pl
from jax.experimental.pallas import tpu as pltpu
from jax.sharding import PartitionSpec as P

F32 = jnp.float32
BF16 = jnp.bfloat16
HD = 128
BLK = 128
TAPS = 4
BACK = 8
LOG2E = 1.4426950408889634
NEG_BIG = -1e30
UNROLL = 4


def dot_nn(a, b):
    return lax.dot_general(a, b, (((1,), (0,)), ((), ())), preferred_element_type=F32)


def dot_nt(a, b):
    return lax.dot_general(a, b, (((1,), (1,)), ((), ())), preferred_element_type=F32)


def dot_tn(a, b):
    return lax.dot_general(a, b, (((0,), (0,)), ((), ())), preferred_element_type=F32)


def doc_bounds(doc_ref):
    s1 = doc_ref[0]
    s2 = s1 + doc_ref[1]
    s3 = s2 + doc_ref[2]
    return s1, s2, s3


def start_at(pos, bounds):
    s1, s2, s3 = bounds
    return jnp.where(pos >= s3, s3, jnp.where(pos >= s2, s2, jnp.where(pos >= s1, s1, 0)))


def next_start(pos, bounds, total):
    s1, s2, s3 = bounds
    return jnp.where(pos < s1, s1, jnp.where(pos < s2, s2, jnp.where(pos < s3, s3, total)))


def twice(a):
    return jnp.concatenate([a, a], axis=1)


def fold_rows(a):
    return jnp.sum(a.reshape(a.shape[0] // 8, 8, a.shape[1]), axis=0)


def split3(a):
    hi = a.astype(BF16)
    rest = a - hi.astype(F32)
    mid = rest.astype(BF16)
    return hi, mid, (rest - mid.astype(F32)).astype(BF16)


def dot_exact(a, ones):
    rows = a.shape[0]
    out = dot_nn(jnp.concatenate(split3(a), axis=0), ones.astype(BF16))
    return out[:rows] + out[rows : 2 * rows] + out[2 * rows :]


def ssm_kernel(
    doc_ref, idx_ref, rate_ref, r_ref, wx_ref, wbc_ref, out_ref,
    xs_s, xp_s, u_s, b_s, c_s, bm_s, cm_s, dsx_s, dsbc_s, st_s, ds_s,
    cols_s, elt_s, x2_s, y2_s, es_s, tapx_s, tapbc_s,
):
    blocks = r_ref.shape[0]
    total = blocks * BLK
    place = idx_ref[0]
    bounds = doc_bounds(doc_ref)
    rate0 = rate_ref[2 * place]
    rate1 = rate_ref[2 * place + 1]
    group = place // (blocks // 2)
    wx = wx_ref[:, pl.ds(pl.multiple_of(place * 256, 256), 256)]
    wbc = jnp.concatenate(
        [
            wbc_ref[:, 0, pl.ds(pl.multiple_of(group * 128, 128), 128)],
            wbc_ref[:, 1, pl.ds(pl.multiple_of(group * 128, 128), 128)],
        ],
        axis=1,
    )

    for c in range(blocks):
        row = jnp.sum(r_ref[c, 3 * BLK : 3 * BLK + 16, :].astype(F32), axis=0, keepdims=True)
        x2_s[c : c + 1] = row[:, :128]
        x2_s[blocks + c : blocks + c + 1] = row[:, 128:]
    raw = x2_s[...]
    step = jnp.log(1.0 + jnp.exp(raw))
    sig = 1.0 / (1.0 + jnp.exp(-raw))
    row_ids = lax.broadcasted_iota(jnp.int32, (2 * blocks, 128), 0)
    rate = jnp.where(row_ids < blocks, rate0, rate1)
    ii = lax.broadcasted_iota(jnp.int32, (128, 128), 0)
    jj = lax.broadcasted_iota(jnp.int32, (128, 128), 1)
    cum = dot_exact(-step * rate, (ii <= jj).astype(F32))
    v_rows = jnp.exp(cum)
    u_hi, u_lo, _ = split3(step * jnp.exp(-cum))
    v_hi, v_lo, _ = split3(v_rows)
    last = jnp.broadcast_to(v_rows[:, 127:128], (2 * blocks, 128))
    pieces = [a.astype(F32) for a in (u_hi, u_lo, v_hi, v_lo)]
    for c in range(blocks):
        rows = [a[at : at + 1] for a in pieces for at in (c, blocks + c)]
        cols_s[c] = jnp.concatenate(rows, axis=0)
        elt_s[c] = jnp.broadcast_to(
            jnp.concatenate([last[c : c + 1], last[blocks + c : blocks + c + 1]], axis=1), (8, 256)
        )
    row8 = lax.broadcasted_iota(jnp.int32, (8, 512), 0)
    lane8 = lax.broadcasted_iota(jnp.int32, (8, 512), 1) // 128
    spread = ((lane8 // 2 == row8 // 4) & (lane8 % 2 == row8 % 2)).astype(BF16)

    edge = jnp.zeros((8, 256), F32)
    st_s[0] = jnp.zeros((128, 256), F32)

    def conv(edge, value, weight, keeps):
        win = jnp.concatenate([edge, value], axis=0)
        pre = value * weight[TAPS - 1 : TAPS]
        for d in range(1, TAPS):
            pre = pre + jnp.where(keeps[d - 1], win[8 - d : 8 - d + BLK], 0.0) * weight[TAPS - 1 - d : TAPS - d]
        sg = 0.5 * jnp.tanh(0.5 * pre) + 0.5
        val = pre * sg
        return val, sg + val * (1.0 - sg)

    def forward(c, carry):
        base = pl.multiple_of(c * BLK, BLK)
        edge_x, edge_bc = carry
        x = r_ref[c, 0:BLK].astype(F32)
        bc_raw = r_ref[c, 2 * BLK : 3 * BLK].astype(F32)
        pos = base + ii
        start = start_at(pos, bounds)
        last_start = start_at(base + BLK - 1, bounds)
        tails = pos >= last_start
        dist = pos - start
        keeps = [twice(dist >= d) for d in range(1, TAPS)]
        xs, dsx = conv(edge_x, x, wx, keeps)
        bc, dsbc = conv(edge_bc, bc_raw, wbc, keeps)
        xs_s[c] = xs
        dsx_s[c] = dsx
        dsbc_s[c] = dsbc
        b = bc[:, :128]
        cc = bc[:, 128:]
        b_s[c] = b.astype(BF16)
        c_s[c] = cc.astype(BF16)
        bm = jnp.where(tails, b, 0.0).astype(BF16)
        bm_s[c] = bm
        cm_s[c] = jnp.where(start < base, cc, 0.0).astype(BF16)
        u = dot_tn(cols_s[c].astype(BF16), spread[:, :256])
        u_s[c] = u
        xp = (xs * u).astype(BF16)
        xp_s[c] = xp
        elt = elt_s[c][0:1]
        keep = jnp.where(last_start < base, elt, 0.0)
        st_s[c + 1] = keep * st_s[c] + elt * dot_tn(bm, xp)
        return x[BLK - 8 :], bc_raw[BLK - 8 :]

    lax.fori_loop(0, blocks, forward, (edge, edge), unroll=UNROLL)

    ds_s[...] = jnp.zeros((128, 256), F32)
    tapx_s[...] = jnp.zeros((TAPS, 8, 256), F32)
    tapbc_s[...] = jnp.zeros((TAPS, 8, 256), F32)
    lane2 = lax.broadcasted_iota(jnp.int32, (16, 256), 1)
    row2 = lax.broadcasted_iota(jnp.int32, (16, 256), 0)
    pick = (lane2 // 128 == row2).astype(BF16)

    def head_sums(out, c, a):
        sums = dot_nt(pick, a.astype(BF16))
        out[pl.ds(c, 1)] = sums[0:1]
        out[pl.ds(blocks + c, 1)] = sums[1:2]

    def conv_back(grad, edge, raw_in, weight, ends, taps):
        win = jnp.concatenate([grad, edge], axis=0)
        total_grad = grad * weight[TAPS - 1 : TAPS]
        taps[TAPS - 1] += fold_rows(grad * raw_in)
        for d in range(1, TAPS):
            moved = jnp.where(ends[d - 1], win[d : d + BLK], 0.0)
            total_grad = total_grad + moved * weight[TAPS - 1 - d : TAPS - d]
            taps[TAPS - 1 - d] += fold_rows(moved * raw_in)
        return total_grad

    def backward(lap, carry):
        c = blocks - 1 - lap
        base = pl.multiple_of(c * BLK, BLK)
        pos = base + ii
        start = start_at(pos, bounds)
        last_start = start_at(base + BLK - 1, bounds)
        causal = (jj <= ii) & (base + jj >= start)
        leads = start < base
        tails = pos >= last_start
        b = b_s[c]
        cc = c_s[c]
        xp = xp_s[c]
        cm = cm_s[c]
        gv = r_ref[c, BLK : 2 * BLK].astype(F32) * dot_tn(cols_s[c].astype(BF16), spread[:, 256:])
        gp = gv.astype(BF16)
        elt = elt_s[c][0:1]
        ds = ds_s[...]
        es_s[pl.ds(pl.multiple_of(c * 8, 8), 8)] = fold_rows(ds * st_s[c + 1])
        sb = st_s[c].astype(BF16)
        ds_e = elt * ds
        dsb = ds_e.astype(BF16)
        ds_s[...] = jnp.where(last_start < base, ds_e, 0.0) + dot_tn(cm, gp)
        w = jnp.where(causal, dot_nt(cc, b), 0.0).astype(BF16)
        yv = dot_nn(w, xp) + dot_nn(cm, sb)
        dxp = dot_tn(w, gp) + dot_nn(bm_s[c], dsb)
        z = jnp.where(causal, dot_nt(gp, xp), 0.0).astype(BF16)
        dc = dot_nn(z, b) + jnp.where(leads, dot_nt(gp, sb), 0.0)
        db = dot_tn(z, cc) + jnp.where(tails, dot_nt(xp, dsb), 0.0)
        dx = u_s[c] * dxp
        head_sums(x2_s, c, xs_s[c] * dx)
        head_sums(y2_s, c, gv * yv)
        left = next_start(pos, bounds, total) - pos
        ends = [twice(left > d) for d in range(1, TAPS)]
        edge_x, edge_bc = carry
        pre_x = dx * dsx_s[c]
        pre_bc = jnp.concatenate([db, dc], axis=1) * dsbc_s[c]
        x = r_ref[c, 0:BLK].astype(F32)
        bc_raw = r_ref[c, 2 * BLK : 3 * BLK].astype(F32)
        out_ref[c, 0:BLK] = conv_back(pre_x, edge_x, x, wx, ends, tapx_s).astype(BF16)
        out_ref[c, BLK : 2 * BLK] = conv_back(
            pre_bc, edge_bc, bc_raw, wbc, ends, tapbc_s
        ).astype(BF16)
        return pre_x[0:8], pre_bc[0:8]

    lax.fori_loop(0, blocks, backward, (edge, edge), unroll=UNROLL)

    xdx = x2_s[...]
    carry_sum = jnp.sum(es_s[...].reshape(blocks, 8, 256), axis=1)
    carry_sum = jnp.concatenate([carry_sum[:, :128], carry_sum[:, 128:]], axis=0)
    d_log = dot_exact(y2_s[...] - xdx, (ii >= jj).astype(F32))
    d_log = d_log + jnp.sum(carry_sum, axis=1, keepdims=True)
    d_raw = (xdx / step - rate * d_log) * sig
    d_raw = jnp.concatenate([d_raw[:blocks], d_raw[blocks:]], axis=1)
    raw_hi = d_raw.astype(BF16).astype(F32)
    raw_lo = d_raw - raw_hi
    tapx = jnp.concatenate([jnp.sum(tapx_s[k], axis=0, keepdims=True) for k in range(TAPS)], axis=0)
    tapbc = jnp.concatenate([jnp.sum(tapbc_s[k], axis=0, keepdims=True) for k in range(TAPS)], axis=0)
    tapx_hi = tapx.astype(BF16).astype(F32)
    rest = jnp.concatenate([tapx_hi, tapx - tapx_hi, tapbc, jnp.zeros((2, 256), F32)], axis=0)
    for c in range(blocks):
        out_ref[c, 2 * BLK : 2 * BLK + 16] = jnp.concatenate(
            [raw_hi[c : c + 1], raw_lo[c : c + 1], rest], axis=0
        ).astype(BF16)


def ssm_core(doc_lengths, place, rate, received, weight_x, weight_bc):
    blocks = received.shape[0]
    smem = pl.BlockSpec(memory_space=pltpu.SMEM)
    vmem = pl.BlockSpec(memory_space=pltpu.VMEM)

    def scratch(*shape, dtype=F32):
        return pltpu.VMEM(shape, dtype)

    return pl.pallas_call(
        ssm_kernel,
        out_shape=jax.ShapeDtypeStruct((blocks, 2 * BLK + 16, 256), BF16),
        in_specs=[smem, smem, smem, vmem, vmem, vmem],
        out_specs=vmem,
        scratch_shapes=[
            scratch(blocks, BLK, 256),
            scratch(blocks, BLK, 256, dtype=BF16),
            scratch(blocks, BLK, 256),
            scratch(blocks, BLK, 128, dtype=BF16),
            scratch(blocks, BLK, 128, dtype=BF16),
            scratch(blocks, BLK, 128, dtype=BF16),
            scratch(blocks, BLK, 128, dtype=BF16),
            scratch(blocks, BLK, 256),
            scratch(blocks, BLK, 256),
            scratch(blocks + 1, 128, 256),
            scratch(128, 256),
            scratch(blocks, 8, 128),
            scratch(blocks, 8, 256),
            scratch(2 * blocks, 128),
            scratch(2 * blocks, 128),
            scratch(8 * blocks, 256),
            scratch(TAPS, 8, 256),
            scratch(TAPS, 8, 256),
        ],
        compiler_params=pltpu.CompilerParams(vmem_limit_bytes=24 * 2**20),
        cost_estimate=pl.CostEstimate(flops=3 * 10**9, bytes_accessed=6 * 2**20, transcendentals=4 * 10**6),
        name="mixer",
    )(doc_lengths, place, rate, received, weight_x, weight_bc)


def attention_kernel(
    doc_ref, idx_ref, q_ref, do_ref, got_q_ref, got_do_ref, kv_ref,
    dq_own, dq_sent, d0, d1, d2, d3, d4, kt_s, dk_s, dv_s, s_s, p_s,
):
    d_refs = (d4, d3, d2, d1, d0)
    count = 2 * len(d_refs)
    bounds = doc_bounds(doc_ref)
    scale = HD ** (-0.5)
    place = idx_ref[0]
    odd = lax.rem(place, 2)
    base = (place - odd) * BLK
    jrow = lax.broadcasted_iota(jnp.int32, (BLK, 2 * BLK), 0)
    icol = lax.broadcasted_iota(jnp.int32, (BLK, 2 * BLK), 1)
    start = start_at(base + icol[0:1], bounds) - base
    heads = got_q_ref.shape[1] // HD

    def rows8(a):
        return a.reshape(BLK // 8, 8, 2 * BLK)

    def half(b):
        return slice((b % 2) * BLK, (b % 2 + 1) * BLK)

    def key_rows(b):
        return kv_ref[jnp.maximum(place - odd - BACK + b, 0), :, 0:HD]

    def value_rows(b):
        return kv_ref[jnp.maximum(place - odd - BACK + b, 0), :, HD : 2 * HD]

    def in_order(own, other):
        first = jnp.where(odd == 0, own, other)
        second = jnp.where(odd == 0, other, own)
        return jnp.concatenate([first, second], axis=0)

    for b in range(count):
        kt_s[b] = key_rows(b).T
    dk_s[...] = jnp.zeros(dk_s.shape, F32)
    dv_s[...] = jnp.zeros(dv_s.shape, F32)

    def turn(head, carry):
        at = pl.multiple_of(head * HD, HD)
        own_at = pl.multiple_of((odd * heads + head) * HD, HD)
        q = in_order(q_ref[:, pl.ds(own_at, HD)], got_q_ref[:, pl.ds(at, HD)])
        do = in_order(
            do_ref[:, pl.ds(own_at, HD)], got_do_ref[:, pl.ds(at, HD)]
        )
        top = jnp.full((8, 2 * BLK), NEG_BIG, F32)
        for b in range(count):
            allowed = jrow >= start + (BACK - b) * BLK
            if b >= BACK:
                allowed = allowed & (jrow + (b - BACK) * BLK <= icol)
            s = jnp.where(allowed, dot_nt(key_rows(b), q), NEG_BIG)
            s_s[b] = s
            top = jnp.maximum(top, jnp.max(rows8(s), axis=0))
            p_s[b] = dot_nt(value_rows(b), do)
        top = jnp.max(top, axis=0, keepdims=True) * (scale * LOG2E)
        norm = jnp.zeros((8, 2 * BLK), F32)
        mean = jnp.zeros((8, 2 * BLK), F32)
        for b in range(count):
            e = jnp.exp2(s_s[b] * (scale * LOG2E) - top)
            s_s[b] = e
            norm = norm + jnp.sum(rows8(e), axis=0)
            mean = mean + jnp.sum(rows8(e * p_s[b]), axis=0)
        inverse = 1.0 / jnp.sum(norm, axis=0, keepdims=True)
        mean = jnp.sum(mean, axis=0, keepdims=True) * inverse
        dqt = jnp.zeros((HD, 2 * BLK), F32)
        for b in range(count):
            prob = s_s[b] * inverse
            grad = (prob * (p_s[b] - mean)).astype(BF16)
            dv_s[b] += dot_nn(prob.astype(BF16), do)
            dk_s[b] += dot_nn(grad, q)
            dqt = dqt + dot_nn(kt_s[b], grad)
        dqt = dqt * scale
        first = dqt[:, :BLK].T
        second = dqt[:, BLK:].T
        dq_own[:, pl.ds(at, HD)] = jnp.where(odd == 0, first, second).astype(BF16)
        dq_sent[:, pl.ds(at, HD)] = jnp.where(odd == 0, second, first).astype(BF16)
        return carry

    lax.fori_loop(0, heads, turn, 0)
    for b in range(count):
        out = d_refs[b // 2]
        out[half(b), 0:HD] = (dk_s[b] * scale).astype(out.dtype)
        out[half(b), HD : 2 * HD] = dv_s[b].astype(out.dtype)


def attention_core(doc_lengths, place, query, d_out, got_q, got_do, kv):
    smem = pl.BlockSpec(memory_space=pltpu.SMEM)
    vmem = pl.BlockSpec(memory_space=pltpu.VMEM)
    pairs = BACK // 2 + 1
    count = 2 * pairs
    rows, width = query.shape
    part = jax.ShapeDtypeStruct((rows, width // 2), BF16)
    kv_shape = (2 * rows, 2 * HD)
    outs = [part, part, jax.ShapeDtypeStruct(kv_shape, F32)]
    outs += [jax.ShapeDtypeStruct(kv_shape, BF16)] * (pairs - 1)
    return pl.pallas_call(
        attention_kernel,
        out_shape=outs,
        in_specs=[smem, smem] + [vmem] * 5,
        out_specs=[vmem] * (2 + pairs),
        scratch_shapes=[
            pltpu.VMEM((count, HD, BLK), BF16),
            pltpu.VMEM((count, BLK, HD), F32),
            pltpu.VMEM((count, BLK, HD), F32),
            pltpu.VMEM((count, BLK, 2 * BLK), F32),
            pltpu.VMEM((count, BLK, 2 * BLK), F32),
        ],
        compiler_params=pltpu.CompilerParams(vmem_limit_bytes=16 * 2**20),
        cost_estimate=pl.CostEstimate(flops=4 * 10**9, bytes_accessed=4 * 2**20, transcendentals=3 * 10**6),
        name="attention",
    )(doc_lengths, place, query, d_out, got_q, got_do, kv)


def shift(a, by):
    devices = lax.axis_size("ctx")
    return lax.ppermute(
        a, "ctx", [(i, i + by) for i in range(devices) if 0 <= i + by < devices]
    )


def partner(a):
    return lax.ppermute(a, "ctx", [(i, i ^ 1) for i in range(lax.axis_size("ctx"))])


def pack_kernel(
    idx_ref, x_ref, g_ref, bc_ref, dt_ref, k_ref, v_ref, q_ref, do_ref, out_ref, kv_ref, qs_ref, dos_ref,
    buf, kv_buf, qo_buf, in_sems, out_sems, kv_sem, qo_sems,
):
    blocks = out_ref.shape[0]
    loads = []
    for d in range(blocks):
        lanes = pl.ds(d * 2 * HD, 2 * HD)
        pair = [
            pltpu.make_async_copy(src, buf.at[d, pl.ds(at * BLK, BLK)], in_sems.at[2 * d + at])
            for at, src in enumerate((x_ref.at[:, lanes], g_ref.at[:, lanes]))
        ]
        for one in pair:
            one.start()
        loads.append(pair)
    half = qs_ref.shape[1]
    at = pl.multiple_of((1 - lax.rem(idx_ref[0], 2)) * half, half)
    qo_loads = [
        pltpu.make_async_copy(src.at[:, pl.ds(at, half)], qo_buf.at[k], qo_sems.at[k])
        for k, src in enumerate((q_ref, do_ref))
    ]
    for one in qo_loads:
        one.start()
    b_all = bc_ref[:, 0, :]
    c_all = bc_ref[:, 1, :]
    bc = [
        jnp.concatenate([b_all[:, at : at + HD], c_all[:, at : at + HD]], axis=1) for at in (0, HD)
    ]
    stores = []
    for d in range(blocks):
        buf[d, 2 * BLK : 3 * BLK] = bc[d // (blocks // 2)]
        raw = jnp.concatenate([dt_ref[2 * d : 2 * d + 1], dt_ref[2 * d + 1 : 2 * d + 2]], axis=1)
        hi = raw.astype(BF16).astype(F32)
        mid = (raw - hi).astype(BF16).astype(F32)
        parts = [hi, mid, raw - hi - mid, jnp.zeros((13, 2 * BLK), F32)]
        buf[d, 3 * BLK : 3 * BLK + 16] = jnp.concatenate(parts, axis=0).astype(BF16)
        for one in loads[d]:
            one.wait()
        stores.append(pltpu.make_async_copy(buf.at[d], out_ref.at[d], out_sems.at[d]))
        stores[-1].start()
    for d in range(blocks):
        head = slice((d % 2) * HD, (d % 2 + 1) * HD)
        kv_buf[d] = jnp.concatenate([k_ref[:, head], v_ref[:, head]], axis=1)
    stores.append(pltpu.make_async_copy(kv_buf, kv_ref, kv_sem))
    stores[-1].start()
    for k, dst in enumerate((qs_ref, dos_ref)):
        qo_loads[k].wait()
        stores.append(pltpu.make_async_copy(qo_buf.at[k], dst, qo_sems.at[2 + k]))
        stores[-1].start()
    for one in stores:
        one.wait()


def pack(place, x_in, grad, bc_sent, dt_raw, key, value, query, d_out, blocks):
    hbm = pl.BlockSpec(memory_space=pltpu.HBM)
    vmem = pl.BlockSpec(memory_space=pltpu.VMEM)
    part = jax.ShapeDtypeStruct((BLK, query.shape[1] // 2), BF16)
    return pl.pallas_call(
        pack_kernel,
        out_shape=[
            jax.ShapeDtypeStruct((blocks, 3 * BLK + 16, 2 * HD), BF16),
            jax.ShapeDtypeStruct((blocks, BLK, 2 * HD), BF16),
            part,
            part,
        ],
        in_specs=[pl.BlockSpec(memory_space=pltpu.SMEM), hbm, hbm, vmem, vmem, vmem, vmem, hbm, hbm],
        out_specs=[hbm] * 4,
        scratch_shapes=[
            pltpu.VMEM((blocks, 3 * BLK + 16, 2 * HD), BF16),
            pltpu.VMEM((blocks, BLK, 2 * HD), BF16),
            pltpu.VMEM((2,) + part.shape, BF16),
            pltpu.SemaphoreType.DMA((2 * blocks,)),
            pltpu.SemaphoreType.DMA((blocks,)),
            pltpu.SemaphoreType.DMA(()),
            pltpu.SemaphoreType.DMA((4,)),
        ],
        cost_estimate=pl.CostEstimate(flops=0, bytes_accessed=7 * 2**20, transcendentals=0),
        name="pack",
    )(place, x_in, grad, bc_sent, dt_raw, key, value, query, d_out)


def unpack_kernel(
    idx_ref, part, dq_own, dq_got, own, dx_ref, dbc_ref, dt_ref, wx_ref, wbc_ref, dq_ref, passed, sems
):
    blocks = part.shape[0]
    half = blocks // 2
    copies = []
    for d in range(blocks):
        lanes = pl.ds(d * 2 * HD, 2 * HD)
        copies.append(pltpu.make_async_copy(part.at[d, pl.ds(0, BLK)], dx_ref.at[:, lanes], sems.at[d]))
        copies[-1].start()
    for group in range(2):
        at = [group * half + d for d in range(half)]
        total = part[at[0], BLK : 2 * BLK].astype(F32)
        taps = part[at[0], 2 * BLK : 2 * BLK + 16].astype(F32)
        for d in at[1:]:
            total = total + part[d, BLK : 2 * BLK].astype(F32)
            taps = taps + part[d, 2 * BLK : 2 * BLK + 16].astype(F32)
        for which in range(2):
            lanes = slice(which * HD, (which + 1) * HD)
            out = slice((2 * which + group) * HD, (2 * which + group + 1) * HD)
            dbc_ref[:, out] = total[:, lanes].astype(BF16)
            wbc_ref[:, which, group * HD : (group + 1) * HD] = taps[10:14, lanes]
    for d in range(blocks):
        small = part[d, 2 * BLK : 2 * BLK + 16].astype(F32)
        raw = small[0:1] + small[1:2]
        dt_ref[2 * d : 2 * d + 1] = raw[:, :BLK]
        dt_ref[2 * d + 1 : 2 * d + 2] = raw[:, BLK:]
        wx_ref[:, d * 2 * HD : (d + 1) * 2 * HD] = small[2:6] + small[6:10]
    odd = lax.rem(idx_ref[0], 2)
    a = dq_own[...]
    b = dq_got[...]
    dq_ref[:, : a.shape[1]] = jnp.where(odd == 0, a, b)
    dq_ref[:, a.shape[1] :] = jnp.where(odd == 0, b, a)
    for done in copies:
        done.wait()


def unpack(place, received, dq_own, dq_got, own):
    blocks = received.shape[0]
    hbm = pl.BlockSpec(memory_space=pltpu.HBM)
    vmem = pl.BlockSpec(memory_space=pltpu.VMEM)
    return pl.pallas_call(
        unpack_kernel,
        out_shape=[
            jax.ShapeDtypeStruct((BLK, blocks * 2 * HD), BF16),
            jax.ShapeDtypeStruct((BLK, 4 * HD), BF16),
            jax.ShapeDtypeStruct((2 * blocks, BLK), F32),
            jax.ShapeDtypeStruct((TAPS, blocks * 2 * HD), F32),
            jax.ShapeDtypeStruct((TAPS, 2, 2 * HD), F32),
            jax.ShapeDtypeStruct((BLK, 2 * dq_own.shape[1]), BF16),
            jax.ShapeDtypeStruct(own.shape, own.dtype),
        ],
        in_specs=[pl.BlockSpec(memory_space=pltpu.SMEM), vmem, vmem, vmem, pl.BlockSpec(memory_space=pl.ANY)],
        out_specs=[hbm, vmem, vmem, vmem, vmem, vmem, pl.BlockSpec(memory_space=pl.ANY)],
        input_output_aliases={4: 6},
        scratch_shapes=[pltpu.SemaphoreType.DMA((blocks,))],
        compiler_params=pltpu.CompilerParams(vmem_limit_bytes=8 * 2**20),
        cost_estimate=pl.CostEstimate(flops=10**6, bytes_accessed=4 * 2**20, transcendentals=0),
        name="unpack",
    )(place, received, dq_own, dq_got, own)


def kv_sum_kernel(idx_ref, own, r1, r2, r3, r4, mine, sent):
    total = own[...]
    for got in (r1, r2, r3, r4):
        total = total + got[...].astype(F32)
    rows = mine.shape[0]
    first = total[:rows].astype(BF16)
    second = total[rows:].astype(BF16)
    odd = lax.rem(idx_ref[0], 2)
    mine[...] = jnp.where(odd == 0, first, second)
    sent[...] = jnp.where(odd == 0, second, first)


def kv_total(place, own, received):
    vmem = pl.BlockSpec(memory_space=pltpu.VMEM)
    half = jax.ShapeDtypeStruct((own.shape[0] // 2, own.shape[1]), BF16)
    return pl.pallas_call(
        kv_sum_kernel,
        out_shape=[half, half],
        in_specs=[pl.BlockSpec(memory_space=pltpu.SMEM)]
        + [vmem] * (1 + len(received)),
        out_specs=[vmem, vmem],
        compiler_params=pltpu.CompilerParams(vmem_limit_bytes=4 * 2**20),
        name="kv_total",
    )(place, own, *received)


def kv_place_kernel(idx_ref, mine, other, dk_ref, dv_ref):
    odd = lax.rem(idx_ref[0], 2)
    a = mine[...]
    b = other[...]
    first = jnp.where(odd == 0, a, b)
    second = jnp.where(odd == 0, b, a)
    dk_ref[...] = jnp.concatenate([first[:, :HD], second[:, :HD]], axis=1)
    dv_ref[...] = jnp.concatenate([first[:, HD:], second[:, HD:]], axis=1)


def kv_place(place, mine, other):
    vmem = pl.BlockSpec(memory_space=pltpu.VMEM)
    return pl.pallas_call(
        kv_place_kernel,
        out_shape=[jax.ShapeDtypeStruct(mine.shape, BF16)] * 2,
        in_specs=[pl.BlockSpec(memory_space=pltpu.SMEM), vmem, vmem],
        out_specs=[vmem, vmem],
        compiler_params=pltpu.CompilerParams(vmem_limit_bytes=4 * 2**20),
        name="kv_place",
    )(place, mine, other)


def swap(a):
    return lax.all_to_all(a, "ctx", 0, 0, tiled=True)


def shards(
    x_in, bc_in, conv_x, conv_bc, dt_raw, rate, grad_ssd, query, key, value, d_out, doc_lengths
):
    ctx = lax.axis_size("ctx")
    rows = x_in.shape[0]
    place = lax.axis_index("ctx").astype(jnp.int32).reshape(1)

    odd = place[0] % 2

    def half(a, which):
        return lax.dynamic_slice_in_dim(a, which * (a.shape[1] // 2), a.shape[1] // 2, 1)

    def pick(own, other):
        return jnp.where(odd == 0, own, other), jnp.where(odd == 0, other, own)

    packed, kv_sent, q_sent, do_sent = pack(
        place, x_in, grad_ssd, bc_in, dt_raw, key, value, query, d_out, ctx
    )
    got = swap(packed)
    got, kv_sent = lax.optimization_barrier((got, kv_sent))
    kv = swap(kv_sent)
    got_q = partner(q_sent)
    got_do = partner(do_sent)
    mixed = ssm_core(doc_lengths, place, rate, got, conv_x, conv_bc)
    mixed, kv, got_q, got_do = lax.optimization_barrier((mixed, kv, got_q, got_do))
    back = swap(mixed)
    dq_own, dq_sent, *d_kv = attention_core(doc_lengths, place, query, d_out, got_q, got_do, kv)
    received = [shift(d_kv[by], -2 * by) for by in range(1, BACK // 2 + 1)]
    d_x, d_bc, d_dt, d_wx, d_wbc, d_query, own = unpack(
        place, back, dq_own, partner(dq_sent), d_kv[0]
    )
    mine, sent = kv_total(place, own, received)
    d_key, d_value = kv_place(place, mine, partner(sent))
    return (
        d_x,
        d_bc.reshape(rows, 2, 2 * HD),
        d_dt,
        d_wx,
        d_wbc,
        d_query,
        d_key,
        d_value,
    )


def solution(mesh):
    tokens = P(("dp", "ctx"), "head")
    in_specs = (
        tokens,
        P(("dp", "ctx"), None, "head"),
        P(None, "head"),
        P(None, None, "head"),
        P("head", ("dp", "ctx")),
        P("head"),
        tokens,
        tokens,
        tokens,
        tokens,
        tokens,
        P("dp"),
    )
    out_specs = (
        tokens,
        P(("dp", "ctx"), None, "head"),
        P("head", ("dp", "ctx")),
        P("dp", "head"),
        P("dp", None, "head"),
        tokens,
        tokens,
        tokens,
    )
    return jax.shard_map(shards, mesh=mesh, in_specs=in_specs, out_specs=out_specs, check_vma=False)
```
